256 devices in a mesh: seq: 32 (over y, z_hi, x), tensor: 8 (over z_lo, core).
Axes of the slice: x: 4, y: 4, z: 8 (z_hi: 2, z_lo: 4; z = z_hi * 4 + z_lo), core: 2. Of those that a mesh axis runs over, the one named last changes fastest.
Arguments:
- tokens: bfloat16 [16384, 4096], P('seq', 'tensor'), may hold values from -6 to 6
- prior_rows: bfloat16 [129, 4096], P(None, 'tensor'), may hold values from -6 to 6
- norm_gain: bfloat16 [4096], P('tensor'), may hold values from 0.25 to 1.75
- in_weight: bfloat16 [3, 4096, 4096], P(None, 'seq', 'tensor'), may hold values from -0.09375 to 0.09375
- short_filter: float32 [3, 3, 4096], P(None, None, 'tensor'), may hold values from -3 to 3
- mr_filter: bfloat16 [256, 128], P('tensor'), may hold values from -3 to 3
- mr_bias: float32 [4096], P('tensor'), may hold values from -4 to 4
- out_weight: bfloat16 [4096, 4096], P('tensor', 'seq'), may hold values from -0.09375 to 0.09375
Outputs:
- block_out: bfloat16 [16384, 4096], P('seq', 'tensor')
The draws below stay inside these ranges and needn't reach their ends.
All inputs are finite; a program needn't handle non-finite values.
Results may differ from the reference program's by a relative error of at most 0.02.
Values may be sent and summed in bfloat16 or wider, within the bound.
No kernel may reach another device: no remote copies, remote signals or barrier semaphores. Data moves between devices by JAX's collectives and lax.ppermute only.
A program may use at most 128 MiB of HBM per device.

```python
import jax
import jax.numpy as jnp
from jax import lax

D = 4096
LH = 128
GSIZE = 16
NGROUPS = 256
PAST = 129
TOKENS = 16384


def draw_mr_filter(key, part):
    key = jax.random.fold_in(key, 11)
    rate_key, noise_key = jax.random.split(key)
    tap_pos = jnp.arange(LH).astype(jnp.float32)
    rates = jnp.exp(jax.random.uniform(rate_key, (NGROUPS,), jnp.float32, jnp.log(1.0 / 400.0), jnp.log(1.0 / 25.0)))
    noise = jnp.clip(jax.random.normal(noise_key, (NGROUPS, LH), jnp.float32), -6.0, 6.0)
    return (0.15 * noise * jnp.exp(-rates[:, None] * tap_pos[None, :])).astype(jnp.bfloat16)


def steps_of(own_key, dims, cuts, low, high):
    factor_of = 1.0
    for position, parts in cuts:
        draws = jax.random.uniform(jax.random.fold_in(jax.random.fold_in(own_key, 6), position), (parts,), jnp.float32, low / len(cuts), high / len(cuts))
        factor_of = factor_of * jnp.repeat(jnp.exp(draws), dims[position] // parts).reshape((-1,) + (1,) * (len(dims) - 1 - position))
    return factor_of


def scatter_about(key, dims, deviation, limit, pieces=(), dtype=jnp.bfloat16):
    level = steps_of(key, dims, pieces, -0.22, 0.18) if pieces else 1.0
    entries = jax.random.normal(key, dims, jnp.float32) * deviation * level
    return jnp.minimum(jnp.maximum(entries, -limit), limit).astype(dtype)


def setup_inputs(seed: int = 0) -> dict:
    key_of = jax.random.split(jax.random.key(seed), 9)
    return {
        "tokens": scatter_about(key_of[0], (TOKENS, D), 1.0, 6.0, ((0, 32), (1, 8))),
        "prior_rows": scatter_about(key_of[1], (PAST, D), 1.0, 6.0, ((1, 8),)),
        "norm_gain": jnp.clip(1.0 + 0.15 * jax.random.normal(key_of[2], (D,), jnp.float32), 0.25, 1.75).astype(jnp.bfloat16),
        "in_weight": scatter_about(key_of[3], (3, D, D), D ** -0.5, 0.09375, ((1, 32), (2, 8))),
        "short_filter": scatter_about(key_of[4], (3, 3, D), 0.6, 3.0, ((2, 8),), jnp.float32),
        "mr_filter": draw_mr_filter(jax.random.fold_in(key_of[8], 71), 0),
        "mr_bias": scatter_about(key_of[6], (D,), 1.0, 4.0, ((0, 8),), jnp.float32),
        "out_weight": scatter_about(key_of[7], (D, D), D ** -0.5, 0.09375, ((0, 8), (1, 32))),
    }


def reference(tokens, prior_rows, norm_gain, in_weight, short_filter, mr_filter, mr_bias, out_weight):
    stacked = jnp.concatenate([prior_rows, tokens], 0).astype(jnp.float32)
    inv_rms = lax.rsqrt(lax.optimization_barrier(jnp.mean(stacked * stacked, axis=-1, keepdims=True)) + 1e-06)
    normed = (stacked * inv_rms * norm_gain.astype(jnp.float32)[None, :]).astype(jnp.bfloat16)
    projected = jnp.stack([jnp.dot(normed, in_weight[part_index], preferred_element_type=jnp.float32) for part_index in range(3)]).astype(jnp.bfloat16)
    lifted = projected.astype(jnp.float32)
    total_rows = lifted.shape[1]
    padded = jnp.pad(lifted, ((0, 0), (2, 0), (0, 0)))
    feats = short_filter[0][:, None, :] * padded[:, 2:] + short_filter[1][:, None, :] * padded[:, 1:total_rows + 1] + short_filter[2][:, None, :] * padded[:, 0:total_rows]
    mixing = (feats[1] * feats[2]).astype(jnp.bfloat16)
    per_channel = jnp.repeat(mr_filter, GSIZE, axis=0).astype(jnp.float32)
    padded_mix = jnp.concatenate([jnp.zeros((LH - 1, mixing.shape[1]), jnp.bfloat16), mixing], 0)

    def add_tap(tap_number, running):
        window = lax.dynamic_slice_in_dim(padded_mix, LH - 1 - tap_number, total_rows, 0)
        coefs = lax.dynamic_slice_in_dim(per_channel, tap_number, 1, 1)[:, 0]
        return running + window.astype(jnp.float32) * coefs[None, :]
    filtered = lax.fori_loop(0, LH, add_tap, jnp.zeros(mixing.shape, jnp.float32))
    gated = (feats[0] * (filtered + mr_bias[None, :] * mixing.astype(jnp.float32))).astype(jnp.bfloat16)[PAST:]
    summed = jnp.dot(gated, out_weight, preferred_element_type=jnp.float32)
    return (tokens.astype(jnp.float32) + summed).astype(jnp.bfloat16)
```

```python
import functools

import jax
import jax.numpy as jnp
from jax import lax
from jax.experimental import pallas as pl
from jax.experimental.pallas import tpu as pltpu
from jax.sharding import Mesh, PartitionSpec as P

GSIZE = 16
LH = 128
ROWS = 512
FRONT = 80
WIDE = 512
CH = 256
GROUPS = CH // GSIZE
HALO = LH + 16
VMEM = 48 * 1024 * 1024
F32 = jnp.float32
BF16 = jnp.bfloat16


def row_iota(shape):
    return lax.broadcasted_iota(jnp.int32, shape, 0)


def three_taps(rows, taps, s):
    return (
        taps[0, s : s + 1] * rows
        + taps[1, s : s + 1] * pltpu.roll(rows, 1, 0)
        + taps[2, s : s + 1] * pltpu.roll(rows, 2, 0)
    )


def project_kernel(x_ref, w_ref, gain_ref, taps_ref, proj_ref, tail_ref, front_ref, acc, ssq):
    step = pl.program_id(0)

    @pl.when(step == 0)
    def _():
        acc[...] = jnp.zeros_like(acc)
        ssq[...] = jnp.zeros_like(ssq)

    for h in range(2):
        parts = []
        for u in range(2):
            lifted = x_ref[h, u].astype(F32)
            ssq[h] += jnp.sum(lifted * lifted, axis=-1, keepdims=True)
            parts.append((lifted * gain_ref[0, u : u + 1]).astype(BF16))
        scaled = jnp.concatenate(parts, axis=1)
        for s in range(3):
            weights = jnp.concatenate(
                [w_ref[x, u, s] for u in range(2) for x in range(4)], axis=0
            )
            acc[h, s] += jnp.dot(scaled, weights, preferred_element_type=F32)

    @pl.when(step == pl.num_programs(0) - 1)
    def _():
        edges = []
        fronts = []
        for h in range(2):
            inv = lax.rsqrt(ssq[h] * (1.0 / 4096.0) + 1e-6)
            ends = []
            heads = []
            for s in range(3):
                rounded = (acc[h, s] * inv).astype(BF16)
                proj_ref[s, h] = rounded[:ROWS]
                ends.append(rounded[ROWS - HALO : ROWS].astype(F32))
                heads.append(rounded[ROWS:].astype(F32))
            edges.append(ends)
            fronts.append(heads)
        place = row_iota((16, CH)) // 2
        for h in range(2):
            mixing = three_taps(edges[h][1], taps_ref, 1) * three_taps(edges[h][2], taps_ref, 2)
            tail_ref[h, :LH] = mixing[HALO - LH :].astype(BF16)
            last = jnp.zeros((16, CH), F32)
            for s in range(3):
                moved = pltpu.roll(edges[h][s][HALO - 16 :], (2 * s + 2) % 16, 0)
                last = jnp.where(place == s, moved, last)
            tail_ref[h, LH:] = last.astype(BF16)
        ahead = [jnp.concatenate([fronts[0][s], fronts[1][s]], axis=0) for s in range(3)]
        mixing = three_taps(ahead[1], taps_ref, 1) * three_taps(ahead[2], taps_ref, 2)
        front_ref[:LH] = pltpu.roll(mixing, 2 * FRONT - 1, 0)[:LH].astype(BF16)
        last = jnp.zeros((16, CH), F32)
        for s in range(3):
            moved = pltpu.roll(ahead[s][LH - 8 : LH + 8], (2 * s - 7) % 16, 0)
            last = jnp.where(place == s, moved, last)
        front_ref[LH:] = last.astype(BF16)


def project(gathered, weights, gain, taps):
    count = ROWS + FRONT
    return pl.pallas_call(
        project_kernel,
        grid=(4,),
        in_specs=[
            pl.BlockSpec((2, 2, count, WIDE), lambda k: (0, k, 0, 0)),
            pl.BlockSpec((4, 2, 3, 128, CH), lambda k: (k, 0, 0, 0, 0)),
            pl.BlockSpec((1, 2, WIDE), lambda k: (k, 0, 0)),
            pl.BlockSpec((3, 3, CH), lambda k: (0, 0, 0)),
        ],
        out_specs=[
            pl.BlockSpec((3, 2, ROWS, CH), lambda k: (0, 0, 0, 0)),
            pl.BlockSpec((2, HALO, CH), lambda k: (0, 0, 0)),
            pl.BlockSpec((HALO, CH), lambda k: (0, 0)),
        ],
        out_shape=[
            jax.ShapeDtypeStruct((3, 2, ROWS, CH), BF16),
            jax.ShapeDtypeStruct((2, HALO, CH), BF16),
            jax.ShapeDtypeStruct((HALO, CH), BF16),
        ],
        scratch_shapes=[
            pltpu.VMEM((2, 3, count, CH), F32),
            pltpu.VMEM((2, count, 1), F32),
        ],
        compiler_params=pltpu.CompilerParams(vmem_limit_bytes=VMEM),
        cost_estimate=pl.CostEstimate(
            flops=2 * 2 * count * 4096 * 3 * CH, bytes_accessed=18_000_000, transcendentals=0
        ),
        name="project",
    )(gathered, weights, gain, taps)


def toeplitz_kernel(u_ref, out_ref):
    for g in range(GROUPS):
        wide = jnp.broadcast_to(u_ref[g : g + 1], (LH, 3 * LH))
        skewed = pltpu.roll(wide, 0, 1, stride=1, stride_axis=0)
        out_ref[g] = skewed[:, : 2 * LH].astype(BF16)


def toeplitz(filters):
    backwards = jnp.flip(filters.astype(F32), 1)
    row = jnp.pad(backwards, ((0, 0), (1, 2 * LH - 1)))
    return pl.pallas_call(
        toeplitz_kernel,
        out_shape=jax.ShapeDtypeStruct((GROUPS, LH, 2 * LH), BF16),
        compiler_params=pltpu.CompilerParams(vmem_limit_bytes=VMEM),
        name="toeplitz",
    )(row)


def mix_kernel(proj_ref, halo_ref, band_ref, taps_ref, bias_ref, w_ref, out_ref, before, edge):
    step = pl.program_id(0)

    @pl.when(step == 0)
    def _():
        for h in range(2):
            before[h] = halo_ref[h, :LH]
            last = halo_ref[h, LH:].astype(F32)
            for s in range(3):
                edge[h, s] = pltpu.roll(last, (6 - 2 * s) % 16, 0)[:8]

    queries = []
    mixes = []
    windows = []
    for h in range(2):
        feats = []
        for s in range(3):
            lifted = proj_ref[s, h].astype(F32)
            rows = jnp.concatenate([edge[h, s], lifted], axis=0)
            feats.append(three_taps(rows, taps_ref, s)[8:])
            edge[h, s] = lifted[LH - 8 :]
        mixing = (feats[1] * feats[2]).astype(BF16)
        queries.append(feats[0])
        mixes.append(mixing)
        windows.append(jnp.concatenate([before[h], mixing], axis=0))
        before[h] = mixing
    lane_group = lax.broadcasted_iota(jnp.int32, (LH, 2 * LH), 1) % LH // GSIZE
    halves = []
    for half in range(2):
        lanes = slice(half * LH, (half + 1) * LH)
        window = jnp.concatenate([windows[0][:, lanes], windows[1][:, lanes]], axis=1)
        total = jnp.zeros((LH, 2 * LH), F32)
        for g in range(GROUPS // 2):
            one = jnp.dot(band_ref[half * 8 + g], window, preferred_element_type=F32)
            total = jnp.where(lane_group == g, one, total)
        halves.append(total)
    gated = []
    for h in range(2):
        rows = slice(h * LH, (h + 1) * LH)
        filtered = jnp.concatenate([halves[0][:, rows], halves[1][:, rows]], axis=1)
        value = queries[h] * (filtered + bias_ref[...] * mixes[h].astype(F32))
        gated.append(value.astype(BF16))
    stacked = jnp.concatenate(gated, axis=0)
    for t in range(8):
        weights = jnp.concatenate([w_ref[t // 2 * 4 + x, t % 2] for x in range(4)], axis=1)
        partial = jnp.dot(stacked, weights, preferred_element_type=F32).astype(BF16)
        for h in range(2):
            out_ref[h, t] = partial[h * LH : (h + 1) * LH]


def mix_out(proj, halo, band, taps, bias, weights):
    return pl.pallas_call(
        mix_kernel,
        grid=(ROWS // LH,),
        in_specs=[
            pl.BlockSpec((3, 2, LH, CH), lambda b: (0, 0, b, 0)),
            pl.BlockSpec((2, HALO, CH), lambda b: (0, 0, 0)),
            pl.BlockSpec((GROUPS, LH, 2 * LH), lambda b: (0, 0, 0)),
            pl.BlockSpec((3, 3, CH), lambda b: (0, 0, 0)),
            pl.BlockSpec((1, CH), lambda b: (0, 0)),
            pl.BlockSpec((16, 2, CH, 128), lambda b: (0, 0, 0, 0)),
        ],
        out_specs=pl.BlockSpec((2, 8, LH, WIDE), lambda b: (0, 0, b, 0)),
        out_shape=jax.ShapeDtypeStruct((2, 8, ROWS, WIDE), BF16),
        scratch_shapes=[
            pltpu.VMEM((2, LH, CH), BF16),
            pltpu.VMEM((2, 3, 8, CH), F32),
        ],
        compiler_params=pltpu.CompilerParams(vmem_limit_bytes=VMEM),
        cost_estimate=pl.CostEstimate(
            flops=2 * 1024 * CH * 4096 * 2, bytes_accessed=14_000_000, transcendentals=0
        ),
        name="mix_out",
    )(proj, halo, band, taps, bias, weights)


def on_device(
    tokens, prior_rows, norm_gain, in_weight, short_filter, mr_filter, mr_bias, out_weight
):
    zh = lax.axis_index("zh")
    column = lax.axis_index("x")
    leading = (column == 0) & (lax.axis_index("y") == 0)

    padded = jnp.pad(prior_rows, ((0, 2 * FRONT - prior_rows.shape[0]), (0, 0)))
    own_front = lax.dynamic_slice_in_dim(padded, zh * FRONT, FRONT, 0)
    own = jnp.concatenate([tokens, own_front], axis=0)
    gathered = lax.all_gather(own, ("zh", "zl", "c"))
    gathered = gathered.reshape(2, 8, ROWS + FRONT, WIDE)
    gain = lax.all_gather(norm_gain, ("zl", "c")).astype(F32).reshape(4, 2, WIDE)

    halves = in_weight.reshape(3, 128, 2, CH).transpose(2, 0, 1, 3)
    halves = lax.all_to_all(halves, "zh", 0, 0)
    w_in = lax.all_gather(halves, ("y", "x"))
    out_halves = lax.all_to_all(out_weight.reshape(2, CH, 128), "zh", 0, 0)
    w_out = lax.all_gather(out_halves, ("y", "x"))

    taps = lax.dynamic_slice_in_dim(short_filter, zh * CH, CH, 2)
    bias = lax.dynamic_slice_in_dim(mr_bias, zh * CH, CH, 0)[None, :]
    band = toeplitz(lax.dynamic_slice_in_dim(mr_filter, zh * GROUPS, GROUPS, 0))

    proj, tail, front = project(gathered, w_in, gain, taps)

    last = column == 3
    to_first = jnp.where(last, tail[1], tail[0])
    to_second = jnp.where(last, tail[0], tail[1])
    first = lax.ppermute(to_first, ("y", "x"), [(i, i + 1) for i in range(15)])
    second = lax.ppermute(
        to_second, ("y", "x"), [(i, i // 4 * 4 + (i + 1) % 4) for i in range(16)]
    )
    halo = jnp.stack([jnp.where(leading, front, first), second])

    partial = mix_out(proj, halo, band, taps, bias, w_out)
    summed = lax.psum_scatter(
        partial.reshape(16, ROWS, WIDE), ("zh", "zl", "c"), scatter_dimension=0
    )
    return (tokens.astype(F32) + summed.astype(F32)).astype(BF16)


def solution(mesh):
    split = Mesh(mesh.devices.reshape(4, 2, 4, 4, 2), ("y", "zh", "x", "zl", "c"))
    seq, tensor = ("y", "zh", "x"), ("zl", "c")
    in_specs = (
        P(seq, tensor),
        P(None, tensor),
        P(tensor),
        P(None, seq, tensor),
        P(None, None, tensor),
        P(tensor, None),
        P(tensor),
        P(tensor, seq),
    )
    return jax.shard_map(
        on_device, mesh=split, in_specs=in_specs, out_specs=P(seq, tensor), check_vma=False
    )
```

```python
import jax
import jax.numpy as jnp
from jax import lax
from jax.experimental import pallas as pl
from jax.experimental.pallas import tpu as pltpu
from jax.sharding import Mesh, PartitionSpec as P

GSIZE = 16
LH = 128
ROWS = 512
FRONT = 80
WIDE = 512
CH = 256
GROUPS = CH // GSIZE
HALO = LH + 16
VMEM = 48 * 1024 * 1024
F32 = jnp.float32
BF16 = jnp.bfloat16


def row_iota(shape):
    return lax.broadcasted_iota(jnp.int32, shape, 0)


def three_taps(rows, taps, s):
    return (
        taps[0, s : s + 1] * rows
        + taps[1, s : s + 1] * pltpu.roll(rows, 1, 0)
        + taps[2, s : s + 1] * pltpu.roll(rows, 2, 0)
    )


def project_kernel(at_ref, x_ref, w_ref, taps_ref, proj_ref, tail_ref, front_ref, scaled, acc, ssq):
    step = pl.program_id(0)
    z_half = at_ref[1]
    column = at_ref[2]

    @pl.when(step == 0)
    def _():
        acc[...] = jnp.zeros_like(acc)
        ssq[...] = jnp.zeros_like(ssq)

    gains = [x_ref[1, u, ROWS + FRONT - 16 :].astype(F32)[15:] for u in range(2)]
    for h in range(2):
        for u in range(2):
            lifted = x_ref[h, u].astype(F32)
            ssq[h] += jnp.sum(lifted * lifted, axis=-1, keepdims=True)
            scaled[u] = (lifted * gains[u]).astype(BF16)
        parts = []
        for kind in range(2):
            block = z_half if kind == 0 else 1 - z_half
            for r in range(4):
                place = pl.multiple_of(lax.rem(column + r, 4) * 128, 128)
                parts.append(scaled[block, :, pl.ds(place, 128)])
        rows = jnp.concatenate(parts, axis=1)
        for s in range(3):
            weights = jnp.concatenate(
                [w_ref[0, kind, r, s] for kind in range(2) for r in range(4)], axis=0
            )
            acc[h, s] += jnp.dot(rows, weights, preferred_element_type=F32)

    @pl.when(step == pl.num_programs(0) - 1)
    def _():
        edges = []
        fronts = []
        for h in range(2):
            inv = lax.rsqrt(ssq[h] * (1.0 / 4096.0) + 1e-6)
            ends = []
            heads = []
            for s in range(3):
                rounded = (acc[h, s] * inv).astype(BF16)
                proj_ref[s, h] = rounded[:ROWS]
                ends.append(rounded[ROWS - HALO : ROWS].astype(F32))
                heads.append(rounded[ROWS:].astype(F32))
            edges.append(ends)
            fronts.append(heads)
        place = row_iota((16, CH)) // 2
        for h in range(2):
            mixing = three_taps(edges[h][1], taps_ref, 1) * three_taps(edges[h][2], taps_ref, 2)
            tail_ref[h, :LH] = mixing[HALO - LH :].astype(BF16)
            last = jnp.zeros((16, CH), F32)
            for s in range(3):
                moved = pltpu.roll(edges[h][s][HALO - 16 :], (2 * s + 2) % 16, 0)
                last = jnp.where(place == s, moved, last)
            tail_ref[h, LH:] = last.astype(BF16)
        ahead = [jnp.concatenate([fronts[0][s], fronts[1][s]], axis=0) for s in range(3)]
        mixing = three_taps(ahead[1], taps_ref, 1) * three_taps(ahead[2], taps_ref, 2)
        front_ref[:LH] = pltpu.roll(mixing, 2 * FRONT - 1, 0)[:LH].astype(BF16)
        last = jnp.zeros((16, CH), F32)
        for s in range(3):
            moved = pltpu.roll(ahead[s][LH - 8 : LH + 8], (2 * s - 7) % 16, 0)
            last = jnp.where(place == s, moved, last)
        front_ref[LH:] = last.astype(BF16)


def project(at, gathered, weights, taps):
    count = ROWS + FRONT
    return pl.pallas_call(
        project_kernel,
        grid_spec=pltpu.PrefetchScalarGridSpec(
            num_scalar_prefetch=1,
            grid=(4,),
            in_specs=[
                pl.BlockSpec((2, 2, count, WIDE), lambda k, at: (0, lax.rem(at[0] + k, 4), 0, 0)),
                pl.BlockSpec((1, 2, 4, 3, 128, CH), lambda k, at: (k, 0, 0, 0, 0, 0)),
                pl.BlockSpec((3, 3, CH), lambda k, at: (0, 0, 0)),
            ],
            out_specs=[
                pl.BlockSpec((3, 2, ROWS, CH), lambda k, at: (0, 0, 0, 0)),
                pl.BlockSpec((2, HALO, CH), lambda k, at: (0, 0, 0)),
                pl.BlockSpec((HALO, CH), lambda k, at: (0, 0)),
            ],
            scratch_shapes=[
                pltpu.VMEM((2, count, WIDE), BF16),
                pltpu.VMEM((2, 3, count, CH), F32),
                pltpu.VMEM((2, count, 1), F32),
            ],
        ),
        out_shape=[
            jax.ShapeDtypeStruct((3, 2, ROWS, CH), BF16),
            jax.ShapeDtypeStruct((2, HALO, CH), BF16),
            jax.ShapeDtypeStruct((HALO, CH), BF16),
        ],
        compiler_params=pltpu.CompilerParams(vmem_limit_bytes=VMEM),
        cost_estimate=pl.CostEstimate(
            flops=2 * 2 * count * 4096 * 3 * CH, bytes_accessed=18_000_000, transcendentals=0
        ),
        name="project",
    )(at, gathered, weights, taps)


def toeplitz_kernel(u_ref, out_ref):
    for g in range(GROUPS):
        wide = jnp.broadcast_to(u_ref[g : g + 1], (LH, 3 * LH))
        skewed = pltpu.roll(wide, 0, 1, stride=1, stride_axis=0)
        out_ref[g] = skewed[:, : 2 * LH].astype(BF16)


def toeplitz(filters):
    backwards = jnp.flip(filters.astype(F32), 1)
    row = jnp.pad(backwards, ((0, 0), (1, 2 * LH - 1)))
    return pl.pallas_call(
        toeplitz_kernel,
        out_shape=jax.ShapeDtypeStruct((GROUPS, LH, 2 * LH), BF16),
        compiler_params=pltpu.CompilerParams(vmem_limit_bytes=VMEM),
        name="toeplitz",
    )(row)


def mix_kernel(at_ref, proj_ref, halo_ref, band_ref, taps_ref, bias_ref, w_ref, out_ref, before, edge):
    step = pl.program_id(0)

    @pl.when(step == 0)
    def _():
        for h in range(2):
            before[h] = halo_ref[h, :LH]
            last = halo_ref[h, LH:].astype(F32)
            for s in range(3):
                edge[h, s] = pltpu.roll(last, (6 - 2 * s) % 16, 0)[:8]

    queries = []
    mixes = []
    windows = []
    for h in range(2):
        feats = []
        for s in range(3):
            lifted = proj_ref[s, h].astype(F32)
            rows = jnp.concatenate([edge[h, s], lifted], axis=0)
            feats.append(three_taps(rows, taps_ref, s)[8:])
            edge[h, s] = lifted[LH - 8 :]
        mixing = (feats[1] * feats[2]).astype(BF16)
        queries.append(feats[0])
        mixes.append(mixing)
        windows.append(jnp.concatenate([before[h], mixing], axis=0))
        before[h] = mixing
    lane_group = lax.broadcasted_iota(jnp.int32, (LH, 2 * LH), 1) % LH // GSIZE
    halves = []
    for half in range(2):
        lanes = slice(half * LH, (half + 1) * LH)
        window = jnp.concatenate([windows[0][:, lanes], windows[1][:, lanes]], axis=1)
        total = jnp.zeros((LH, 2 * LH), F32)
        for g in range(GROUPS // 2):
            one = jnp.dot(band_ref[half * 8 + g], window, preferred_element_type=F32)
            total = jnp.where(lane_group == g, one, total)
        halves.append(total)
    gated = []
    for h in range(2):
        rows = slice(h * LH, (h + 1) * LH)
        filtered = jnp.concatenate([halves[0][:, rows], halves[1][:, rows]], axis=1)
        value = queries[h] * (filtered + bias_ref[...] * mixes[h].astype(F32))
        gated.append(value.astype(BF16))
    stacked = jnp.concatenate(gated, axis=0)
    for k in range(4):
        for kind in range(2):
            z_half = at_ref[1] if kind == 0 else 1 - at_ref[1]
            block = 2 * lax.rem(at_ref[0] + k, 4) + z_half
            weights = jnp.concatenate([w_ref[k, kind, r] for r in range(4)], axis=1)
            partial = jnp.dot(stacked, weights, preferred_element_type=F32).astype(BF16)
            for r in range(4):
                place = pl.multiple_of(lax.rem(at_ref[2] + r, 4) * 128, 128)
                for h in range(2):
                    out_ref[h, block, :, pl.ds(place, 128)] = partial[
                        h * LH : (h + 1) * LH, r * 128 : (r + 1) * 128
                    ]


def mix_out(at, proj, halo, band, taps, bias, weights):
    return pl.pallas_call(
        mix_kernel,
        grid_spec=pltpu.PrefetchScalarGridSpec(
            num_scalar_prefetch=1,
            grid=(ROWS // LH,),
            in_specs=[
                pl.BlockSpec((3, 2, LH, CH), lambda b, at: (0, 0, b, 0)),
                pl.BlockSpec((2, HALO, CH), lambda b, at: (0, 0, 0)),
                pl.BlockSpec((GROUPS, LH, 2 * LH), lambda b, at: (0, 0, 0)),
                pl.BlockSpec((3, 3, CH), lambda b, at: (0, 0, 0)),
                pl.BlockSpec((1, CH), lambda b, at: (0, 0)),
                pl.BlockSpec((4, 2, 4, CH, 128), lambda b, at: (0, 0, 0, 0, 0)),
            ],
            out_specs=pl.BlockSpec((2, 8, LH, WIDE), lambda b, at: (0, 0, b, 0)),
            scratch_shapes=[
                pltpu.VMEM((2, LH, CH), BF16),
                pltpu.VMEM((2, 3, 8, CH), F32),
            ],
        ),
        out_shape=jax.ShapeDtypeStruct((2, 8, ROWS, WIDE), BF16),
        compiler_params=pltpu.CompilerParams(vmem_limit_bytes=VMEM),
        cost_estimate=pl.CostEstimate(
            flops=2 * 1024 * CH * 4096 * 2, bytes_accessed=14_000_000, transcendentals=0
        ),
        name="mix_out",
    )(at, proj, halo, band, taps, bias, weights)


UP = [(i, (i + 1) % 4) for i in range(4)]
DOWN = [(i, (i + 3) % 4) for i in range(4)]


def ring_gather(piece, axis, cut):
    behind = lax.ppermute(piece, axis, UP)
    ahead = lax.ppermute(piece, axis, DOWN)
    half = piece.shape[cut] // 2
    far = jnp.concatenate(
        [
            lax.ppermute(lax.slice_in_dim(behind, 0, half, axis=cut), axis, UP),
            lax.ppermute(lax.slice_in_dim(ahead, half, 2 * half, axis=cut), axis, DOWN),
        ],
        axis=cut,
    )
    return jnp.stack([piece, ahead, far, behind])


def plane_gather(piece, first):
    line = ring_gather(piece, first, piece.ndim - 2)
    both = ring_gather(line, "x" if first == "y" else "y", 0)
    return both.swapaxes(0, 1) if first == "y" else both


def on_device(
    tokens, prior_rows, norm_gain, in_weight, short_filter, mr_filter, mr_bias, out_weight
):
    zh = lax.axis_index("zh")
    column = lax.axis_index("x")
    leading = (column == 0) & (lax.axis_index("y") == 0)

    at = jnp.stack([lax.axis_index("y"), zh, column])
    spare = 2 * FRONT - prior_rows.shape[0]
    padded = jnp.concatenate(
        [prior_rows, jnp.zeros((spare - 1, WIDE), BF16), norm_gain[None, :]], axis=0
    )
    own_front = lax.dynamic_slice_in_dim(padded, zh * FRONT, FRONT, 0)
    own = jnp.concatenate([tokens, own_front], axis=0)
    gathered = lax.all_gather(own, ("zh", "zl", "c"))
    gathered = gathered.reshape(2, 8, ROWS + FRONT, WIDE)

    def swapped(left, right):
        kept = jnp.where(zh == 0, left, right)
        other = jnp.where(zh == 0, right, left)
        return kept, lax.ppermute(other, "zh", [(0, 1), (1, 0)])

    kept, got = swapped(in_weight[..., :CH], in_weight[..., CH:])
    w_in = jnp.stack([plane_gather(kept, "x"), plane_gather(got, "y")], axis=1)
    kept, got = swapped(out_weight[:CH], out_weight[CH:])
    w_out = jnp.stack([plane_gather(kept, "x"), plane_gather(got, "y")], axis=1)

    taps = lax.dynamic_slice_in_dim(short_filter, zh * CH, CH, 2)
    bias = lax.dynamic_slice_in_dim(mr_bias, zh * CH, CH, 0)[None, :]
    band = toeplitz(lax.dynamic_slice_in_dim(mr_filter, zh * GROUPS, GROUPS, 0))

    proj, tail, front = project(at, gathered, w_in, taps)

    last = column == 3
    to_first = jnp.where(last, tail[1], tail[0])
    to_second = jnp.where(last, tail[0], tail[1])
    first = lax.ppermute(to_first, ("y", "x"), [(i, i + 1) for i in range(15)])
    second = lax.ppermute(
        to_second, ("y", "x"), [(i, i // 4 * 4 + (i + 1) % 4) for i in range(16)]
    )
    halo = jnp.stack([jnp.where(leading, front, first), second])

    partial = mix_out(at, proj, halo, band, taps, bias, w_out)
    summed = lax.psum_scatter(
        partial.reshape(16, ROWS, WIDE), ("zh", "zl", "c"), scatter_dimension=0
    )
    return (tokens.astype(F32) + summed.astype(F32)).astype(BF16)


def solution(mesh):
    split = Mesh(mesh.devices.reshape(4, 2, 4, 4, 2), ("y", "zh", "x", "zl", "c"))
    seq, tensor = ("y", "zh", "x"), ("zl", "c")
    in_specs = (
        P(seq, tensor),
        P(None, tensor),
        P(tensor),
        P(None, seq, tensor),
        P(None, None, tensor),
        P(tensor, None),
        P(tensor),
        P(tensor, seq),
    )
    return jax.shard_map(
        on_device, mesh=split, in_specs=in_specs, out_specs=P(seq, tensor), check_vma=False
    )
```

```python
import jax
import jax.numpy as jnp
from jax import lax
from jax.experimental import pallas as pl
from jax.experimental.pallas import tpu as pltpu
from jax.sharding import Mesh, PartitionSpec as P

GSIZE = 16
LH = 128
ROWS = 512
FRONT = 80
WIDE = 512
CH = 256
GROUPS = CH // GSIZE
HALO = LH + 16
VMEM = 48 * 1024 * 1024
F32 = jnp.float32
BF16 = jnp.bfloat16


def row_iota(shape):
    return lax.broadcasted_iota(jnp.int32, shape, 0)


def three_taps(rows, taps, s):
    return (
        taps[0, s : s + 1] * rows
        + taps[1, s : s + 1] * pltpu.roll(rows, 1, 0)
        + taps[2, s : s + 1] * pltpu.roll(rows, 2, 0)
    )


def project_kernel(at_ref, x_ref, *refs):
    kept, got = refs[:5], refs[5:10]
    taps_ref, proj_ref, tail_ref, front_ref, wide, acc, ssq, sems = refs[10:]
    step = pl.program_id(0)
    row, z_half, column = at_ref[0], at_ref[1], at_ref[2]

    copies = []
    for kind, parts in enumerate((kept, got)):
        half = z_half if kind == 0 else 1 - z_half
        own, ahead, far_a, far_b, behind = parts
        for i in range(4):
            for j in range(4):
                if i == 2:
                    source = (far_a if j < 2 else far_b).at[j % 2]
                else:
                    source = (own, ahead, None, behind)[i].at[j]
                y, x = (i, j) if kind == 0 else (j, i)
                place = wide.at[lax.rem(row + y, 4), :, half, lax.rem(column + x, 4)]
                copies.append((y, pltpu.make_async_copy(source, place, sems.at[kind, i, j])))

    @pl.when(step == 0)
    def _():
        acc[...] = jnp.zeros_like(acc)
        ssq[...] = jnp.zeros_like(ssq)
        for k in range(4):
            for y, copy in copies:
                if y == k:
                    copy.start()

    for k in range(4):

        @pl.when(step == k)
        def _(k=k):
            for y, copy in copies:
                if y == k:
                    copy.wait()

    place = lax.rem(row + step, 4)
    gains = [x_ref[1, u, ROWS + FRONT - 16 :].astype(F32)[15:] for u in range(2)]
    for h in range(2):
        parts = []
        for u in range(2):
            lifted = x_ref[h, u].astype(F32)
            ssq[h] += jnp.sum(lifted * lifted, axis=-1, keepdims=True)
            parts.append((lifted * gains[u]).astype(BF16))
        scaled = jnp.concatenate(parts, axis=1)
        for s in range(3):
            weights = wide[place, s].reshape(2 * WIDE, CH)
            acc[h, s] += jnp.dot(scaled, weights, preferred_element_type=F32)

    @pl.when(step == pl.num_programs(0) - 1)
    def _():
        edges = []
        fronts = []
        for h in range(2):
            inv = lax.rsqrt(ssq[h] * (1.0 / 4096.0) + 1e-6)
            ends = []
            heads = []
            for s in range(3):
                rounded = (acc[h, s] * inv).astype(BF16)
                proj_ref[s, h] = rounded[:ROWS]
                ends.append(rounded[ROWS - HALO : ROWS].astype(F32))
                heads.append(rounded[ROWS:].astype(F32))
            edges.append(ends)
            fronts.append(heads)
        place = row_iota((16, CH)) // 2
        for h in range(2):
            mixing = three_taps(edges[h][1], taps_ref, 1) * three_taps(edges[h][2], taps_ref, 2)
            tail_ref[h, :LH] = mixing[HALO - LH :].astype(BF16)
            last = jnp.zeros((16, CH), F32)
            for s in range(3):
                moved = pltpu.roll(edges[h][s][HALO - 16 :], (2 * s + 2) % 16, 0)
                last = jnp.where(place == s, moved, last)
            tail_ref[h, LH:] = last.astype(BF16)
        ahead = [jnp.concatenate([fronts[0][s], fronts[1][s]], axis=0) for s in range(3)]
        mixing = three_taps(ahead[1], taps_ref, 1) * three_taps(ahead[2], taps_ref, 2)
        front_ref[:LH] = pltpu.roll(mixing, 2 * FRONT - 1, 0)[:LH].astype(BF16)
        last = jnp.zeros((16, CH), F32)
        for s in range(3):
            moved = pltpu.roll(ahead[s][LH - 8 : LH + 8], (2 * s - 7) % 16, 0)
            last = jnp.where(place == s, moved, last)
        front_ref[LH:] = last.astype(BF16)


def project(at, gathered, kept, got, taps):
    count = ROWS + FRONT
    return pl.pallas_call(
        project_kernel,
        grid_spec=pltpu.PrefetchScalarGridSpec(
            num_scalar_prefetch=1,
            grid=(4,),
            in_specs=[
                pl.BlockSpec((2, 2, count, WIDE), lambda k, at: (0, lax.rem(at[0] + k, 4), 0, 0)),
                *[pl.BlockSpec(memory_space=pl.ANY)] * 10,
                pl.BlockSpec((3, 3, CH), lambda k, at: (0, 0, 0)),
            ],
            out_specs=[
                pl.BlockSpec((3, 2, ROWS, CH), lambda k, at: (0, 0, 0, 0)),
                pl.BlockSpec((2, HALO, CH), lambda k, at: (0, 0, 0)),
                pl.BlockSpec((HALO, CH), lambda k, at: (0, 0)),
            ],
            scratch_shapes=[
                pltpu.VMEM((4, 3, 2, 4, 128, CH), BF16),
                pltpu.VMEM((2, 3, count, CH), F32),
                pltpu.VMEM((2, count, 1), F32),
                pltpu.SemaphoreType.DMA((2, 4, 4)),
            ],
        ),
        out_shape=[
            jax.ShapeDtypeStruct((3, 2, ROWS, CH), BF16),
            jax.ShapeDtypeStruct((2, HALO, CH), BF16),
            jax.ShapeDtypeStruct((HALO, CH), BF16),
        ],
        compiler_params=pltpu.CompilerParams(vmem_limit_bytes=VMEM),
        cost_estimate=pl.CostEstimate(
            flops=2 * 2 * count * 4096 * 3 * CH, bytes_accessed=18_000_000, transcendentals=0
        ),
        name="project",
    )(at, gathered, *kept, *got, taps)


def toeplitz_kernel(u_ref, out_ref):
    for g in range(GROUPS):
        wide = jnp.broadcast_to(u_ref[g : g + 1], (LH, 3 * LH))
        skewed = pltpu.roll(wide, 0, 1, stride=1, stride_axis=0)
        out_ref[g] = skewed[:, : 2 * LH].astype(BF16)


def toeplitz(filters):
    backwards = jnp.flip(filters.astype(F32), 1)
    row = jnp.pad(backwards, ((0, 0), (1, 2 * LH - 1)))
    return pl.pallas_call(
        toeplitz_kernel,
        out_shape=jax.ShapeDtypeStruct((GROUPS, LH, 2 * LH), BF16),
        compiler_params=pltpu.CompilerParams(vmem_limit_bytes=VMEM),
        name="toeplitz",
    )(row)


def mix_kernel(proj_ref, halo_ref, band_ref, taps_ref, bias_ref, out_ref, before, edge):
    step = pl.program_id(0)

    @pl.when(step == 0)
    def _():
        for h in range(2):
            before[h] = halo_ref[h, :LH]
            last = halo_ref[h, LH:].astype(F32)
            for s in range(3):
                edge[h, s] = pltpu.roll(last, (6 - 2 * s) % 16, 0)[:8]

    queries = []
    mixes = []
    windows = []
    for h in range(2):
        feats = []
        for s in range(3):
            lifted = proj_ref[s, h].astype(F32)
            rows = jnp.concatenate([edge[h, s], lifted], axis=0)
            feats.append(three_taps(rows, taps_ref, s)[8:])
            edge[h, s] = lifted[LH - 8 :]
        mixing = (feats[1] * feats[2]).astype(BF16)
        queries.append(feats[0])
        mixes.append(mixing)
        windows.append(jnp.concatenate([before[h], mixing], axis=0))
        before[h] = mixing
    lane_group = lax.broadcasted_iota(jnp.int32, (LH, 2 * LH), 1) % LH // GSIZE
    halves = []
    for half in range(2):
        lanes = slice(half * LH, (half + 1) * LH)
        window = jnp.concatenate([windows[0][:, lanes], windows[1][:, lanes]], axis=1)
        total = jnp.zeros((LH, 2 * LH), F32)
        for g in range(GROUPS // 2):
            one = jnp.dot(band_ref[half * 8 + g], window, preferred_element_type=F32)
            total = jnp.where(lane_group == g, one, total)
        halves.append(total)
    for h in range(2):
        rows = slice(h * LH, (h + 1) * LH)
        filtered = jnp.concatenate([halves[0][:, rows], halves[1][:, rows]], axis=1)
        value = queries[h] * (filtered + bias_ref[...] * mixes[h].astype(F32))
        out_ref[h] = value.astype(BF16)


def mix(proj, halo, band, taps, bias):
    return pl.pallas_call(
        mix_kernel,
        grid=(ROWS // LH,),
        in_specs=[
            pl.BlockSpec((3, 2, LH, CH), lambda b: (0, 0, b, 0)),
            pl.BlockSpec((2, HALO, CH), lambda b: (0, 0, 0)),
            pl.BlockSpec((GROUPS, LH, 2 * LH), lambda b: (0, 0, 0)),
            pl.BlockSpec((3, 3, CH), lambda b: (0, 0, 0)),
            pl.BlockSpec((1, CH), lambda b: (0, 0)),
        ],
        out_specs=pl.BlockSpec((2, LH, CH), lambda b: (0, b, 0)),
        out_shape=jax.ShapeDtypeStruct((2, ROWS, CH), BF16),
        scratch_shapes=[
            pltpu.VMEM((2, LH, CH), BF16),
            pltpu.VMEM((2, 3, 8, CH), F32),
        ],
        compiler_params=pltpu.CompilerParams(vmem_limit_bytes=VMEM),
        cost_estimate=pl.CostEstimate(
            flops=2 * 1024 * CH * 2048, bytes_accessed=4_000_000, transcendentals=0
        ),
        name="mix",
    )(proj, halo, band, taps, bias)


def out_kernel(at_ref, mine_ref, other_ref, *refs):
    parts, (out_ref, wide, sems) = refs[:5], refs[5:]
    own, ahead, far_a, far_b, behind = parts
    row, column, crossed = at_ref[0], at_ref[2], at_ref[3]
    copies = []
    for i in range(4):
        for j in range(4):
            if i == 2:
                source = (far_a if j < 2 else far_b).at[j % 2]
            else:
                source = (own, ahead, None, behind)[i].at[j]
            lanes = pl.ds(pl.multiple_of(lax.rem(column + j, 4) * 128, 128), 128)
            place = wide.at[lax.rem(row + i, 4), :, lanes]
            copies.append(pltpu.make_async_copy(source, place, sems.at[i, j]))

    @pl.when(pl.program_id(0) == 0)
    def _():
        for copy in copies:
            copy.start()
        for copy in copies:
            copy.wait()

    swap = crossed == 1
    first = jnp.where(swap, other_ref[0], mine_ref[0])
    second = jnp.where(swap, mine_ref[0], other_ref[0])
    rows = jnp.concatenate([first, second], axis=1)
    for y in range(4):
        out_ref[0, y] = jnp.dot(rows, wide[y], preferred_element_type=F32).astype(BF16)


def project_out(at, mine, other, parts):
    return pl.pallas_call(
        out_kernel,
        grid_spec=pltpu.PrefetchScalarGridSpec(
            num_scalar_prefetch=1,
            grid=(2,),
            in_specs=[
                pl.BlockSpec((1, ROWS, CH), lambda h, at: (h, 0, 0)),
                pl.BlockSpec((1, ROWS, CH), lambda h, at: (h, 0, 0)),
                *[pl.BlockSpec(memory_space=pl.ANY)] * 5,
            ],
            out_specs=pl.BlockSpec((1, 4, ROWS, WIDE), lambda h, at: (h, 0, 0, 0)),
            scratch_shapes=[
                pltpu.VMEM((4, 2 * CH, WIDE), BF16),
                pltpu.SemaphoreType.DMA((4, 4)),
            ],
        ),
        out_shape=jax.ShapeDtypeStruct((2, 4, ROWS, WIDE), BF16),
        compiler_params=pltpu.CompilerParams(vmem_limit_bytes=VMEM),
        cost_estimate=pl.CostEstimate(
            flops=2 * 1024 * 2 * CH * 2048, bytes_accessed=8_000_000, transcendentals=0
        ),
        name="project_out",
    )(at, mine, other, *parts)


UP = [(i, (i + 1) % 4) for i in range(4)]
DOWN = [(i, (i + 3) % 4) for i in range(4)]


def ring_parts(piece, axis, cut):
    behind = lax.ppermute(piece, axis, UP)
    ahead = lax.ppermute(piece, axis, DOWN)
    half = piece.shape[cut] // 2
    far_a = lax.ppermute(lax.slice_in_dim(behind, 0, half, axis=cut), axis, UP)
    far_b = lax.ppermute(lax.slice_in_dim(ahead, half, 2 * half, axis=cut), axis, DOWN)
    return piece, ahead, far_a, far_b, behind


def ring_line(piece, axis, cut):
    own, ahead, far_a, far_b, behind = ring_parts(piece, axis, cut)
    return jnp.stack([own, ahead, jnp.concatenate([far_a, far_b], axis=cut), behind])


def on_device(
    tokens, prior_rows, norm_gain, in_weight, short_filter, mr_filter, mr_bias, out_weight
):
    zh = lax.axis_index("zh")
    column = lax.axis_index("x")
    leading = (column == 0) & (lax.axis_index("y") == 0)

    core = lax.axis_index("c")
    at = jnp.stack([lax.axis_index("y"), zh, column, zh ^ core])
    spare = 2 * FRONT - prior_rows.shape[0]
    padded = jnp.concatenate(
        [prior_rows, jnp.zeros((spare - 1, WIDE), BF16), norm_gain[None, :]], axis=0
    )
    own_front = lax.dynamic_slice_in_dim(padded, zh * FRONT, FRONT, 0)
    own = jnp.concatenate([tokens, own_front], axis=0)
    gathered = lax.all_gather(own, ("zh", "zl", "c"))
    gathered = gathered.reshape(2, 8, ROWS + FRONT, WIDE)

    left, right = in_weight[..., :CH], in_weight[..., CH:]
    kept = jnp.where(zh == 0, left, right)
    got = lax.ppermute(jnp.where(zh == 0, right, left), "zh", [(0, 1), (1, 0)])
    kept_line = ring_line(kept, "x", 1)
    got_line = ring_line(got, "y", 1)
    kept_parts = ring_parts(kept_line, "y", 0)
    got_parts = ring_parts(got_line, "x", 0)

    out_weight, kept_parts = lax.optimization_barrier((out_weight, kept_parts))
    pieces = []
    for k in range(2):
        chosen = lax.dynamic_slice_in_dim(out_weight, (core ^ k) * CH, CH, 0)
        pairs = [(a * 2 + b, (b ^ k) * 2 + a) for a in range(2) for b in range(2)]
        pieces.append(lax.ppermute(chosen, ("zh", "c"), pairs))
    out_line = ring_line(jnp.concatenate(pieces, axis=0), "x", 0)
    out_line, kept_parts, got_parts = lax.optimization_barrier((out_line, kept_parts, got_parts))
    out_parts = ring_parts(out_line, "y", 0)

    taps = lax.dynamic_slice_in_dim(short_filter, zh * CH, CH, 2)
    bias = lax.dynamic_slice_in_dim(mr_bias, zh * CH, CH, 0)[None, :]
    band = toeplitz(lax.dynamic_slice_in_dim(mr_filter, zh * GROUPS, GROUPS, 0))

    proj, tail, front = project(at, gathered, kept_parts, got_parts, taps)

    last = column == 3
    to_first = jnp.where(last, tail[1], tail[0])
    to_second = jnp.where(last, tail[0], tail[1])
    first = lax.ppermute(to_first, ("y", "x"), [(i, i + 1) for i in range(15)])
    second = lax.ppermute(
        to_second, ("y", "x"), [(i, i // 4 * 4 + (i + 1) % 4) for i in range(16)]
    )
    halo = jnp.stack([jnp.where(leading, front, first), second])

    mine = mix(proj, halo, band, taps, bias)
    other = lax.ppermute(mine, "c", [(0, 1), (1, 0)])
    partial = project_out(at, mine, other, out_parts)
    summed = lax.psum_scatter(
        partial.reshape(8, ROWS, WIDE), ("zh", "zl"), scatter_dimension=0
    )
    return (tokens.astype(F32) + summed.astype(F32)).astype(BF16)


def solution(mesh):
    split = Mesh(mesh.devices.reshape(4, 2, 4, 4, 2), ("y", "zh", "x", "zl", "c"))
    seq, tensor = ("y", "zh", "x"), ("zl", "c")
    in_specs = (
        P(seq, tensor),
        P(None, tensor),
        P(tensor),
        P(None, seq, tensor),
        P(None, None, tensor),
        P(tensor, None),
        P(tensor),
        P(tensor, seq),
    )
    return jax.shard_map(
        on_device, mesh=split, in_specs=in_specs, out_specs=P(seq, tensor), check_vma=False
    )
```

```python
import jax
import jax.numpy as jnp
from jax import lax
from jax.experimental import pallas as pl
from jax.experimental.pallas import tpu as pltpu
from jax.sharding import Mesh, PartitionSpec as P

GSIZE = 16
LH = 128
ROWS = 512
TILE = 80
SHARE = 72
HALF = ROWS // 2
WIDE = 512
CH = 256
GROUPS = CH // GSIZE
HALO = LH + 16
MIB = 1024 * 1024
F32 = jnp.float32
BF16 = jnp.bfloat16


def row_iota(shape):
    return lax.broadcasted_iota(jnp.int32, shape, 0)


def three_taps(rows, taps, s):
    return (
        taps[0, s : s + 1] * rows
        + taps[1, s : s + 1] * pltpu.roll(rows, 1, 0)
        + taps[2, s : s + 1] * pltpu.roll(rows, 2, 0)
    )


def weight_copies(at_ref, refs, wide, sems):
    copies = []
    for kind in range(2):
        half = at_ref[8] if kind == 0 else 1 - at_ref[8]
        for i in range(4):
            for j in range(4):
                source = refs[2 * kind + i // 2].at[i % 2, j]
                y, x = (i, j) if kind == 0 else (j, i)
                place = wide.at[:, at_ref[y], half, at_ref[4 + x]]
                copies.append(pltpu.make_async_copy(source, place, sems.at[kind, i, j]))
    return copies


def last_rows(parts, first, shift):
    place = row_iota((16, CH)) // 2
    out = jnp.zeros((16, CH), F32)
    for s in range(3):
        moved = pltpu.roll(parts[s][first : first + 16], (2 * s + shift) % 16, 0)
        out = jnp.where(place == s, moved, out)
    return out.astype(BF16)


def project_kernel(at_ref, x_ref, *refs):
    taps_ref, proj_ref, tail_ref, mid_ref, front_ref, wide, scaled, ahead, sems = refs[4:]
    copies = weight_copies(at_ref, refs, wide, sems)
    first_step = pl.program_id(0) == 0

    @pl.when(first_step)
    def _():
        for copy in copies:
            copy.start()

    ssq = jnp.zeros((ROWS + TILE, 1), F32)
    for t in range(8):
        lifted = x_ref[0, t].astype(F32)
        ssq += jnp.sum(lifted * lifted, axis=-1, keepdims=True)
        gain = lifted[ROWS + TILE - 1 :]
        scaled[:, t * WIDE : (t + 1) * WIDE] = (lifted * gain).astype(BF16)
    inv = lax.rsqrt(ssq * (1.0 / 4096.0) + 1e-6)

    @pl.when(first_step)
    def _():
        for copy in copies:
            copy.wait()

    for s in range(3):
        total = jnp.dot(
            scaled[...], wide[s].reshape(8 * WIDE, CH), preferred_element_type=F32
        )
        rounded = (total * inv).astype(BF16)
        proj_ref[s, 0] = rounded[:ROWS]

        @pl.when(first_step)
        def _(s=s, rounded=rounded):
            ahead[s, :SHARE] = rounded[ROWS:].astype(F32)[:SHARE]

        @pl.when(pl.program_id(0) == 1)
        def _(s=s, rounded=rounded):
            ahead[s, SHARE:] = rounded[ROWS:].astype(F32)

    for end, ref in ((ROWS, tail_ref), (HALF, mid_ref)):
        rows = [proj_ref[s, 0, end - HALO : end].astype(F32) for s in range(3)]
        mixing = three_taps(rows[1], taps_ref, 1) * three_taps(rows[2], taps_ref, 2)
        ref[0, :LH] = mixing[HALO - LH :].astype(BF16)
        ref[0, LH:] = last_rows(rows, HALO - 16, 2)

    @pl.when(pl.program_id(0) == 1)
    def _():
        mixing = three_taps(ahead[1], taps_ref, 1) * three_taps(ahead[2], taps_ref, 2)
        front_ref[:LH] = pltpu.roll(mixing, SHARE + TILE - 1, 0)[:LH].astype(BF16)
        front_ref[LH:] = last_rows(ahead, LH - 8, -7)


def project(at, gathered, weights, taps):
    return pl.pallas_call(
        project_kernel,
        grid_spec=pltpu.PrefetchScalarGridSpec(
            num_scalar_prefetch=1,
            grid=(2,),
            in_specs=[
                pl.BlockSpec((1, 8, ROWS + TILE, WIDE), lambda h, at: (h, 0, 0, 0)),
                *[pl.BlockSpec(memory_space=pl.ANY)] * 4,
                pl.BlockSpec((3, 3, CH), lambda h, at: (0, 0, 0)),
            ],
            out_specs=[
                pl.BlockSpec((3, 1, ROWS, CH), lambda h, at: (0, h, 0, 0)),
                pl.BlockSpec((1, HALO, CH), lambda h, at: (h, 0, 0)),
                pl.BlockSpec((1, HALO, CH), lambda h, at: (h, 0, 0)),
                pl.BlockSpec((HALO, CH), lambda h, at: (0, 0)),
            ],
            scratch_shapes=[
                pltpu.VMEM((3, 4, 2, 4, 128, CH), BF16),
                pltpu.VMEM((ROWS + TILE, 8 * WIDE), BF16),
                pltpu.VMEM((3, SHARE + TILE, CH), F32),
                pltpu.SemaphoreType.DMA((2, 4, 4)),
            ],
        ),
        out_shape=[
            jax.ShapeDtypeStruct((3, 2, ROWS, CH), BF16),
            jax.ShapeDtypeStruct((2, HALO, CH), BF16),
            jax.ShapeDtypeStruct((2, HALO, CH), BF16),
            jax.ShapeDtypeStruct((HALO, CH), BF16),
        ],
        compiler_params=pltpu.CompilerParams(vmem_limit_bytes=46 * MIB),
        cost_estimate=pl.CostEstimate(
            flops=2 * 2 * ROWS * 4096 * 3 * CH, bytes_accessed=18_000_000, transcendentals=0
        ),
        name="project",
    )(at, gathered, *weights, taps)


def toeplitz_kernel(u_ref, out_ref):
    for g in range(GROUPS):
        wide = jnp.broadcast_to(u_ref[g : g + 1], (LH, 3 * LH))
        skewed = pltpu.roll(wide, 0, 1, stride=1, stride_axis=0)
        out_ref[g] = skewed[:, : 2 * LH].astype(BF16)


def toeplitz(filters):
    backwards = jnp.flip(filters.astype(F32), 1)
    row = jnp.pad(backwards, ((0, 0), (1, 2 * LH - 1)))
    return pl.pallas_call(
        toeplitz_kernel,
        out_shape=jax.ShapeDtypeStruct((GROUPS, LH, 2 * LH), BF16),
        compiler_params=pltpu.CompilerParams(vmem_limit_bytes=8 * MIB),
        name="toeplitz",
    )(row)


def mix_kernel(proj_ref, halo_ref, band_ref, taps_ref, bias_ref, out_ref, before, edge):
    step = pl.program_id(0)

    @pl.when(step == 0)
    def _():
        for h in range(2):
            before[h] = halo_ref[h, :LH]
            last = halo_ref[h, LH:].astype(F32)
            for s in range(3):
                edge[h, s] = pltpu.roll(last, (6 - 2 * s) % 16, 0)[:8]

    queries = []
    mixes = []
    windows = []
    for h in range(2):
        feats = []
        for s in range(3):
            lifted = proj_ref[s, h].astype(F32)
            rows = jnp.concatenate([edge[h, s], lifted], axis=0)
            feats.append(three_taps(rows, taps_ref, s)[8:])
            edge[h, s] = lifted[LH - 8 :]
        mixing = (feats[1] * feats[2]).astype(BF16)
        queries.append(feats[0])
        mixes.append(mixing)
        windows.append(jnp.concatenate([before[h], mixing], axis=0))
        before[h] = mixing
    lane_group = lax.broadcasted_iota(jnp.int32, (LH, 2 * LH), 1) % LH // GSIZE
    halves = []
    for half in range(2):
        lanes = slice(half * LH, (half + 1) * LH)
        window = jnp.concatenate([windows[0][:, lanes], windows[1][:, lanes]], axis=1)
        total = jnp.zeros((LH, 2 * LH), F32)
        for g in range(GROUPS // 2):
            one = jnp.dot(band_ref[half * 8 + g], window, preferred_element_type=F32)
            total = jnp.where(lane_group == g, one, total)
        halves.append(total)
    for h in range(2):
        rows = slice(h * LH, (h + 1) * LH)
        filtered = jnp.concatenate([halves[0][:, rows], halves[1][:, rows]], axis=1)
        value = queries[h] * (filtered + bias_ref[...] * mixes[h].astype(F32))
        out_ref[h] = value.astype(BF16)


def mix(proj, halo, band, taps, bias, first, count):
    return pl.pallas_call(
        mix_kernel,
        grid=(count,),
        in_specs=[
            pl.BlockSpec((3, 2, LH, CH), lambda b: (0, 0, b + first, 0)),
            pl.BlockSpec((2, HALO, CH), lambda b: (0, 0, 0)),
            pl.BlockSpec((GROUPS, LH, 2 * LH), lambda b: (0, 0, 0)),
            pl.BlockSpec((3, 3, CH), lambda b: (0, 0, 0)),
            pl.BlockSpec((1, CH), lambda b: (0, 0)),
        ],
        out_specs=pl.BlockSpec((2, LH, CH), lambda b: (0, b, 0)),
        out_shape=jax.ShapeDtypeStruct((2, count * LH, CH), BF16),
        scratch_shapes=[
            pltpu.VMEM((2, LH, CH), BF16),
            pltpu.VMEM((2, 3, 8, CH), F32),
        ],
        compiler_params=pltpu.CompilerParams(vmem_limit_bytes=16 * MIB),
        cost_estimate=pl.CostEstimate(
            flops=2 * 512 * CH * 2048, bytes_accessed=2_000_000, transcendentals=0
        ),
        name="mix",
    )(proj, halo, band, taps, bias)


def out_kernel(at_ref, mine_ref, other_ref, here_ref, there_ref, *refs):
    out_ref, wide, sems = refs[-3:]
    copies = []
    for i in range(4):
        for j in range(4):
            source = (here_ref, there_ref)[i // 2].at[i % 2, j]
            lanes = pl.ds(pl.multiple_of(at_ref[4 + j] * 128, 128), 128)
            place = wide.at[at_ref[i], :, lanes]
            copies.append(pltpu.make_async_copy(source, place, sems.at[i, j]))

    @pl.when(pl.program_id(0) == 0)
    def _():
        for copy in copies:
            copy.start()
        for copy in copies:
            copy.wait()

    swap = at_ref[9] == 1
    first = jnp.where(swap, other_ref[0], mine_ref[0])
    second = jnp.where(swap, mine_ref[0], other_ref[0])
    rows = jnp.concatenate([first, second], axis=1)
    for y in range(4):
        out_ref[0, y] = jnp.dot(rows, wide[y], preferred_element_type=F32).astype(BF16)


def project_out(at, mine, other, parts, half, base=None):
    more = () if base is None else (base,)
    return pl.pallas_call(
        out_kernel,
        grid_spec=pltpu.PrefetchScalarGridSpec(
            num_scalar_prefetch=1,
            grid=(2,),
            in_specs=[
                pl.BlockSpec((1, HALF, CH), lambda h, at: (h, 0, 0)),
                pl.BlockSpec((1, HALF, CH), lambda h, at: (h, 0, 0)),
                *[pl.BlockSpec(memory_space=pl.ANY)] * (2 + len(more)),
            ],
            out_specs=pl.BlockSpec((1, 4, HALF, WIDE), lambda h, at: (h, 0, half, 0)),
            scratch_shapes=[
                pltpu.VMEM((4, 2 * CH, WIDE), BF16),
                pltpu.SemaphoreType.DMA((4, 4)),
            ],
        ),
        out_shape=jax.ShapeDtypeStruct((2, 4, ROWS, WIDE), BF16),
        input_output_aliases={} if base is None else {5: 0},
        compiler_params=pltpu.CompilerParams(vmem_limit_bytes=52 * MIB),
        cost_estimate=pl.CostEstimate(
            flops=2 * 512 * 2 * CH * 2048, bytes_accessed=5_000_000, transcendentals=0
        ),
        name="project_out",
    )(at, mine, other, *parts, *more)


FIRST, SECOND = (1, 3), (3, 1)


def pair_step(value, axis, masks):
    pairs = [(i * 2 + c, (i ^ masks[c]) * 2 + c) for i in range(4) for c in range(2)]
    return lax.ppermute(value, (axis, "c"), pairs)


def ring_pairs(piece, axis):
    here = jnp.stack([piece, pair_step(piece, axis, FIRST)])
    return here, pair_step(here, axis, SECOND)


def ring_line(piece, axis):
    return jnp.concatenate(ring_pairs(piece, axis), axis=0)


def on_device(
    tokens, prior_rows, norm_gain, in_weight, short_filter, mr_filter, mr_bias, out_weight
):
    zh = lax.axis_index("zh")
    column = lax.axis_index("x")
    leading = (column == 0) & (lax.axis_index("y") == 0)

    core = lax.axis_index("c")
    turns = jnp.where(core == 0, jnp.array([0, 1, 3, 2]), jnp.array([0, 3, 1, 2]))
    at = jnp.concatenate(
        [lax.axis_index("y") ^ turns, column ^ turns, jnp.stack([zh, zh ^ core])]
    ).astype(jnp.int32)
    ring = ("zh", "zl", "c")
    padded = jnp.pad(prior_rows, ((0, SHARE + TILE - 1 - prior_rows.shape[0]), (0, 0)))
    some = lax.dynamic_slice_in_dim(padded, zh * SHARE, TILE - 1, 0)
    own = jnp.concatenate([tokens, some, norm_gain[None, :]], axis=0)
    gathered = lax.all_gather(own, ring).reshape(2, 8, ROWS + TILE, WIDE)

    left, right = in_weight[..., :CH], in_weight[..., CH:]
    kept = jnp.where(zh == 0, left, right)
    got = lax.ppermute(jnp.where(zh == 0, right, left), "zh", [(0, 1), (1, 0)])
    kept_line, got_line = ring_line(kept, "x"), ring_line(got, "y")

    out_weight, _, _ = lax.optimization_barrier((out_weight, kept_line, got_line))
    pieces = []
    for k in range(2):
        chosen = lax.dynamic_slice_in_dim(out_weight, (core ^ k) * CH, CH, 0)
        pairs = [(a * 2 + b, (b ^ k) * 2 + a) for a in range(2) for b in range(2)]
        pieces.append(lax.ppermute(chosen, ("zh", "c"), pairs))
    kept_here = jnp.stack([kept_line, pair_step(kept_line, "y", FIRST)])
    got_here = jnp.stack([got_line, pair_step(got_line, "x", FIRST)])
    out_piece = jnp.concatenate(pieces, axis=0)
    out_piece, _, _ = lax.optimization_barrier((out_piece, kept_here, got_here))
    out_line = ring_line(out_piece, "x")
    weights = (
        kept_here,
        pair_step(kept_here, "y", SECOND),
        got_here,
        pair_step(got_here, "x", SECOND),
    )
    out_line, weights, gathered = lax.optimization_barrier((out_line, weights, gathered))
    out_here = jnp.stack([out_line, pair_step(out_line, "y", FIRST)])

    taps = lax.dynamic_slice_in_dim(short_filter, zh * CH, CH, 2)
    bias = lax.dynamic_slice_in_dim(mr_bias, zh * CH, CH, 0)[None, :]
    band = toeplitz(lax.dynamic_slice_in_dim(mr_filter, zh * GROUPS, GROUPS, 0))

    proj, tail, mid, front = project(at, gathered, weights, taps)
    out_here, tail = lax.optimization_barrier((out_here, tail))
    out_parts = (out_here, pair_step(out_here, "y", SECOND))

    last = column == 3
    to_first = jnp.where(last, tail[1], tail[0])
    to_second = jnp.where(last, tail[0], tail[1])
    first = lax.ppermute(to_first, ("y", "x"), [(i, i + 1) for i in range(15)])
    second = lax.ppermute(
        to_second, ("y", "x"), [(i, i // 4 * 4 + (i + 1) % 4) for i in range(16)]
    )
    halo = jnp.stack([jnp.where(leading, front, first), second])

    def swapped(mine):
        return mine, lax.ppermute(mine, "c", [(0, 1), (1, 0)])

    partial = project_out(at, *swapped(mix(proj, mid, band, taps, bias, 2, 2)), out_parts, 1)
    partial = project_out(
        at, *swapped(mix(proj, halo, band, taps, bias, 0, 2)), out_parts, 0, partial
    )
    summed = lax.psum_scatter(
        partial.reshape(8, ROWS, WIDE), ("zh", "zl"), scatter_dimension=0
    )
    return (tokens.astype(F32) + summed.astype(F32)).astype(BF16)


def solution(mesh):
    split = Mesh(mesh.devices.reshape(4, 2, 4, 4, 2), ("y", "zh", "x", "zl", "c"))
    seq, tensor = ("y", "zh", "x"), ("zl", "c")
    in_specs = (
        P(seq, tensor),
        P(None, tensor),
        P(tensor),
        P(None, seq, tensor),
        P(None, None, tensor),
        P(tensor, None),
        P(tensor),
        P(tensor, seq),
    )
    return jax.shard_map(
        on_device, mesh=split, in_specs=in_specs, out_specs=P(seq, tensor), check_vma=False
    )
```

```python
import jax
import jax.numpy as jnp
from jax import lax
from jax.experimental import pallas as pl
from jax.experimental.pallas import tpu as pltpu
from jax.sharding import Mesh, PartitionSpec as P

GSIZE = 16
LH = 128
ROWS = 512
TILE = 80
SHARE = 72
HALF = ROWS // 2
WIDE = 512
CH = 256
GROUPS = CH // GSIZE
HALO = LH + 16
MIB = 1024 * 1024
F32 = jnp.float32
BF16 = jnp.bfloat16


def row_iota(shape):
    return lax.broadcasted_iota(jnp.int32, shape, 0)


def three_taps(rows, taps, s):
    return (
        taps[0, s : s + 1] * rows
        + taps[1, s : s + 1] * pltpu.roll(rows, 1, 0)
        + taps[2, s : s + 1] * pltpu.roll(rows, 2, 0)
    )


def last_rows(parts, first, shift):
    place = row_iota((16, CH)) // 2
    out = jnp.zeros((16, CH), F32)
    for s in range(3):
        moved = pltpu.roll(parts[s][first : first + 16], (2 * s + shift) % 16, 0)
        out = jnp.where(place == s, moved, out)
    return out.astype(BF16)


def add_products(kind, at_ref, x_ref, here_ref, there_ref, acc, stat, wide, sems):
    step = pl.program_id(0)
    turns = []
    for y in range(4):
        copies = []
        for x in range(4):
            i, j = (y, x) if kind == 0 else (x, y)
            source = (here_ref, there_ref)[i // 2].at[i % 2, j]
            place = wide.at[y, :, at_ref[4 + x]]
            copies.append(pltpu.make_async_copy(source, place, sems.at[y, x]))
        turns.append(copies)

    @pl.when(step == 0)
    def _():
        for copies in turns:
            for copy in copies:
                copy.start()

    for k in range(4):

        @pl.when(step == k)
        def _(k=k):
            for copy in turns[k]:
                copy.wait()

    for h in range(2):
        rows = x_ref[h, 0]
        stat[h] += rows[ROWS + TILE - 16 :].astype(F32)[8:]
        for s in range(3):
            weights = wide[step, s].reshape(WIDE, CH)
            acc[h, s] += jnp.dot(rows, weights, preferred_element_type=F32)


def first_kernel(at_ref, x_ref, here_ref, there_ref, acc, stat, wide, sems):
    @pl.when(pl.program_id(0) == 0)
    def _():
        acc[...] = jnp.zeros_like(acc)
        stat[...] = jnp.zeros_like(stat)

    add_products(0, at_ref, x_ref, here_ref, there_ref, acc, stat, wide, sems)


def as_column(row):
    column = jnp.broadcast_to(row, (128, row.shape[1])).T
    return jnp.concatenate([column] * (CH // 128), axis=1)


def second_kernel(at_ref, x_ref, here_ref, there_ref, part_ref, sums_ref, taps_ref, *refs):
    proj_ref, tail_ref, mid_ref, front_ref, acc, stat, wide, ahead, sems = refs

    @pl.when(pl.program_id(0) == 0)
    def _():
        acc[...] = part_ref[...]
        stat[...] = sums_ref[...]

    add_products(1, at_ref, x_ref, here_ref, there_ref, acc, stat, wide, sems)

    @pl.when(pl.program_id(0) == pl.num_programs(0) - 1)
    def _():
        for h in range(2):
            sums = stat[h]
            own = lax.rsqrt((sums[0:1] + sums[1:2]) * (1.0 / 4096.0) + 1e-6)
            extra = lax.rsqrt((sums[2:3] + sums[3:4]) * (1.0 / 4096.0) + 1e-6)
            own, extra = as_column(own), as_column(extra[:, :128])[:TILE]
            for s in range(3):
                proj_ref[s, h] = (acc[h, s, :ROWS] * own).astype(BF16)
                carried = (acc[h, s, ROWS:] * extra).astype(BF16).astype(F32)
                if h == 0:
                    ahead[s, :SHARE] = carried[:SHARE]
                else:
                    ahead[s, SHARE:] = carried
            for end, ref in ((ROWS, tail_ref), (HALF, mid_ref)):
                rows = [proj_ref[s, h, end - HALO : end].astype(F32) for s in range(3)]
                mixing = three_taps(rows[1], taps_ref, 1) * three_taps(rows[2], taps_ref, 2)
                ref[h, :LH] = mixing[HALO - LH :].astype(BF16)
                ref[h, LH:] = last_rows(rows, HALO - 16, 2)
        mixing = three_taps(ahead[1], taps_ref, 1) * three_taps(ahead[2], taps_ref, 2)
        front_ref[:LH] = pltpu.roll(mixing, SHARE + TILE - 1, 0)[:LH].astype(BF16)
        front_ref[LH:] = last_rows(ahead, LH - 8, -7)


def project(at, gathered, kept, got, taps):
    count = ROWS + TILE
    acc = (2, 3, count, CH)
    stat = (2, 8, WIDE)
    wide = pltpu.VMEM((4, 3, 4, 128, CH), BF16)
    sems = pltpu.SemaphoreType.DMA((4, 4))

    def whole(shape):
        return pl.BlockSpec(shape, lambda k, at: (0,) * len(shape))

    def inputs(kind):
        def features(k, at):
            return 0, 2 * at[k] + (at[8] if kind == 0 else 1 - at[8]), 0, 0

        return [
            pl.BlockSpec((2, 1, count, WIDE), features),
            *[pl.BlockSpec(memory_space=pl.ANY)] * 2,
        ]

    options = dict(
        compiler_params=pltpu.CompilerParams(vmem_limit_bytes=40 * MIB),
        cost_estimate=pl.CostEstimate(
            flops=2 * count * 4096 * 3 * CH, bytes_accessed=12_000_000, transcendentals=0
        ),
    )
    part, sums = pl.pallas_call(
        first_kernel,
        grid_spec=pltpu.PrefetchScalarGridSpec(
            num_scalar_prefetch=1,
            grid=(4,),
            in_specs=inputs(0),
            out_specs=[whole(acc), whole(stat)],
            scratch_shapes=[wide, sems],
        ),
        out_shape=[jax.ShapeDtypeStruct(acc, F32), jax.ShapeDtypeStruct(stat, F32)],
        name="project_first",
        **options,
    )(at, gathered, *kept)
    shapes = [(3, 2, ROWS, CH), (2, HALO, CH), (2, HALO, CH), (HALO, CH)]
    return pl.pallas_call(
        second_kernel,
        grid_spec=pltpu.PrefetchScalarGridSpec(
            num_scalar_prefetch=1,
            grid=(4,),
            in_specs=[*inputs(1), whole(acc), whole(stat), whole((3, 3, CH))],
            out_specs=[whole(shape) for shape in shapes],
            scratch_shapes=[
                pltpu.VMEM(acc, F32),
                pltpu.VMEM(stat, F32),
                wide,
                pltpu.VMEM((3, SHARE + TILE, CH), F32),
                sems,
            ],
        ),
        out_shape=[jax.ShapeDtypeStruct(shape, BF16) for shape in shapes],
        name="project_second",
        **options,
    )(at, gathered, *got, part, sums, taps)


def toeplitz_kernel(u_ref, out_ref):
    for g in range(GROUPS):
        wide = jnp.broadcast_to(u_ref[g : g + 1], (LH, 3 * LH))
        skewed = pltpu.roll(wide, 0, 1, stride=1, stride_axis=0)
        out_ref[g] = skewed[:, : 2 * LH].astype(BF16)


def toeplitz(filters):
    backwards = jnp.flip(filters.astype(F32), 1)
    row = jnp.pad(backwards, ((0, 0), (1, 2 * LH - 1)))
    return pl.pallas_call(
        toeplitz_kernel,
        out_shape=jax.ShapeDtypeStruct((GROUPS, LH, 2 * LH), BF16),
        compiler_params=pltpu.CompilerParams(vmem_limit_bytes=8 * MIB),
        name="toeplitz",
    )(row)


def mix_kernel(proj_ref, halo_ref, band_ref, taps_ref, bias_ref, out_ref, before, edge):
    step = pl.program_id(0)

    @pl.when(step == 0)
    def _():
        for h in range(2):
            before[h] = halo_ref[h, :LH]
            last = halo_ref[h, LH:].astype(F32)
            for s in range(3):
                edge[h, s] = pltpu.roll(last, (6 - 2 * s) % 16, 0)[:8]

    queries = []
    mixes = []
    windows = []
    for h in range(2):
        feats = []
        for s in range(3):
            lifted = proj_ref[s, h].astype(F32)
            rows = jnp.concatenate([edge[h, s], lifted], axis=0)
            feats.append(three_taps(rows, taps_ref, s)[8:])
            edge[h, s] = lifted[LH - 8 :]
        mixing = (feats[1] * feats[2]).astype(BF16)
        queries.append(feats[0])
        mixes.append(mixing)
        windows.append(jnp.concatenate([before[h], mixing], axis=0))
        before[h] = mixing
    lane_group = lax.broadcasted_iota(jnp.int32, (LH, 2 * LH), 1) % LH // GSIZE
    halves = []
    for half in range(2):
        lanes = slice(half * LH, (half + 1) * LH)
        window = jnp.concatenate([windows[0][:, lanes], windows[1][:, lanes]], axis=1)
        total = jnp.zeros((LH, 2 * LH), F32)
        for g in range(GROUPS // 2):
            one = jnp.dot(band_ref[half * 8 + g], window, preferred_element_type=F32)
            total = jnp.where(lane_group == g, one, total)
        halves.append(total)
    for h in range(2):
        rows = slice(h * LH, (h + 1) * LH)
        filtered = jnp.concatenate([halves[0][:, rows], halves[1][:, rows]], axis=1)
        value = queries[h] * (filtered + bias_ref[...] * mixes[h].astype(F32))
        out_ref[h] = value.astype(BF16)


def mix(proj, halo, band, taps, bias, first, count):
    return pl.pallas_call(
        mix_kernel,
        grid=(count,),
        in_specs=[
            pl.BlockSpec((3, 2, LH, CH), lambda b: (0, 0, b + first, 0)),
            pl.BlockSpec((2, HALO, CH), lambda b: (0, 0, 0)),
            pl.BlockSpec((GROUPS, LH, 2 * LH), lambda b: (0, 0, 0)),
            pl.BlockSpec((3, 3, CH), lambda b: (0, 0, 0)),
            pl.BlockSpec((1, CH), lambda b: (0, 0)),
        ],
        out_specs=pl.BlockSpec((2, LH, CH), lambda b: (0, b, 0)),
        out_shape=jax.ShapeDtypeStruct((2, count * LH, CH), BF16),
        scratch_shapes=[
            pltpu.VMEM((2, LH, CH), BF16),
            pltpu.VMEM((2, 3, 8, CH), F32),
        ],
        compiler_params=pltpu.CompilerParams(vmem_limit_bytes=16 * MIB),
        cost_estimate=pl.CostEstimate(
            flops=2 * 512 * CH * 2048, bytes_accessed=2_000_000, transcendentals=0
        ),
        name="mix",
    )(proj, halo, band, taps, bias)


def out_kernel(at_ref, mine_ref, other_ref, here_ref, there_ref, *refs):
    out_ref, wide, rows, sems = refs[-4:]
    step = pl.program_id(0)
    turns = []
    for i in range(4):
        copies = []
        for j in range(4):
            lanes = pl.ds(pl.multiple_of(at_ref[4 + j] * 128, 128), 128)
            for part in range(4):
                source = (here_ref, there_ref)[i // 2].at[
                    i % 2, j, part // 2, :, pl.ds(part % 2 * 128, 128)
                ]
                place = wide.at[i, pl.ds(part * 128, 128), lanes]
                copies.append(pltpu.make_async_copy(source, place, sems.at[i, j, part]))
        turns.append(copies)

    @pl.when(step == 0)
    def _():
        for copies in turns:
            for copy in copies:
                copy.start()
        swap = at_ref[9] == 1
        for h in range(2):
            place = slice(h * HALF, (h + 1) * HALF)
            rows[place, :CH] = jnp.where(swap, other_ref[h], mine_ref[h])
            rows[place, CH:] = jnp.where(swap, mine_ref[h], other_ref[h])

    for k in range(4):

        @pl.when(step == k)
        def _(k=k):
            for copy in turns[k]:
                copy.wait()

    products = jnp.dot(rows[...], wide[step], preferred_element_type=F32).astype(BF16)
    for h in range(2):
        out_ref[h, 0] = products[h * HALF : (h + 1) * HALF]


def project_out(at, mine, other, parts, half, base=None):
    more = () if base is None else (base,)
    return pl.pallas_call(
        out_kernel,
        grid_spec=pltpu.PrefetchScalarGridSpec(
            num_scalar_prefetch=1,
            grid=(4,),
            in_specs=[
                *[pl.BlockSpec((2, HALF, CH), lambda k, at: (0, 0, 0))] * 2,
                *[pl.BlockSpec(memory_space=pl.ANY)] * (2 + len(more)),
            ],
            out_specs=pl.BlockSpec((2, 1, HALF, WIDE), lambda k, at: (0, at[k], half, 0)),
            scratch_shapes=[
                pltpu.VMEM((4, 2 * CH, WIDE), BF16),
                pltpu.VMEM((2 * HALF, 2 * CH), BF16),
                pltpu.SemaphoreType.DMA((4, 4, 4)),
            ],
        ),
        out_shape=jax.ShapeDtypeStruct((2, 4, ROWS, WIDE), BF16),
        input_output_aliases={} if base is None else {5: 0},
        compiler_params=pltpu.CompilerParams(vmem_limit_bytes=46 * MIB),
        cost_estimate=pl.CostEstimate(
            flops=2 * 512 * 2 * CH * 2048, bytes_accessed=5_000_000, transcendentals=0
        ),
        name="project_out",
    )(at, mine, other, *parts, *more)


FIRST, SECOND = (1, 3), (3, 1)


def pair_step(value, axis, masks):
    pairs = [(i * 2 + c, (i ^ masks[c]) * 2 + c) for i in range(4) for c in range(2)]
    return lax.ppermute(value, (axis, "c"), pairs)


def ring_pairs(piece, axis):
    here = jnp.stack([piece, pair_step(piece, axis, FIRST)])
    return here, pair_step(here, axis, SECOND)


def on_device(
    tokens, prior_rows, norm_gain, in_weight, short_filter, mr_filter, mr_bias, out_weight
):
    zh = lax.axis_index("zh")
    column = lax.axis_index("x")
    leading = (column == 0) & (lax.axis_index("y") == 0)

    core = lax.axis_index("c")
    turns = jnp.where(core == 0, jnp.array([0, 1, 3, 2]), jnp.array([0, 3, 1, 2]))
    at = jnp.concatenate(
        [lax.axis_index("y") ^ turns, column ^ turns, jnp.stack([zh, zh ^ core])]
    ).astype(jnp.int32)
    ring = ("zh", "zl", "c")
    padded = jnp.pad(prior_rows, ((0, 2 * SHARE - prior_rows.shape[0]), (0, 0)))
    some = lax.dynamic_slice_in_dim(padded, zh * SHARE, SHARE, 0)
    lifted, carried = tokens.astype(F32), some.astype(F32)
    gain = norm_gain.astype(F32)
    sums = jnp.sum(lifted * lifted, axis=1)
    more = jnp.pad(jnp.sum(carried * carried, axis=1), (0, WIDE - SHARE))
    sums = jnp.stack([sums, more])
    coarse = lax.reduce_precision(sums, 8, 7)
    terms = jnp.stack([coarse, sums - coarse], axis=1).reshape(4, WIDE).astype(BF16)
    own = jnp.concatenate(
        [
            (lifted * gain).astype(BF16),
            (carried * gain).astype(BF16),
            jnp.pad(terms, ((0, TILE - SHARE - 4), (0, 0))),
        ],
        axis=0,
    )
    gathered = lax.all_gather(own, ring).reshape(2, 8, ROWS + TILE, WIDE)

    left, right = in_weight[..., :CH], in_weight[..., CH:]
    kept = jnp.where(zh == 0, left, right)
    got = lax.ppermute(jnp.where(zh == 0, right, left), "zh", [(0, 1), (1, 0)])
    pieces = []
    for k in range(2):
        chosen = lax.dynamic_slice_in_dim(out_weight, (core ^ k) * CH, CH, 0)
        pairs = [(a * 2 + b, (b ^ k) * 2 + a) for a in range(2) for b in range(2)]
        pieces.append(lax.ppermute(chosen, ("zh", "c"), pairs))
    got, pieces = lax.optimization_barrier((got, pieces))
    pieces = [jnp.concatenate([p[:128], p[128:]], axis=1)[None] for p in pieces]
    kept = jnp.concatenate([kept, *pieces], axis=0)
    kept = jnp.stack([kept, pair_step(kept, "x", FIRST)])
    got = jnp.stack([got, pair_step(got, "y", FIRST)])
    kept, got = lax.optimization_barrier((kept, got))
    line = jnp.concatenate([kept, pair_step(kept, "x", SECOND)], axis=0)
    got = jnp.concatenate([got, pair_step(got, "y", SECOND)], axis=0)
    kept = ring_pairs(line[:, :3], "y")
    got = ring_pairs(got, "x")
    out_line, _ = lax.optimization_barrier((line[:, 3:], kept[1]))
    out_here = jnp.stack([out_line, pair_step(out_line, "y", FIRST)])
    out_here, _ = lax.optimization_barrier((out_here, got[1]))
    out_parts = (out_here, pair_step(out_here, "y", SECOND))

    taps = lax.dynamic_slice_in_dim(short_filter, zh * CH, CH, 2)
    bias = lax.dynamic_slice_in_dim(mr_bias, zh * CH, CH, 0)[None, :]
    band = toeplitz(lax.dynamic_slice_in_dim(mr_filter, zh * GROUPS, GROUPS, 0))

    proj, tail, mid, front = project(at, gathered, kept, got, taps)

    last = column == 3
    to_first = jnp.where(last, tail[1], tail[0])
    to_second = jnp.where(last, tail[0], tail[1])
    first = lax.ppermute(to_first, ("y", "x"), [(i, i + 1) for i in range(15)])
    second = lax.ppermute(
        to_second, ("y", "x"), [(i, i // 4 * 4 + (i + 1) % 4) for i in range(16)]
    )
    halo = jnp.stack([jnp.where(leading, front, first), second])

    def swapped(mine):
        return mine, lax.ppermute(mine, "c", [(0, 1), (1, 0)])

    partial = project_out(at, *swapped(mix(proj, mid, band, taps, bias, 2, 2)), out_parts, 1)
    partial = project_out(
        at, *swapped(mix(proj, halo, band, taps, bias, 0, 2)), out_parts, 0, partial
    )
    summed = lax.psum_scatter(
        partial.reshape(8, ROWS, WIDE), ("zh", "zl"), scatter_dimension=0
    )
    return (tokens.astype(F32) + summed.astype(F32)).astype(BF16)


def solution(mesh):
    split = Mesh(mesh.devices.reshape(4, 2, 4, 4, 2), ("y", "zh", "x", "zl", "c"))
    seq, tensor = ("y", "zh", "x"), ("zl", "c")
    in_specs = (
        P(seq, tensor),
        P(None, tensor),
        P(tensor),
        P(None, seq, tensor),
        P(None, None, tensor),
        P(tensor, None),
        P(tensor),
        P(tensor, seq),
    )
    return jax.shard_map(
        on_device, mesh=split, in_specs=in_specs, out_specs=P(seq, tensor), check_vma=False
    )
```

```python
import jax
import jax.numpy as jnp
from jax import lax
from jax.experimental import pallas as pl
from jax.experimental.pallas import tpu as pltpu
from jax.sharding import Mesh, PartitionSpec as P

GSIZE = 16
LH = 128
ROWS = 512
TILE = 80
SHARE = 72
HALF = ROWS // 2
WIDE = 512
CH = 256
GROUPS = CH // GSIZE
HALO = LH + 16
MIB = 1024 * 1024
F32 = jnp.float32
BF16 = jnp.bfloat16


def row_iota(shape):
    return lax.broadcasted_iota(jnp.int32, shape, 0)


def three_taps(rows, taps, s):
    return (
        taps[0, s : s + 1] * rows
        + taps[1, s : s + 1] * pltpu.roll(rows, 1, 0)
        + taps[2, s : s + 1] * pltpu.roll(rows, 2, 0)
    )


def last_rows(parts, first, shift):
    place = row_iota((16, CH)) // 2
    out = jnp.zeros((16, CH), F32)
    for s in range(3):
        moved = pltpu.roll(parts[s][first : first + 16], (2 * s + shift) % 16, 0)
        out = jnp.where(place == s, moved, out)
    return out.astype(BF16)


def add_products(kind, at_ref, x_ref, here_ref, there_ref, acc, stat, wide, sems):
    step = pl.program_id(0)
    turns = []
    for y in range(4):
        copies = []
        for x in range(4):
            i, j = (y, x) if kind == 0 else (x, y)
            rows = pl.ds(pl.multiple_of(at_ref[4 + x] * 128, 128), 128)
            for s in range(3):
                source = (here_ref, there_ref)[i // 2].at[i % 2, j, s]
                place = wide.at[y, rows, pl.ds(s * CH, CH)]
                copies.append(pltpu.make_async_copy(source, place, sems.at[y, x, s]))
        turns.append(copies)

    @pl.when(step == 0)
    def _():
        for copies in turns:
            for copy in copies:
                copy.start()

    for k in range(4):

        @pl.when(step == k)
        def _(k=k):
            for copy in turns[k]:
                copy.wait()

    products = jnp.dot(
        x_ref[...].reshape(2 * (ROWS + TILE), WIDE), wide[step], preferred_element_type=F32
    )
    sums = x_ref[:, 0, ROWS + TILE - 16 :].astype(F32)[:, 8:]

    @pl.when(step == 0)
    def _():
        acc[...] = products
        stat[...] = sums

    @pl.when(step > 0)
    def _():
        acc[...] += products
        stat[...] += sums


def first_kernel(at_ref, x_ref, here_ref, there_ref, acc, stat, wide, sems):
    add_products(1, at_ref, x_ref, here_ref, there_ref, acc, stat, wide, sems)


def as_column(row):
    column = jnp.broadcast_to(row, (128, row.shape[1])).T
    return jnp.concatenate([column] * (CH // 128), axis=1)


def second_kernel(at_ref, x_ref, here_ref, there_ref, part_ref, sums_ref, taps_ref, *refs):
    proj_ref, tail_ref, mid_ref, front_ref, acc, stat, wide, ahead, sems = refs

    add_products(0, at_ref, x_ref, here_ref, there_ref, acc, stat, wide, sems)

    @pl.when(pl.program_id(0) == pl.num_programs(0) - 1)
    def _():
        for h in range(2):
            sums = stat[h] + sums_ref[h]
            own = lax.rsqrt((sums[0:1] + sums[1:2]) * (1.0 / 4096.0) + 1e-6)
            extra = lax.rsqrt((sums[2:3] + sums[3:4]) * (1.0 / 4096.0) + 1e-6)
            own, extra = as_column(own), as_column(extra[:, :128])[:TILE]
            start = h * (ROWS + TILE)
            for s in range(3):
                lanes = slice(s * CH, (s + 1) * CH)
                rows = slice(start, start + ROWS)
                proj_ref[s, h] = ((acc[rows, lanes] + part_ref[rows, lanes]) * own).astype(BF16)
                rows = slice(start + ROWS, start + ROWS + TILE)
                carried = (acc[rows, lanes] + part_ref[rows, lanes]) * extra
                carried = carried.astype(BF16).astype(F32)
                if h == 0:
                    ahead[s, :SHARE] = carried[:SHARE]
                else:
                    ahead[s, SHARE:] = carried
            for end, ref in ((ROWS, tail_ref), (HALF, mid_ref)):
                rows = [proj_ref[s, h, end - HALO : end].astype(F32) for s in range(3)]
                mixing = three_taps(rows[1], taps_ref, 1) * three_taps(rows[2], taps_ref, 2)
                ref[h, :LH] = mixing[HALO - LH :].astype(BF16)
                ref[h, LH:] = last_rows(rows, HALO - 16, 2)
        mixing = three_taps(ahead[1], taps_ref, 1) * three_taps(ahead[2], taps_ref, 2)
        front_ref[:LH] = pltpu.roll(mixing, SHARE + TILE - 1, 0)[:LH].astype(BF16)
        front_ref[LH:] = last_rows(ahead, LH - 8, -7)


def project(at, gathered, kept, got, taps):
    count = ROWS + TILE
    acc = (2 * count, 3 * CH)
    stat = (2, 8, WIDE)
    wide = pltpu.VMEM((4, WIDE, 3 * CH), BF16)
    sems = pltpu.SemaphoreType.DMA((4, 4, 3))

    def whole(shape):
        return pl.BlockSpec(shape, lambda k, at: (0,) * len(shape))

    def inputs(kind):
        def features(k, at):
            return 0, 2 * at[k] + (at[8] if kind == 0 else 1 - at[8]), 0, 0

        return [
            pl.BlockSpec((2, 1, count, WIDE), features),
            *[pl.BlockSpec(memory_space=pl.ANY)] * 2,
        ]

    options = dict(
        compiler_params=pltpu.CompilerParams(vmem_limit_bytes=40 * MIB),
        cost_estimate=pl.CostEstimate(
            flops=2 * count * 4096 * 3 * CH, bytes_accessed=12_000_000, transcendentals=0
        ),
    )
    part, sums = pl.pallas_call(
        first_kernel,
        grid_spec=pltpu.PrefetchScalarGridSpec(
            num_scalar_prefetch=1,
            grid=(4,),
            in_specs=inputs(1),
            out_specs=[whole(acc), whole(stat)],
            scratch_shapes=[wide, sems],
        ),
        out_shape=[jax.ShapeDtypeStruct(acc, F32), jax.ShapeDtypeStruct(stat, F32)],
        name="project_first",
        **options,
    )(at, gathered, *got)
    shapes = [(3, 2, ROWS, CH), (2, HALO, CH), (2, HALO, CH), (HALO, CH)]
    return pl.pallas_call(
        second_kernel,
        grid_spec=pltpu.PrefetchScalarGridSpec(
            num_scalar_prefetch=1,
            grid=(4,),
            in_specs=[*inputs(0), whole(acc), whole(stat), whole((3, 3, CH))],
            out_specs=[whole(shape) for shape in shapes],
            scratch_shapes=[
                pltpu.VMEM(acc, F32),
                pltpu.VMEM(stat, F32),
                wide,
                pltpu.VMEM((3, SHARE + TILE, CH), F32),
                sems,
            ],
        ),
        out_shape=[jax.ShapeDtypeStruct(shape, BF16) for shape in shapes],
        name="project_second",
        **options,
    )(at, gathered, *kept, part, sums, taps)


def toeplitz_kernel(u_ref, out_ref):
    for g in range(GROUPS):
        wide = jnp.broadcast_to(u_ref[g : g + 1], (LH, 3 * LH))
        skewed = pltpu.roll(wide, 0, 1, stride=1, stride_axis=0)
        out_ref[g] = skewed[:, : 2 * LH].astype(BF16)


def toeplitz(filters):
    backwards = jnp.flip(filters.astype(F32), 1)
    row = jnp.pad(backwards, ((0, 0), (1, 2 * LH - 1)))
    return pl.pallas_call(
        toeplitz_kernel,
        out_shape=jax.ShapeDtypeStruct((GROUPS, LH, 2 * LH), BF16),
        compiler_params=pltpu.CompilerParams(vmem_limit_bytes=8 * MIB),
        name="toeplitz",
    )(row)


def mix_kernel(proj_ref, halo_ref, band_ref, taps_ref, bias_ref, out_ref, before, edge):
    step = pl.program_id(0)

    @pl.when(step == 0)
    def _():
        for h in range(2):
            before[h] = halo_ref[h, :LH]
            last = halo_ref[h, LH:].astype(F32)
            for s in range(3):
                edge[h, s] = pltpu.roll(last, (6 - 2 * s) % 16, 0)[:8]

    queries = []
    mixes = []
    windows = []
    for h in range(2):
        feats = []
        for s in range(3):
            lifted = proj_ref[s, h].astype(F32)
            rows = jnp.concatenate([edge[h, s], lifted], axis=0)
            feats.append(three_taps(rows, taps_ref, s)[8:])
            edge[h, s] = lifted[LH - 8 :]
        mixing = (feats[1] * feats[2]).astype(BF16)
        queries.append(feats[0])
        mixes.append(mixing)
        windows.append(jnp.concatenate([before[h], mixing], axis=0))
        before[h] = mixing
    lane_group = lax.broadcasted_iota(jnp.int32, (LH, 2 * LH), 1) % LH // GSIZE
    halves = []
    for half in range(2):
        lanes = slice(half * LH, (half + 1) * LH)
        window = jnp.concatenate([windows[0][:, lanes], windows[1][:, lanes]], axis=1)
        total = jnp.zeros((LH, 2 * LH), F32)
        for g in range(GROUPS // 2):
            one = jnp.dot(band_ref[half * 8 + g], window, preferred_element_type=F32)
            total = jnp.where(lane_group == g, one, total)
        halves.append(total)
    for h in range(2):
        rows = slice(h * LH, (h + 1) * LH)
        filtered = jnp.concatenate([halves[0][:, rows], halves[1][:, rows]], axis=1)
        value = queries[h] * (filtered + bias_ref[...] * mixes[h].astype(F32))
        out_ref[h] = value.astype(BF16)


def mix(proj, halo, band, taps, bias, first, count):
    return pl.pallas_call(
        mix_kernel,
        grid=(count,),
        in_specs=[
            pl.BlockSpec((3, 2, LH, CH), lambda b: (0, 0, b + first, 0)),
            pl.BlockSpec((2, HALO, CH), lambda b: (0, 0, 0)),
            pl.BlockSpec((GROUPS, LH, 2 * LH), lambda b: (0, 0, 0)),
            pl.BlockSpec((3, 3, CH), lambda b: (0, 0, 0)),
            pl.BlockSpec((1, CH), lambda b: (0, 0)),
        ],
        out_specs=pl.BlockSpec((2, LH, CH), lambda b: (0, b, 0)),
        out_shape=jax.ShapeDtypeStruct((2, count * LH, CH), BF16),
        scratch_shapes=[
            pltpu.VMEM((2, LH, CH), BF16),
            pltpu.VMEM((2, 3, 8, CH), F32),
        ],
        compiler_params=pltpu.CompilerParams(vmem_limit_bytes=16 * MIB),
        cost_estimate=pl.CostEstimate(
            flops=2 * 512 * CH * 2048, bytes_accessed=2_000_000, transcendentals=0
        ),
        name="mix",
    )(proj, halo, band, taps, bias)


def out_kernel(at_ref, mine_ref, other_ref, w_ref, *refs):
    out_ref, wide, rows, sems = refs[-4:]
    step = pl.program_id(0)
    turns = []
    for y in range(4):
        copies = []
        for j in range(4):
            lanes = pl.ds(pl.multiple_of(at_ref[4 + j] * 128, 128), 128)
            for part in range(4):
                source = w_ref.at[y, j, part // 2, :, pl.ds(part % 2 * 128, 128)]
                place = wide.at[y, pl.ds(part * 128, 128), lanes]
                copies.append(pltpu.make_async_copy(source, place, sems.at[y, j, part]))
        turns.append(copies)

    @pl.when(step == 0)
    def _():
        for copies in turns:
            for copy in copies:
                copy.start()
        swap = at_ref[9] == 1
        for h in range(2):
            place = slice(h * HALF, (h + 1) * HALF)
            rows[place, :CH] = jnp.where(swap, other_ref[h], mine_ref[h])
            rows[place, CH:] = jnp.where(swap, mine_ref[h], other_ref[h])

    for k in range(4):

        @pl.when(step == k)
        def _(k=k):
            for copy in turns[k]:
                copy.wait()

    products = jnp.dot(rows[...], wide[step], preferred_element_type=F32).astype(BF16)
    for h in range(2):
        out_ref[h, 0] = products[h * HALF : (h + 1) * HALF]


def project_out(at, mine, other, weights, half, base=None):
    more = () if base is None else (base,)
    return pl.pallas_call(
        out_kernel,
        grid_spec=pltpu.PrefetchScalarGridSpec(
            num_scalar_prefetch=1,
            grid=(4,),
            in_specs=[
                *[pl.BlockSpec((2, HALF, CH), lambda k, at: (0, 0, 0))] * 2,
                *[pl.BlockSpec(memory_space=pl.ANY)] * (1 + len(more)),
            ],
            out_specs=pl.BlockSpec((2, 1, HALF, WIDE), lambda k, at: (0, k, half, 0)),
            scratch_shapes=[
                pltpu.VMEM((4, 2 * CH, WIDE), BF16),
                pltpu.VMEM((2 * HALF, 2 * CH), BF16),
                pltpu.SemaphoreType.DMA((4, 4, 4)),
            ],
        ),
        out_shape=jax.ShapeDtypeStruct((2, 4, ROWS, WIDE), BF16),
        input_output_aliases={} if base is None else {4: 0},
        compiler_params=pltpu.CompilerParams(vmem_limit_bytes=52 * MIB),
        cost_estimate=pl.CostEstimate(
            flops=2 * 512 * 2 * CH * 2048, bytes_accessed=5_000_000, transcendentals=0
        ),
        name="project_out",
    )(at, mine, other, weights, *more)


FIRST, SECOND = (1, 3), (3, 1)


def pair_step(value, axis, masks):
    pairs = [(i * 2 + c, (i ^ masks[c]) * 2 + c) for i in range(4) for c in range(2)]
    return lax.ppermute(value, (axis, "c"), pairs)


def ring_pairs(piece, axis):
    here = jnp.stack([piece, pair_step(piece, axis, FIRST)])
    return here, pair_step(here, axis, SECOND)


def on_device(
    tokens, prior_rows, norm_gain, in_weight, short_filter, mr_filter, mr_bias, out_weight
):
    zh = lax.axis_index("zh")
    column = lax.axis_index("x")
    leading = (column == 0) & (lax.axis_index("y") == 0)

    core = lax.axis_index("c")
    turns = jnp.where(core == 0, jnp.array([0, 1, 3, 2]), jnp.array([0, 3, 1, 2]))
    at = jnp.concatenate(
        [lax.axis_index("y") ^ turns, column ^ turns, jnp.stack([zh, zh ^ core])]
    ).astype(jnp.int32)
    ring = ("zh", "zl", "c")
    padded = jnp.pad(prior_rows, ((0, 2 * SHARE - prior_rows.shape[0]), (0, 0)))
    some = lax.dynamic_slice_in_dim(padded, zh * SHARE, SHARE, 0)
    lifted, carried = tokens.astype(F32), some.astype(F32)
    gain = norm_gain.astype(F32)
    sums = jnp.sum(lifted * lifted, axis=1)
    more = jnp.pad(jnp.sum(carried * carried, axis=1), (0, WIDE - SHARE))
    sums = jnp.stack([sums, more])
    coarse = lax.reduce_precision(sums, 8, 7)
    terms = jnp.stack([coarse, sums - coarse], axis=1).reshape(4, WIDE).astype(BF16)
    own = jnp.concatenate(
        [
            (lifted * gain).astype(BF16),
            (carried * gain).astype(BF16),
            jnp.pad(terms, ((0, TILE - SHARE - 4), (0, 0))),
        ],
        axis=0,
    )
    gathered = lax.all_gather(own, ring).reshape(2, 8, ROWS + TILE, WIDE)

    left, right = in_weight[..., :CH], in_weight[..., CH:]
    kept = jnp.where(zh == 0, left, right)
    got = lax.ppermute(jnp.where(zh == 0, right, left), "zh", [(0, 1), (1, 0)])
    pieces = []
    for k in range(2):
        chosen = lax.dynamic_slice_in_dim(out_weight, (core ^ k) * CH, CH, 0)
        pairs = [(a * 2 + b, (b ^ k) * 2 + a) for a in range(2) for b in range(2)]
        pieces.append(lax.ppermute(chosen, ("zh", "c"), pairs))
    pieces = [jnp.concatenate([p[:128], p[128:]], axis=1)[None] for p in pieces]
    line = jnp.concatenate(ring_pairs(jnp.concatenate([kept, *pieces], axis=0), "x"), axis=0)
    kept = ring_pairs(line[:, :3], "y")
    got = ring_pairs(jnp.concatenate(ring_pairs(got, "y"), axis=0), "x")
    out_line, got = lax.optimization_barrier((line[:, 3:], got))
    w_out = lax.all_gather(out_line, "y")

    taps = lax.dynamic_slice_in_dim(short_filter, zh * CH, CH, 2)
    bias = lax.dynamic_slice_in_dim(mr_bias, zh * CH, CH, 0)[None, :]
    band = toeplitz(lax.dynamic_slice_in_dim(mr_filter, zh * GROUPS, GROUPS, 0))

    proj, tail, mid, front = project(at, gathered, kept, got, taps)

    last = column == 3
    to_first = jnp.where(last, tail[1], tail[0])
    to_second = jnp.where(last, tail[0], tail[1])
    first = lax.ppermute(to_first, ("y", "x"), [(i, i + 1) for i in range(15)])
    second = lax.ppermute(
        to_second, ("y", "x"), [(i, i // 4 * 4 + (i + 1) % 4) for i in range(16)]
    )
    def swapped(mine):
        return mine, lax.ppermute(mine, "c", [(0, 1), (1, 0)])

    partial = project_out(at, *swapped(mix(proj, mid, band, taps, bias, 2, 2)), w_out, 1)
    first, second, partial = lax.optimization_barrier((first, second, partial))
    halo = jnp.stack([jnp.where(leading, front, first), second])
    partial = project_out(
        at, *swapped(mix(proj, halo, band, taps, bias, 0, 2)), w_out, 0, partial
    )
    summed = lax.psum_scatter(
        partial.reshape(8, ROWS, WIDE), ("zh", "zl"), scatter_dimension=0
    )
    return (tokens.astype(F32) + summed.astype(F32)).astype(BF16)


def solution(mesh):
    split = Mesh(mesh.devices.reshape(4, 2, 4, 4, 2), ("y", "zh", "x", "zl", "c"))
    seq, tensor = ("y", "zh", "x"), ("zl", "c")
    in_specs = (
        P(seq, tensor),
        P(None, tensor),
        P(tensor),
        P(None, seq, tensor),
        P(None, None, tensor),
        P(tensor, None),
        P(tensor),
        P(tensor, seq),
    )
    return jax.shard_map(
        on_device, mesh=split, in_specs=in_specs, out_specs=P(seq, tensor), check_vma=False
    )
```

```python
import jax
import jax.numpy as jnp
from jax import lax
from jax.experimental import pallas as pl
from jax.experimental.pallas import tpu as pltpu
from jax.sharding import Mesh, PartitionSpec as P

GSIZE = 16
LH = 128
ROWS = 512
TILE = 80
SHARE = 72
HALF = ROWS // 2
WIDE = 512
CH = 256
GROUPS = CH // GSIZE
HALO = LH + 16
MIB = 1024 * 1024
F32 = jnp.float32
BF16 = jnp.bfloat16


def row_iota(shape):
    return lax.broadcasted_iota(jnp.int32, shape, 0)


def three_taps(rows, taps, s):
    return (
        taps[0, s : s + 1] * rows
        + taps[1, s : s + 1] * pltpu.roll(rows, 1, 0)
        + taps[2, s : s + 1] * pltpu.roll(rows, 2, 0)
    )


def last_rows(parts, first, shift):
    place = row_iota((16, CH)) // 2
    out = jnp.zeros((16, CH), F32)
    for s in range(3):
        moved = pltpu.roll(parts[s][first : first + 16], (2 * s + shift) % 16, 0)
        out = jnp.where(place == s, moved, out)
    return out.astype(BF16)


def as_column(row):
    column = jnp.broadcast_to(row, (128, row.shape[1])).T
    return jnp.concatenate([column] * (CH // 128), axis=1)


def project_kernel(at_ref, x_ref, *refs):
    taps_ref, proj_ref, tail_ref, mid_ref, front_ref, wide, ahead, sems = refs[4:]
    z_half = at_ref[8]
    copies = []
    for kind in range(2):
        half = z_half if kind == 0 else 1 - z_half
        for i in range(4):
            for j in range(4):
                y, x = (i, j) if kind == 0 else (j, i)
                start = (2 * at_ref[y] + half) * WIDE + at_ref[4 + x] * 128
                rows = pl.ds(pl.multiple_of(start, 128), 128)
                for s in range(3):
                    source = refs[2 * kind + i // 2].at[i % 2, j, s]
                    place = wide.at[rows, pl.ds(s * CH, CH)]
                    copies.append(pltpu.make_async_copy(source, place, sems.at[kind, i, j, s]))

    @pl.when(pl.program_id(0) == 0)
    def _():
        for copy in copies:
            copy.start()
        for copy in copies:
            copy.wait()

    features = jnp.concatenate([x_ref[0, t] for t in range(8)], axis=1)
    products = jnp.dot(features, wide[...], preferred_element_type=F32)
    sums = jnp.zeros((8, WIDE), F32)
    for t in range(8):
        sums += x_ref[0, t, ROWS + TILE - 16 :].astype(F32)[8:]
    own = lax.rsqrt((sums[0:1] + sums[1:2]) * (1.0 / 4096.0) + 1e-6)
    extra = lax.rsqrt((sums[2:3] + sums[3:4]) * (1.0 / 4096.0) + 1e-6)
    own, extra = as_column(own), as_column(extra[:, :128])[:TILE]
    for s in range(3):
        lanes = slice(s * CH, (s + 1) * CH)
        proj_ref[s, 0] = (products[:ROWS, lanes] * own).astype(BF16)
        carried = (products[ROWS:, lanes] * extra).astype(BF16).astype(F32)

        @pl.when(pl.program_id(0) == 0)
        def _(s=s, carried=carried):
            ahead[s, :SHARE] = carried[:SHARE]

        @pl.when(pl.program_id(0) == 1)
        def _(s=s, carried=carried):
            ahead[s, SHARE:] = carried

    for end, ref in ((ROWS, tail_ref), (HALF, mid_ref)):
        rows = [proj_ref[s, 0, end - HALO : end].astype(F32) for s in range(3)]
        mixing = three_taps(rows[1], taps_ref, 1) * three_taps(rows[2], taps_ref, 2)
        ref[0, :LH] = mixing[HALO - LH :].astype(BF16)
        ref[0, LH:] = last_rows(rows, HALO - 16, 2)

    @pl.when(pl.program_id(0) == 1)
    def _():
        mixing = three_taps(ahead[1], taps_ref, 1) * three_taps(ahead[2], taps_ref, 2)
        front_ref[:LH] = pltpu.roll(mixing, SHARE + TILE - 1, 0)[:LH].astype(BF16)
        front_ref[LH:] = last_rows(ahead, LH - 8, -7)


def project(at, gathered, weights, taps):
    return pl.pallas_call(
        project_kernel,
        grid_spec=pltpu.PrefetchScalarGridSpec(
            num_scalar_prefetch=1,
            grid=(2,),
            in_specs=[
                pl.BlockSpec((1, 8, ROWS + TILE, WIDE), lambda h, at: (h, 0, 0, 0)),
                *[pl.BlockSpec(memory_space=pl.ANY)] * 4,
                pl.BlockSpec((3, 3, CH), lambda h, at: (0, 0, 0)),
            ],
            out_specs=[
                pl.BlockSpec((3, 1, ROWS, CH), lambda h, at: (0, h, 0, 0)),
                pl.BlockSpec((1, HALO, CH), lambda h, at: (h, 0, 0)),
                pl.BlockSpec((1, HALO, CH), lambda h, at: (h, 0, 0)),
                pl.BlockSpec((HALO, CH), lambda h, at: (0, 0)),
            ],
            scratch_shapes=[
                pltpu.VMEM((8 * WIDE, 3 * CH), BF16),
                pltpu.VMEM((3, SHARE + TILE, CH), F32),
                pltpu.SemaphoreType.DMA((2, 4, 4, 3)),
            ],
        ),
        out_shape=[
            jax.ShapeDtypeStruct((3, 2, ROWS, CH), BF16),
            jax.ShapeDtypeStruct((2, HALO, CH), BF16),
            jax.ShapeDtypeStruct((2, HALO, CH), BF16),
            jax.ShapeDtypeStruct((HALO, CH), BF16),
        ],
        compiler_params=pltpu.CompilerParams(vmem_limit_bytes=46 * MIB),
        cost_estimate=pl.CostEstimate(
            flops=2 * 2 * ROWS * 4096 * 3 * CH, bytes_accessed=18_000_000, transcendentals=0
        ),
        name="project",
    )(at, gathered, *weights, taps)


def toeplitz_kernel(u_ref, out_ref):
    for g in range(GROUPS):
        wide = jnp.broadcast_to(u_ref[g : g + 1], (LH, 3 * LH))
        skewed = pltpu.roll(wide, 0, 1, stride=1, stride_axis=0)
        out_ref[g] = skewed[:, : 2 * LH].astype(BF16)


def toeplitz(filters):
    backwards = jnp.flip(filters.astype(F32), 1)
    row = jnp.pad(backwards, ((0, 0), (1, 2 * LH - 1)))
    return pl.pallas_call(
        toeplitz_kernel,
        out_shape=jax.ShapeDtypeStruct((GROUPS, LH, 2 * LH), BF16),
        compiler_params=pltpu.CompilerParams(vmem_limit_bytes=8 * MIB),
        name="toeplitz",
    )(row)


def mix_kernel(proj_ref, halo_ref, band_ref, taps_ref, bias_ref, out_ref, before, edge):
    step = pl.program_id(0)

    @pl.when(step == 0)
    def _():
        for h in range(2):
            before[h] = halo_ref[h, :LH]
            last = halo_ref[h, LH:].astype(F32)
            for s in range(3):
                edge[h, s] = pltpu.roll(last, (6 - 2 * s) % 16, 0)[:8]

    queries = []
    mixes = []
    windows = []
    for h in range(2):
        feats = []
        for s in range(3):
            lifted = proj_ref[s, h].astype(F32)
            rows = jnp.concatenate([edge[h, s], lifted], axis=0)
            feats.append(three_taps(rows, taps_ref, s)[8:])
            edge[h, s] = lifted[LH - 8 :]
        mixing = (feats[1] * feats[2]).astype(BF16)
        queries.append(feats[0])
        mixes.append(mixing)
        windows.append(jnp.concatenate([before[h], mixing], axis=0))
        before[h] = mixing
    lane_group = lax.broadcasted_iota(jnp.int32, (LH, 2 * LH), 1) % LH // GSIZE
    halves = []
    for half in range(2):
        lanes = slice(half * LH, (half + 1) * LH)
        window = jnp.concatenate([windows[0][:, lanes], windows[1][:, lanes]], axis=1)
        total = jnp.zeros((LH, 2 * LH), F32)
        for g in range(GROUPS // 2):
            one = jnp.dot(band_ref[half * 8 + g], window, preferred_element_type=F32)
            total = jnp.where(lane_group == g, one, total)
        halves.append(total)
    for h in range(2):
        rows = slice(h * LH, (h + 1) * LH)
        filtered = jnp.concatenate([halves[0][:, rows], halves[1][:, rows]], axis=1)
        value = queries[h] * (filtered + bias_ref[...] * mixes[h].astype(F32))
        out_ref[h] = value.astype(BF16)


def mix(proj, halo, band, taps, bias, first, count):
    return pl.pallas_call(
        mix_kernel,
        grid=(count,),
        in_specs=[
            pl.BlockSpec((3, 2, LH, CH), lambda b: (0, 0, b + first, 0)),
            pl.BlockSpec((2, HALO, CH), lambda b: (0, 0, 0)),
            pl.BlockSpec((GROUPS, LH, 2 * LH), lambda b: (0, 0, 0)),
            pl.BlockSpec((3, 3, CH), lambda b: (0, 0, 0)),
            pl.BlockSpec((1, CH), lambda b: (0, 0)),
        ],
        out_specs=pl.BlockSpec((2, LH, CH), lambda b: (0, b, 0)),
        out_shape=jax.ShapeDtypeStruct((2, count * LH, CH), BF16),
        scratch_shapes=[
            pltpu.VMEM((2, LH, CH), BF16),
            pltpu.VMEM((2, 3, 8, CH), F32),
        ],
        compiler_params=pltpu.CompilerParams(vmem_limit_bytes=16 * MIB),
        cost_estimate=pl.CostEstimate(
            flops=2 * 512 * CH * 2048, bytes_accessed=2_000_000, transcendentals=0
        ),
        name="mix",
    )(proj, halo, band, taps, bias)


def out_kernel(at_ref, mine_ref, other_ref, w_ref, *refs):
    out_ref, wide, rows, sems = refs[-4:]
    step = pl.program_id(0)
    turns = []
    for y in range(4):
        copies = []
        for x in range(4):
            place = wide.at[y, :, pl.ds(x * 128, 128)]
            copies.append(pltpu.make_async_copy(w_ref.at[y, x], place, sems.at[y, x]))
        turns.append(copies)

    @pl.when(step == 0)
    def _():
        for copies in turns:
            for copy in copies:
                copy.start()
        swap = at_ref[9] == 1
        for h in range(2):
            place = slice(h * HALF, (h + 1) * HALF)
            rows[place, :CH] = jnp.where(swap, other_ref[h], mine_ref[h])
            rows[place, CH:] = jnp.where(swap, mine_ref[h], other_ref[h])

    for k in range(4):

        @pl.when(step == k)
        def _(k=k):
            for copy in turns[k]:
                copy.wait()

    products = jnp.dot(rows[...], wide[step], preferred_element_type=F32).astype(BF16)
    for h in range(2):
        out_ref[h, 0] = products[h * HALF : (h + 1) * HALF]


def project_out(at, mine, other, weights, half, base=None):
    more = () if base is None else (base,)
    return pl.pallas_call(
        out_kernel,
        grid_spec=pltpu.PrefetchScalarGridSpec(
            num_scalar_prefetch=1,
            grid=(4,),
            in_specs=[
                *[pl.BlockSpec((2, HALF, CH), lambda k, at: (0, 0, 0))] * 2,
                *[pl.BlockSpec(memory_space=pl.ANY)] * (1 + len(more)),
            ],
            out_specs=pl.BlockSpec((2, 1, HALF, WIDE), lambda k, at: (0, k, half, 0)),
            scratch_shapes=[
                pltpu.VMEM((4, 2 * CH, WIDE), BF16),
                pltpu.VMEM((2 * HALF, 2 * CH), BF16),
                pltpu.SemaphoreType.DMA((4, 4)),
            ],
        ),
        out_shape=jax.ShapeDtypeStruct((2, 4, ROWS, WIDE), BF16),
        input_output_aliases={} if base is None else {4: 0},
        compiler_params=pltpu.CompilerParams(vmem_limit_bytes=52 * MIB),
        cost_estimate=pl.CostEstimate(
            flops=2 * 512 * 2 * CH * 2048, bytes_accessed=5_000_000, transcendentals=0
        ),
        name="project_out",
    )(at, mine, other, weights, *more)


FIRST, SECOND = (1, 3), (3, 1)


def pair_step(value, axis, masks):
    pairs = [(i * 2 + c, (i ^ masks[c]) * 2 + c) for i in range(4) for c in range(2)]
    return lax.ppermute(value, (axis, "c"), pairs)


def ring_pairs(piece, axis):
    here = jnp.stack([piece, pair_step(piece, axis, FIRST)])
    return here, pair_step(here, axis, SECOND)


def on_device(
    tokens, prior_rows, norm_gain, in_weight, short_filter, mr_filter, mr_bias, out_weight
):
    zh = lax.axis_index("zh")
    column = lax.axis_index("x")
    leading = (column == 0) & (lax.axis_index("y") == 0)

    core = lax.axis_index("c")
    turns = jnp.where(core == 0, jnp.array([0, 1, 3, 2]), jnp.array([0, 3, 1, 2]))
    at = jnp.concatenate(
        [lax.axis_index("y") ^ turns, column ^ turns, jnp.stack([zh, zh ^ core])]
    ).astype(jnp.int32)
    ring = ("zh", "zl", "c")
    padded = jnp.pad(prior_rows, ((0, 2 * SHARE - prior_rows.shape[0]), (0, 0)))
    some = lax.dynamic_slice_in_dim(padded, zh * SHARE, SHARE, 0)
    lifted, carried = tokens.astype(F32), some.astype(F32)
    gain = norm_gain.astype(F32)
    sums = jnp.sum(lifted * lifted, axis=1)
    more = jnp.pad(jnp.sum(carried * carried, axis=1), (0, WIDE - SHARE))
    sums = jnp.stack([sums, more])
    coarse = lax.reduce_precision(sums, 8, 7)
    terms = jnp.stack([coarse, sums - coarse], axis=1).reshape(4, WIDE).astype(BF16)
    own = jnp.concatenate(
        [
            (lifted * gain).astype(BF16),
            (carried * gain).astype(BF16),
            jnp.pad(terms, ((0, TILE - SHARE - 4), (0, 0))),
        ],
        axis=0,
    )
    gathered = lax.all_gather(own, ring).reshape(2, 8, ROWS + TILE, WIDE)

    left, right = in_weight[..., :CH], in_weight[..., CH:]
    kept = jnp.where(zh == 0, left, right)
    got = lax.ppermute(jnp.where(zh == 0, right, left), "zh", [(0, 1), (1, 0)])
    kept_line = jnp.concatenate(ring_pairs(kept, "x"), axis=0)
    got_line = jnp.concatenate(ring_pairs(got, "y"), axis=0)

    out_weight, _, _ = lax.optimization_barrier((out_weight, kept_line, got_line))
    pieces = []
    for k in range(2):
        chosen = lax.dynamic_slice_in_dim(out_weight, (core ^ k) * CH, CH, 0)
        pairs = [(a * 2 + b, (b ^ k) * 2 + a) for a in range(2) for b in range(2)]
        pieces.append(lax.ppermute(chosen, ("zh", "c"), pairs))
    kept = jnp.stack([kept_line, pair_step(kept_line, "y", FIRST)])
    got = jnp.stack([got_line, pair_step(got_line, "x", FIRST)])
    kept, got, pieces = lax.optimization_barrier((kept, got, pieces))
    weights = (kept, pair_step(kept, "y", SECOND), got, pair_step(got, "x", SECOND))
    weights, gathered, pieces = lax.optimization_barrier((weights, gathered, pieces))
    w_out = lax.all_gather(jnp.concatenate(pieces, axis=0), "x")

    taps = lax.dynamic_slice_in_dim(short_filter, zh * CH, CH, 2)
    bias = lax.dynamic_slice_in_dim(mr_bias, zh * CH, CH, 0)[None, :]
    band = toeplitz(lax.dynamic_slice_in_dim(mr_filter, zh * GROUPS, GROUPS, 0))

    proj, tail, mid, front = project(at, gathered, weights, taps)
    w_out, tail = lax.optimization_barrier((w_out, tail))
    w_out = lax.all_gather(w_out, "y")

    last = column == 3
    to_first = jnp.where(last, tail[1], tail[0])
    to_second = jnp.where(last, tail[0], tail[1])
    first = lax.ppermute(to_first, ("y", "x"), [(i, i + 1) for i in range(15)])
    second = lax.ppermute(
        to_second, ("y", "x"), [(i, i // 4 * 4 + (i + 1) % 4) for i in range(16)]
    )
    def swapped(mine):
        return mine, lax.ppermute(mine, "c", [(0, 1), (1, 0)])

    partial = project_out(at, *swapped(mix(proj, mid, band, taps, bias, 2, 2)), w_out, 1)
    first, second, partial = lax.optimization_barrier((first, second, partial))
    halo = jnp.stack([jnp.where(leading, front, first), second])
    partial = project_out(
        at, *swapped(mix(proj, halo, band, taps, bias, 0, 2)), w_out, 0, partial
    )
    summed = lax.psum_scatter(
        partial.reshape(8, ROWS, WIDE), ("zh", "zl"), scatter_dimension=0
    )
    return (tokens.astype(F32) + summed.astype(F32)).astype(BF16)


def solution(mesh):
    split = Mesh(mesh.devices.reshape(4, 2, 4, 4, 2), ("y", "zh", "x", "zl", "c"))
    seq, tensor = ("y", "zh", "x"), ("zl", "c")
    in_specs = (
        P(seq, tensor),
        P(None, tensor),
        P(tensor),
        P(None, seq, tensor),
        P(None, None, tensor),
        P(tensor, None),
        P(tensor),
        P(tensor, seq),
    )
    return jax.shard_map(
        on_device, mesh=split, in_specs=in_specs, out_specs=P(seq, tensor), check_vma=False
    )
```

```python
import jax
import jax.numpy as jnp
from jax import lax
from jax.experimental import pallas as pl
from jax.experimental.pallas import tpu as pltpu
from jax.sharding import Mesh, PartitionSpec as P

GSIZE = 16
LH = 128
ROWS = 512
TILE = 80
SHARE = 72
HALF = ROWS // 2
WIDE = 512
CH = 256
GROUPS = CH // GSIZE
HALO = LH + 16
MIB = 1024 * 1024
F32 = jnp.float32
BF16 = jnp.bfloat16


def row_iota(shape):
    return lax.broadcasted_iota(jnp.int32, shape, 0)


def three_taps(rows, taps, s):
    return (
        taps[0, s : s + 1] * rows
        + taps[1, s : s + 1] * pltpu.roll(rows, 1, 0)
        + taps[2, s : s + 1] * pltpu.roll(rows, 2, 0)
    )


def last_rows(parts, first, shift):
    place = row_iota((16, CH)) // 2
    out = jnp.zeros((16, CH), F32)
    for s in range(3):
        moved = pltpu.roll(parts[s][first : first + 16], (2 * s + shift) % 16, 0)
        out = jnp.where(place == s, moved, out)
    return out.astype(BF16)


def as_column(row):
    column = jnp.broadcast_to(row, (128, row.shape[1])).T
    return jnp.concatenate([column] * (CH // 128), axis=1)


def project_kernel(at_ref, x_ref, *refs):
    taps_ref, proj_ref, tail_ref, mid_ref, front_ref, wide, acc, stat, ahead, sems = refs[4:]
    first_row, kind = pl.program_id(0) == 0, pl.program_id(1)
    turns = []
    for k in range(2):
        copies = []
        for i in range(4):
            for j in range(4):
                y, x = (i, j) if k == 0 else (j, i)
                start = at_ref[y] * WIDE + at_ref[4 + x] * 128
                rows = pl.ds(pl.multiple_of(start, 128), 128)
                for s in range(3):
                    source = refs[2 * k + i // 2].at[i % 2, j, s]
                    place = wide.at[k, rows, pl.ds(s * CH, CH)]
                    copies.append(pltpu.make_async_copy(source, place, sems.at[k, i, j, s]))
        turns.append(copies)

    @pl.when(first_row & (kind == 0))
    def _():
        for copies in turns:
            for copy in copies:
                copy.start()

    for k in range(2):

        @pl.when(first_row & (kind == k))
        def _(k=k):
            for copy in turns[k]:
                copy.wait()

    features = jnp.concatenate([x_ref[0, y, 0] for y in range(4)], axis=1)
    products = jnp.dot(features, wide[kind], preferred_element_type=F32)
    sums = jnp.zeros((8, WIDE), F32)
    for y in range(4):
        sums += x_ref[0, y, 0, ROWS + TILE - 16 :].astype(F32)[8:]

    @pl.when(kind == 0)
    def _():
        acc[...] = products
        stat[...] = sums

    @pl.when(kind == 1)
    def _():
        total = stat[...] + sums
        own = lax.rsqrt((total[0:1] + total[1:2]) * (1.0 / 4096.0) + 1e-6)
        extra = lax.rsqrt((total[2:3] + total[3:4]) * (1.0 / 4096.0) + 1e-6)
        own, extra = as_column(own), as_column(extra[:, :128])[:TILE]
        for s in range(3):
            lanes = slice(s * CH, (s + 1) * CH)
            whole = acc[:, lanes] + products[:, lanes]
            proj_ref[s, 0] = (whole[:ROWS] * own).astype(BF16)
            carried = (whole[ROWS:] * extra).astype(BF16).astype(F32)

            @pl.when(first_row)
            def _(s=s, carried=carried):
                ahead[s, :SHARE] = carried[:SHARE]

            @pl.when(jnp.logical_not(first_row))
            def _(s=s, carried=carried):
                ahead[s, SHARE:] = carried

        for end, ref in ((ROWS, tail_ref), (HALF, mid_ref)):
            rows = [proj_ref[s, 0, end - HALO : end].astype(F32) for s in range(3)]
            mixing = three_taps(rows[1], taps_ref, 1) * three_taps(rows[2], taps_ref, 2)
            ref[0, :LH] = mixing[HALO - LH :].astype(BF16)
            ref[0, LH:] = last_rows(rows, HALO - 16, 2)

    @pl.when((pl.program_id(0) == 1) & (kind == 1))
    def _():
        mixing = three_taps(ahead[1], taps_ref, 1) * three_taps(ahead[2], taps_ref, 2)
        front_ref[:LH] = pltpu.roll(mixing, SHARE + TILE - 1, 0)[:LH].astype(BF16)
        front_ref[LH:] = last_rows(ahead, LH - 8, -7)


def project(at, gathered, weights, taps):
    return pl.pallas_call(
        project_kernel,
        grid_spec=pltpu.PrefetchScalarGridSpec(
            num_scalar_prefetch=1,
            grid=(2, 2),
            in_specs=[
                pl.BlockSpec(
                    (1, 4, 1, ROWS + TILE, WIDE),
                    lambda h, k, at: (h, 0, at[8] + k - 2 * at[8] * k, 0, 0),
                ),
                *[pl.BlockSpec(memory_space=pl.ANY)] * 4,
                pl.BlockSpec((3, 3, CH), lambda h, k, at: (0, 0, 0)),
            ],
            out_specs=[
                pl.BlockSpec((3, 1, ROWS, CH), lambda h, k, at: (0, h, 0, 0)),
                pl.BlockSpec((1, HALO, CH), lambda h, k, at: (h, 0, 0)),
                pl.BlockSpec((1, HALO, CH), lambda h, k, at: (h, 0, 0)),
                pl.BlockSpec((HALO, CH), lambda h, k, at: (0, 0)),
            ],
            scratch_shapes=[
                pltpu.VMEM((2, 4 * WIDE, 3 * CH), BF16),
                pltpu.VMEM((ROWS + TILE, 3 * CH), F32),
                pltpu.VMEM((8, WIDE), F32),
                pltpu.VMEM((3, SHARE + TILE, CH), F32),
                pltpu.SemaphoreType.DMA((2, 4, 4, 3)),
            ],
        ),
        out_shape=[
            jax.ShapeDtypeStruct((3, 2, ROWS, CH), BF16),
            jax.ShapeDtypeStruct((2, HALO, CH), BF16),
            jax.ShapeDtypeStruct((2, HALO, CH), BF16),
            jax.ShapeDtypeStruct((HALO, CH), BF16),
        ],
        compiler_params=pltpu.CompilerParams(vmem_limit_bytes=46 * MIB),
        cost_estimate=pl.CostEstimate(
            flops=2 * 2 * ROWS * 4096 * 3 * CH, bytes_accessed=18_000_000, transcendentals=0
        ),
        name="project",
    )(at, gathered, *weights, taps)


def toeplitz_kernel(u_ref, out_ref):
    for g in range(GROUPS):
        wide = jnp.broadcast_to(u_ref[g : g + 1], (LH, 3 * LH))
        skewed = pltpu.roll(wide, 0, 1, stride=1, stride_axis=0)
        out_ref[g] = skewed[:, : 2 * LH].astype(BF16)


def toeplitz(filters):
    backwards = jnp.flip(filters.astype(F32), 1)
    row = jnp.pad(backwards, ((0, 0), (1, 2 * LH - 1)))
    return pl.pallas_call(
        toeplitz_kernel,
        out_shape=jax.ShapeDtypeStruct((GROUPS, LH, 2 * LH), BF16),
        compiler_params=pltpu.CompilerParams(vmem_limit_bytes=8 * MIB),
        name="toeplitz",
    )(row)


def mix_kernel(proj_ref, halo_ref, band_ref, taps_ref, bias_ref, out_ref, before, edge):
    step = pl.program_id(0)

    @pl.when(step == 0)
    def _():
        for h in range(2):
            before[h] = halo_ref[h, :LH]
            last = halo_ref[h, LH:].astype(F32)
            for s in range(3):
                edge[h, s] = pltpu.roll(last, (6 - 2 * s) % 16, 0)[:8]

    queries = []
    mixes = []
    windows = []
    for h in range(2):
        feats = []
        for s in range(3):
            lifted = proj_ref[s, h].astype(F32)
            rows = jnp.concatenate([edge[h, s], lifted], axis=0)
            feats.append(three_taps(rows, taps_ref, s)[8:])
            edge[h, s] = lifted[LH - 8 :]
        mixing = (feats[1] * feats[2]).astype(BF16)
        queries.append(feats[0])
        mixes.append(mixing)
        windows.append(jnp.concatenate([before[h], mixing], axis=0))
        before[h] = mixing
    lane_group = lax.broadcasted_iota(jnp.int32, (LH, 2 * LH), 1) % LH // GSIZE
    halves = []
    for half in range(2):
        lanes = slice(half * LH, (half + 1) * LH)
        window = jnp.concatenate([windows[0][:, lanes], windows[1][:, lanes]], axis=1)
        total = jnp.zeros((LH, 2 * LH), F32)
        for g in range(GROUPS // 2):
            one = jnp.dot(band_ref[half * 8 + g], window, preferred_element_type=F32)
            total = jnp.where(lane_group == g, one, total)
        halves.append(total)
    for h in range(2):
        rows = slice(h * LH, (h + 1) * LH)
        filtered = jnp.concatenate([halves[0][:, rows], halves[1][:, rows]], axis=1)
        value = queries[h] * (filtered + bias_ref[...] * mixes[h].astype(F32))
        out_ref[h] = value.astype(BF16)


def mix(proj, halo, band, taps, bias, first, count):
    return pl.pallas_call(
        mix_kernel,
        grid=(count,),
        in_specs=[
            pl.BlockSpec((3, 2, LH, CH), lambda b: (0, 0, b + first, 0)),
            pl.BlockSpec((2, HALO, CH), lambda b: (0, 0, 0)),
            pl.BlockSpec((GROUPS, LH, 2 * LH), lambda b: (0, 0, 0)),
            pl.BlockSpec((3, 3, CH), lambda b: (0, 0, 0)),
            pl.BlockSpec((1, CH), lambda b: (0, 0)),
        ],
        out_specs=pl.BlockSpec((2, LH, CH), lambda b: (0, b, 0)),
        out_shape=jax.ShapeDtypeStruct((2, count * LH, CH), BF16),
        scratch_shapes=[
            pltpu.VMEM((2, LH, CH), BF16),
            pltpu.VMEM((2, 3, 8, CH), F32),
        ],
        compiler_params=pltpu.CompilerParams(vmem_limit_bytes=16 * MIB),
        cost_estimate=pl.CostEstimate(
            flops=2 * 512 * CH * 2048, bytes_accessed=2_000_000, transcendentals=0
        ),
        name="mix",
    )(proj, halo, band, taps, bias)


def out_kernel(at_ref, mine_ref, other_ref, *refs):
    out_ref, wide, rows, sems = refs[-4:]
    step = pl.program_id(0)

    @pl.when(step == 0)
    def _():
        copies = []
        for k in range(2):
            for i in range(4):
                for j in range(4):
                    y, x = (i, j) if k == 0 else (j, i)
                    lanes = pl.ds(pl.multiple_of(at_ref[4 + x] * 128, 128), 128)
                    for part in range(2):
                        source = refs[2 * k + i // 2].at[i % 2, j, 3, :, pl.ds(part * 128, 128)]
                        place = wide.at[at_ref[y], pl.ds(k * CH + part * 128, 128), lanes]
                        sem = sems.at[k, i, j, part]
                        copies.append(pltpu.make_async_copy(source, place, sem))
        for copy in copies:
            copy.start()
        swap = at_ref[9] == 1
        for h in range(2):
            place = slice(h * HALF, (h + 1) * HALF)
            rows[place, :CH] = jnp.where(swap, other_ref[h], mine_ref[h])
            rows[place, CH:] = jnp.where(swap, mine_ref[h], other_ref[h])

        for copy in copies:
            copy.wait()

    products = jnp.dot(rows[...], wide[step], preferred_element_type=F32).astype(BF16)
    for h in range(2):
        out_ref[h, 0] = products[h * HALF : (h + 1) * HALF]


def project_out(at, mine, other, weights, half, base=None):
    more = () if base is None else (base,)
    return pl.pallas_call(
        out_kernel,
        grid_spec=pltpu.PrefetchScalarGridSpec(
            num_scalar_prefetch=1,
            grid=(4,),
            in_specs=[
                *[pl.BlockSpec((2, HALF, CH), lambda k, at: (0, 0, 0))] * 2,
                *[pl.BlockSpec(memory_space=pl.ANY)] * (4 + len(more)),
            ],
            out_specs=pl.BlockSpec((2, 1, HALF, WIDE), lambda k, at: (0, k, half, 0)),
            scratch_shapes=[
                pltpu.VMEM((4, 2 * CH, WIDE), BF16),
                pltpu.VMEM((2 * HALF, 2 * CH), BF16),
                pltpu.SemaphoreType.DMA((2, 4, 4, 2)),
            ],
        ),
        out_shape=jax.ShapeDtypeStruct((2, 4, ROWS, WIDE), BF16),
        input_output_aliases={} if base is None else {7: 0},
        compiler_params=pltpu.CompilerParams(vmem_limit_bytes=45 * MIB),
        cost_estimate=pl.CostEstimate(
            flops=2 * 512 * 2 * CH * 2048, bytes_accessed=5_000_000, transcendentals=0
        ),
        name="project_out",
    )(at, mine, other, *weights, *more)


FIRST, SECOND = (1, 3), (3, 1)


def pair_step(value, axis, masks):
    pairs = [(i * 2 + c, (i ^ masks[c]) * 2 + c) for i in range(4) for c in range(2)]
    return lax.ppermute(value, (axis, "c"), pairs)


def ring_pairs(piece, axis):
    here = jnp.stack([piece, pair_step(piece, axis, FIRST)])
    return here, pair_step(here, axis, SECOND)


def on_device(
    tokens, prior_rows, norm_gain, in_weight, short_filter, mr_filter, mr_bias, out_weight
):
    zh = lax.axis_index("zh")
    column = lax.axis_index("x")
    leading = (column == 0) & (lax.axis_index("y") == 0)

    core = lax.axis_index("c")
    turns = jnp.where(core == 0, jnp.array([0, 1, 3, 2]), jnp.array([0, 3, 1, 2]))
    at = jnp.concatenate(
        [lax.axis_index("y") ^ turns, column ^ turns, jnp.stack([zh, zh ^ core])]
    ).astype(jnp.int32)
    ring = ("zh", "zl", "c")
    padded = jnp.pad(prior_rows, ((0, 2 * SHARE - prior_rows.shape[0]), (0, 0)))
    some = lax.dynamic_slice_in_dim(padded, zh * SHARE, SHARE, 0)
    lifted, carried = tokens.astype(F32), some.astype(F32)
    gain = norm_gain.astype(F32)
    sums = jnp.sum(lifted * lifted, axis=1)
    more = jnp.pad(jnp.sum(carried * carried, axis=1), (0, WIDE - SHARE))
    sums = jnp.stack([sums, more])
    coarse = lax.reduce_precision(sums, 8, 7)
    terms = jnp.stack([coarse, sums - coarse], axis=1).reshape(4, WIDE).astype(BF16)
    own = jnp.concatenate(
        [
            (lifted * gain).astype(BF16),
            (carried * gain).astype(BF16),
            jnp.pad(terms, ((0, TILE - SHARE - 4), (0, 0))),
        ],
        axis=0,
    )
    gathered = lax.all_gather(own, ring).reshape(2, 4, 2, ROWS + TILE, WIDE)

    left, right = in_weight[..., :CH], in_weight[..., CH:]
    kept = jnp.where(zh == 0, left, right)
    got = lax.ppermute(jnp.where(zh == 0, right, left), "zh", [(0, 1), (1, 0)])
    pieces = []
    for k in range(2):
        chosen = lax.dynamic_slice_in_dim(out_weight, (core ^ k) * CH, CH, 0)
        pairs = [(a * 2 + b, (b ^ k) * 2 + a) for a in range(2) for b in range(2)]
        chosen = lax.ppermute(chosen, ("zh", "c"), pairs)
        pieces.append(jnp.concatenate([chosen[:128], chosen[128:]], axis=1)[None])
    kept = jnp.concatenate([kept, pieces[0]], axis=0)
    got = jnp.concatenate([got, pieces[1]], axis=0)
    weights = (
        *ring_pairs(jnp.concatenate(ring_pairs(kept, "x"), axis=0), "y"),
        *ring_pairs(jnp.concatenate(ring_pairs(got, "y"), axis=0), "x"),
    )
    weights, gathered = lax.optimization_barrier((weights, gathered))

    taps = lax.dynamic_slice_in_dim(short_filter, zh * CH, CH, 2)
    bias = lax.dynamic_slice_in_dim(mr_bias, zh * CH, CH, 0)[None, :]
    band = toeplitz(lax.dynamic_slice_in_dim(mr_filter, zh * GROUPS, GROUPS, 0))

    proj, tail, mid, front = project(at, gathered, weights, taps)

    last = column == 3
    to_first = jnp.where(last, tail[1], tail[0])
    to_second = jnp.where(last, tail[0], tail[1])
    first = lax.ppermute(to_first, ("y", "x"), [(i, i + 1) for i in range(15)])
    second = lax.ppermute(
        to_second, ("y", "x"), [(i, i // 4 * 4 + (i + 1) % 4) for i in range(16)]
    )
    def swapped(mine):
        return mine, lax.ppermute(mine, "c", [(0, 1), (1, 0)])

    partial = project_out(at, *swapped(mix(proj, mid, band, taps, bias, 2, 2)), weights, 1)
    first, second, partial = lax.optimization_barrier((first, second, partial))
    halo = jnp.stack([jnp.where(leading, front, first), second])
    partial = project_out(
        at, *swapped(mix(proj, halo, band, taps, bias, 0, 2)), weights, 0, partial
    )
    summed = lax.psum_scatter(
        partial.reshape(8, ROWS, WIDE), ("zh", "zl"), scatter_dimension=0
    )
    return (tokens.astype(F32) + summed.astype(F32)).astype(BF16)


def solution(mesh):
    split = Mesh(mesh.devices.reshape(4, 2, 4, 4, 2), ("y", "zh", "x", "zl", "c"))
    seq, tensor = ("y", "zh", "x"), ("zl", "c")
    in_specs = (
        P(seq, tensor),
        P(None, tensor),
        P(tensor),
        P(None, seq, tensor),
        P(None, None, tensor),
        P(tensor, None),
        P(tensor),
        P(tensor, seq),
    )
    return jax.shard_map(
        on_device, mesh=split, in_specs=in_specs, out_specs=P(seq, tensor), check_vma=False
    )
```

```python
import jax
import jax.numpy as jnp
from jax import lax
from jax.experimental import pallas as pl
from jax.experimental.pallas import tpu as pltpu
from jax.sharding import Mesh, PartitionSpec as P

GSIZE = 16
LH = 128
ROWS = 512
TILE = 80
SHARE = 72
HALF = ROWS // 2
WIDE = 512
CH = 256
GROUPS = CH // GSIZE
HALO = LH + 16
MIB = 1024 * 1024
F32 = jnp.float32
BF16 = jnp.bfloat16


def row_iota(shape):
    return lax.broadcasted_iota(jnp.int32, shape, 0)


def three_taps(rows, taps, s):
    return (
        taps[0, s : s + 1] * rows
        + taps[1, s : s + 1] * pltpu.roll(rows, 1, 0)
        + taps[2, s : s + 1] * pltpu.roll(rows, 2, 0)
    )


def last_rows(parts, first, shift):
    place = row_iota((16, CH)) // 2
    out = jnp.zeros((16, CH), F32)
    for s in range(3):
        moved = pltpu.roll(parts[s][first : first + 16], (2 * s + shift) % 16, 0)
        out = jnp.where(place == s, moved, out)
    return out.astype(BF16)


def as_column(row):
    column = jnp.broadcast_to(row, (128, row.shape[1])).T
    return jnp.concatenate([column] * (CH // 128), axis=1)


def project_kernel(at_ref, x_ref, *refs):
    taps_ref, proj_ref, tail_ref, mid_ref, front_ref, out_w_ref = refs[4:10]
    wide, acc, stat, ahead, sems, out_sems = refs[10:]
    first_row, kind = pl.program_id(0) == 0, pl.program_id(1)
    turns = []
    out_copies = []
    for k in range(2):
        copies = []
        for i in range(4):
            for j in range(4):
                y, x = (i, j) if k == 0 else (j, i)
                start = at_ref[y] * WIDE + at_ref[4 + x] * 128
                rows = pl.ds(pl.multiple_of(start, 128), 128)
                for s in range(3):
                    source = refs[2 * k + i // 2].at[i % 2, j, s]
                    place = wide.at[k, rows, pl.ds(s * CH, CH)]
                    copies.append(pltpu.make_async_copy(source, place, sems.at[k, i, j, s]))
                lanes = pl.ds(pl.multiple_of(at_ref[4 + x] * 128, 128), 128)
                for part in range(2):
                    source = refs[2 * k + i // 2].at[i % 2, j, 3, :, pl.ds(part * 128, 128)]
                    place = out_w_ref.at[at_ref[y], pl.ds(k * CH + part * 128, 128), lanes]
                    sem = out_sems.at[k, i, j, part]
                    out_copies.append(pltpu.make_async_copy(source, place, sem))
        turns.append(copies)

    @pl.when(first_row & (kind == 0))
    def _():
        for copies in turns:
            for copy in copies:
                copy.start()
        for copy in out_copies:
            copy.start()

    for k in range(2):

        @pl.when(first_row & (kind == k))
        def _(k=k):
            for copy in turns[k]:
                copy.wait()

    features = jnp.concatenate([x_ref[0, y, 0] for y in range(4)], axis=1)
    products = jnp.dot(features, wide[kind], preferred_element_type=F32)
    sums = jnp.zeros((8, WIDE), F32)
    for y in range(4):
        sums += x_ref[0, y, 0, ROWS + TILE - 16 :].astype(F32)[8:]

    @pl.when(kind == 0)
    def _():
        acc[...] = products
        stat[...] = sums

    @pl.when(kind == 1)
    def _():
        total = stat[...] + sums
        own = lax.rsqrt((total[0:1] + total[1:2]) * (1.0 / 4096.0) + 1e-6)
        extra = lax.rsqrt((total[2:3] + total[3:4]) * (1.0 / 4096.0) + 1e-6)
        own, extra = as_column(own), as_column(extra[:, :128])[:TILE]
        for s in range(3):
            lanes = slice(s * CH, (s + 1) * CH)
            whole = acc[:, lanes] + products[:, lanes]
            proj_ref[s, 0] = (whole[:ROWS] * own).astype(BF16)
            carried = (whole[ROWS:] * extra).astype(BF16).astype(F32)

            @pl.when(first_row)
            def _(s=s, carried=carried):
                ahead[s, :SHARE] = carried[:SHARE]

            @pl.when(jnp.logical_not(first_row))
            def _(s=s, carried=carried):
                ahead[s, SHARE:] = carried

        for end, ref in ((ROWS, tail_ref), (HALF, mid_ref)):
            rows = [proj_ref[s, 0, end - HALO : end].astype(F32) for s in range(3)]
            mixing = three_taps(rows[1], taps_ref, 1) * three_taps(rows[2], taps_ref, 2)
            ref[0, :LH] = mixing[HALO - LH :].astype(BF16)
            ref[0, LH:] = last_rows(rows, HALO - 16, 2)

    @pl.when((pl.program_id(0) == 1) & (kind == 1))
    def _():
        mixing = three_taps(ahead[1], taps_ref, 1) * three_taps(ahead[2], taps_ref, 2)
        front_ref[:LH] = pltpu.roll(mixing, SHARE + TILE - 1, 0)[:LH].astype(BF16)
        front_ref[LH:] = last_rows(ahead, LH - 8, -7)
        for copy in out_copies:
            copy.wait()


def project(at, gathered, weights, taps):
    return pl.pallas_call(
        project_kernel,
        grid_spec=pltpu.PrefetchScalarGridSpec(
            num_scalar_prefetch=1,
            grid=(2, 2),
            in_specs=[
                pl.BlockSpec(
                    (1, 4, 1, ROWS + TILE, WIDE),
                    lambda h, k, at: (h, 0, at[8] + k - 2 * at[8] * k, 0, 0),
                ),
                *[pl.BlockSpec(memory_space=pl.ANY)] * 4,
                pl.BlockSpec((3, 3, CH), lambda h, k, at: (0, 0, 0)),
            ],
            out_specs=[
                pl.BlockSpec((3, 1, ROWS, CH), lambda h, k, at: (0, h, 0, 0)),
                pl.BlockSpec((1, HALO, CH), lambda h, k, at: (h, 0, 0)),
                pl.BlockSpec((1, HALO, CH), lambda h, k, at: (h, 0, 0)),
                pl.BlockSpec((HALO, CH), lambda h, k, at: (0, 0)),
                pl.BlockSpec(memory_space=pl.ANY),
            ],
            scratch_shapes=[
                pltpu.VMEM((2, 4 * WIDE, 3 * CH), BF16),
                pltpu.VMEM((ROWS + TILE, 3 * CH), F32),
                pltpu.VMEM((8, WIDE), F32),
                pltpu.VMEM((3, SHARE + TILE, CH), F32),
                pltpu.SemaphoreType.DMA((2, 4, 4, 3)),
                pltpu.SemaphoreType.DMA((2, 4, 4, 2)),
            ],
        ),
        out_shape=[
            jax.ShapeDtypeStruct((3, 2, ROWS, CH), BF16),
            jax.ShapeDtypeStruct((2, HALO, CH), BF16),
            jax.ShapeDtypeStruct((2, HALO, CH), BF16),
            jax.ShapeDtypeStruct((HALO, CH), BF16),
            jax.ShapeDtypeStruct((4, 2 * CH, WIDE), BF16),
        ],
        compiler_params=pltpu.CompilerParams(vmem_limit_bytes=46 * MIB),
        cost_estimate=pl.CostEstimate(
            flops=2 * 2 * ROWS * 4096 * 3 * CH, bytes_accessed=18_000_000, transcendentals=0
        ),
        name="project",
    )(at, gathered, *weights, taps)


def toeplitz_kernel(u_ref, out_ref):
    for g in range(GROUPS):
        wide = jnp.broadcast_to(u_ref[g : g + 1], (LH, 3 * LH))
        skewed = pltpu.roll(wide, 0, 1, stride=1, stride_axis=0)
        out_ref[g] = skewed[:, : 2 * LH].astype(BF16)


def toeplitz(filters):
    backwards = jnp.flip(filters.astype(F32), 1)
    row = jnp.pad(backwards, ((0, 0), (1, 2 * LH - 1)))
    return pl.pallas_call(
        toeplitz_kernel,
        out_shape=jax.ShapeDtypeStruct((GROUPS, LH, 2 * LH), BF16),
        compiler_params=pltpu.CompilerParams(vmem_limit_bytes=8 * MIB),
        name="toeplitz",
    )(row)


def mix_kernel(proj_ref, halo_ref, band_ref, taps_ref, bias_ref, out_ref, before, edge):
    step = pl.program_id(0)

    @pl.when(step == 0)
    def _():
        for h in range(2):
            before[h] = halo_ref[h, :LH]
            last = halo_ref[h, LH:].astype(F32)
            for s in range(3):
                edge[h, s] = pltpu.roll(last, (6 - 2 * s) % 16, 0)[:8]

    queries = []
    mixes = []
    windows = []
    for h in range(2):
        feats = []
        for s in range(3):
            lifted = proj_ref[s, h].astype(F32)
            rows = jnp.concatenate([edge[h, s], lifted], axis=0)
            feats.append(three_taps(rows, taps_ref, s)[8:])
            edge[h, s] = lifted[LH - 8 :]
        mixing = (feats[1] * feats[2]).astype(BF16)
        queries.append(feats[0])
        mixes.append(mixing)
        windows.append(jnp.concatenate([before[h], mixing], axis=0))
        before[h] = mixing
    lane_group = lax.broadcasted_iota(jnp.int32, (LH, 2 * LH), 1) % LH // GSIZE
    halves = []
    for half in range(2):
        lanes = slice(half * LH, (half + 1) * LH)
        window = jnp.concatenate([windows[0][:, lanes], windows[1][:, lanes]], axis=1)
        total = jnp.zeros((LH, 2 * LH), F32)
        for g in range(GROUPS // 2):
            one = jnp.dot(band_ref[half * 8 + g], window, preferred_element_type=F32)
            total = jnp.where(lane_group == g, one, total)
        halves.append(total)
    for h in range(2):
        rows = slice(h * LH, (h + 1) * LH)
        filtered = jnp.concatenate([halves[0][:, rows], halves[1][:, rows]], axis=1)
        value = queries[h] * (filtered + bias_ref[...] * mixes[h].astype(F32))
        out_ref[h] = value.astype(BF16)


def mix(proj, halo, band, taps, bias, first, count):
    return pl.pallas_call(
        mix_kernel,
        grid=(count,),
        in_specs=[
            pl.BlockSpec((3, 2, LH, CH), lambda b: (0, 0, b + first, 0)),
            pl.BlockSpec((2, HALO, CH), lambda b: (0, 0, 0)),
            pl.BlockSpec((GROUPS, LH, 2 * LH), lambda b: (0, 0, 0)),
            pl.BlockSpec((3, 3, CH), lambda b: (0, 0, 0)),
            pl.BlockSpec((1, CH), lambda b: (0, 0)),
        ],
        out_specs=pl.BlockSpec((2, LH, CH), lambda b: (0, b, 0)),
        out_shape=jax.ShapeDtypeStruct((2, count * LH, CH), BF16),
        scratch_shapes=[
            pltpu.VMEM((2, LH, CH), BF16),
            pltpu.VMEM((2, 3, 8, CH), F32),
        ],
        compiler_params=pltpu.CompilerParams(vmem_limit_bytes=16 * MIB),
        cost_estimate=pl.CostEstimate(
            flops=2 * 512 * CH * 2048, bytes_accessed=2_000_000, transcendentals=0
        ),
        name="mix",
    )(proj, halo, band, taps, bias)


def out_kernel(at_ref, mine_ref, other_ref, w_ref, *refs):
    out_ref, rows = refs[-2:]

    @pl.when(pl.program_id(0) == 0)
    def _():
        swap = at_ref[9] == 1
        for h in range(2):
            place = slice(h * HALF, (h + 1) * HALF)
            rows[place, :CH] = jnp.where(swap, other_ref[h], mine_ref[h])
            rows[place, CH:] = jnp.where(swap, mine_ref[h], other_ref[h])

    products = jnp.dot(rows[...], w_ref[0], preferred_element_type=F32).astype(BF16)
    for h in range(2):
        out_ref[h, 0] = products[h * HALF : (h + 1) * HALF]


def project_out(at, mine, other, weights, half, base=None):
    more = () if base is None else (base,)
    return pl.pallas_call(
        out_kernel,
        grid_spec=pltpu.PrefetchScalarGridSpec(
            num_scalar_prefetch=1,
            grid=(4,),
            in_specs=[
                *[pl.BlockSpec((2, HALF, CH), lambda k, at: (0, 0, 0))] * 2,
                pl.BlockSpec((1, 2 * CH, WIDE), lambda k, at: (k, 0, 0)),
                *[pl.BlockSpec(memory_space=pl.ANY)] * len(more),
            ],
            out_specs=pl.BlockSpec((2, 1, HALF, WIDE), lambda k, at: (0, k, half, 0)),
            scratch_shapes=[pltpu.VMEM((2 * HALF, 2 * CH), BF16)],
        ),
        out_shape=jax.ShapeDtypeStruct((2, 4, ROWS, WIDE), BF16),
        input_output_aliases={} if base is None else {4: 0},
        compiler_params=pltpu.CompilerParams(vmem_limit_bytes=52 * MIB),
        cost_estimate=pl.CostEstimate(
            flops=2 * 512 * 2 * CH * 2048, bytes_accessed=5_000_000, transcendentals=0
        ),
        name="project_out",
    )(at, mine, other, weights, *more)


FIRST, SECOND = (1, 3), (3, 1)


def pair_step(value, axis, masks):
    pairs = [(i * 2 + c, (i ^ masks[c]) * 2 + c) for i in range(4) for c in range(2)]
    return lax.ppermute(value, (axis, "c"), pairs)


def ring_pairs(piece, axis):
    here = jnp.stack([piece, pair_step(piece, axis, FIRST)])
    return here, pair_step(here, axis, SECOND)


def on_device(
    tokens, prior_rows, norm_gain, in_weight, short_filter, mr_filter, mr_bias, out_weight
):
    zh = lax.axis_index("zh")
    column = lax.axis_index("x")
    leading = (column == 0) & (lax.axis_index("y") == 0)

    core = lax.axis_index("c")
    turns = jnp.where(core == 0, jnp.array([0, 1, 3, 2]), jnp.array([0, 3, 1, 2]))
    at = jnp.concatenate(
        [lax.axis_index("y") ^ turns, column ^ turns, jnp.stack([zh, zh ^ core])]
    ).astype(jnp.int32)
    ring = ("zh", "zl", "c")
    padded = jnp.pad(prior_rows, ((0, 2 * SHARE - prior_rows.shape[0]), (0, 0)))
    some = lax.dynamic_slice_in_dim(padded, zh * SHARE, SHARE, 0)
    lifted, carried = tokens.astype(F32), some.astype(F32)
    gain = norm_gain.astype(F32)
    sums = jnp.sum(lifted * lifted, axis=1)
    more = jnp.pad(jnp.sum(carried * carried, axis=1), (0, WIDE - SHARE))
    sums = jnp.stack([sums, more])
    coarse = lax.reduce_precision(sums, 8, 7)
    terms = jnp.stack([coarse, sums - coarse], axis=1).reshape(4, WIDE).astype(BF16)
    own = jnp.concatenate(
        [
            (lifted * gain).astype(BF16),
            (carried * gain).astype(BF16),
            jnp.pad(terms, ((0, TILE - SHARE - 4), (0, 0))),
        ],
        axis=0,
    )

    left, right = in_weight[..., :CH], in_weight[..., CH:]
    kept = jnp.where(zh == 0, left, right)
    got = lax.ppermute(jnp.where(zh == 0, right, left), "zh", [(0, 1), (1, 0)])
    pieces = []
    for k in range(2):
        chosen = lax.dynamic_slice_in_dim(out_weight, (core ^ k) * CH, CH, 0)
        pairs = [(a * 2 + b, (b ^ k) * 2 + a) for a in range(2) for b in range(2)]
        chosen = lax.ppermute(chosen, ("zh", "c"), pairs)
        pieces.append(jnp.concatenate([chosen[:128], chosen[128:]], axis=1)[None])
    own, got, pieces = lax.optimization_barrier((own, got, pieces))
    gathered = lax.all_gather(own, ring).reshape(2, 4, 2, ROWS + TILE, WIDE)
    kept = jnp.concatenate([kept, pieces[0]], axis=0)
    got = jnp.concatenate([got, pieces[1]], axis=0)
    weights = (
        *ring_pairs(jnp.concatenate(ring_pairs(kept, "x"), axis=0), "y"),
        *ring_pairs(jnp.concatenate(ring_pairs(got, "y"), axis=0), "x"),
    )
    weights, gathered = lax.optimization_barrier((weights, gathered))

    taps = lax.dynamic_slice_in_dim(short_filter, zh * CH, CH, 2)
    bias = lax.dynamic_slice_in_dim(mr_bias, zh * CH, CH, 0)[None, :]
    band = toeplitz(lax.dynamic_slice_in_dim(mr_filter, zh * GROUPS, GROUPS, 0))

    proj, tail, mid, front, w_out = project(at, gathered, weights, taps)

    last = column == 3
    to_first = jnp.where(last, tail[1], tail[0])
    to_second = jnp.where(last, tail[0], tail[1])
    first = lax.ppermute(to_first, ("y", "x"), [(i, i + 1) for i in range(15)])
    second = lax.ppermute(
        to_second, ("y", "x"), [(i, i // 4 * 4 + (i + 1) % 4) for i in range(16)]
    )
    def swapped(mine):
        return mine, lax.ppermute(mine, "c", [(0, 1), (1, 0)])

    partial = project_out(at, *swapped(mix(proj, mid, band, taps, bias, 2, 2)), w_out, 1)
    first, second, partial = lax.optimization_barrier((first, second, partial))
    halo = jnp.stack([jnp.where(leading, front, first), second])
    partial = project_out(
        at, *swapped(mix(proj, halo, band, taps, bias, 0, 2)), w_out, 0, partial
    )
    summed = lax.psum_scatter(
        partial.reshape(8, ROWS, WIDE), ("zh", "zl"), scatter_dimension=0
    )
    return (tokens.astype(F32) + summed.astype(F32)).astype(BF16)


def solution(mesh):
    split = Mesh(mesh.devices.reshape(4, 2, 4, 4, 2), ("y", "zh", "x", "zl", "c"))
    seq, tensor = ("y", "zh", "x"), ("zl", "c")
    in_specs = (
        P(seq, tensor),
        P(None, tensor),
        P(tensor),
        P(None, seq, tensor),
        P(None, None, tensor),
        P(tensor, None),
        P(tensor),
        P(tensor, seq),
    )
    return jax.shard_map(
        on_device, mesh=split, in_specs=in_specs, out_specs=P(seq, tensor), check_vma=False
    )
```

```python
import jax
import jax.numpy as jnp
from jax import lax
from jax.experimental import pallas as pl
from jax.experimental.pallas import tpu as pltpu
from jax.sharding import Mesh, PartitionSpec as P

GSIZE = 16
LH = 128
ROWS = 512
TILE = 80
SHARE = 72
HALF = ROWS // 2
WIDE = 512
CH = 256
GROUPS = CH // GSIZE
HALO = LH + 16
MIB = 1024 * 1024
F32 = jnp.float32
BF16 = jnp.bfloat16


def row_iota(shape):
    return lax.broadcasted_iota(jnp.int32, shape, 0)


def three_taps(rows, taps, s):
    return (
        taps[0, s : s + 1] * rows
        + taps[1, s : s + 1] * pltpu.roll(rows, 1, 0)
        + taps[2, s : s + 1] * pltpu.roll(rows, 2, 0)
    )


def last_rows(parts, first, shift):
    place = row_iota((16, CH)) // 2
    out = jnp.zeros((16, CH), F32)
    for s in range(3):
        moved = pltpu.roll(parts[s][first : first + 16], (2 * s + shift) % 16, 0)
        out = jnp.where(place == s, moved, out)
    return out.astype(BF16)


def as_column(row):
    column = jnp.broadcast_to(row, (128, row.shape[1])).T
    return jnp.concatenate([column] * (CH // 128), axis=1)


def project_kernel(at_ref, x_ref, *refs):
    taps_ref, proj_ref, tail_ref, mid_ref, front_ref, out_w_ref = refs[4:10]
    wide, acc, stat, ahead, sems, out_sems = refs[10:]
    first_row, kind = pl.program_id(0) == 0, pl.program_id(1)
    turns = []
    out_copies = []
    for k in range(2):
        copies = []
        for i in range(4):
            for j in range(4):
                y, x = (i, j) if k == 0 else (j, i)
                start = at_ref[y] * WIDE + at_ref[4 + x] * 128
                rows = pl.ds(pl.multiple_of(start, 128), 128)
                for s in range(3):
                    source = refs[2 * k + i // 2].at[i % 2, j, s]
                    place = wide.at[k, rows, pl.ds(s * CH, CH)]
                    copies.append(pltpu.make_async_copy(source, place, sems.at[k, i, j, s]))
                lanes = pl.ds(pl.multiple_of(at_ref[4 + x] * 128, 128), 128)
                for part in range(2):
                    source = refs[2 * k + i // 2].at[i % 2, j, 3, :, pl.ds(part * 128, 128)]
                    place = out_w_ref.at[at_ref[y], pl.ds(k * CH + part * 128, 128), lanes]
                    sem = out_sems.at[k, i, j, part]
                    out_copies.append(pltpu.make_async_copy(source, place, sem))
        turns.append(copies)

    @pl.when(first_row & (kind == 0))
    def _():
        for copies in turns:
            for copy in copies:
                copy.start()
        for copy in out_copies:
            copy.start()

    for k in range(2):

        @pl.when(first_row & (kind == k))
        def _(k=k):
            for copy in turns[k]:
                copy.wait()

    features = jnp.concatenate([x_ref[0, y, 0] for y in range(4)], axis=1)
    products = jnp.dot(features, wide[kind], preferred_element_type=F32)
    sums = jnp.zeros((8, WIDE), F32)
    for y in range(4):
        sums += x_ref[0, y, 0, ROWS + TILE - 16 :].astype(F32)[8:]

    @pl.when(kind == 0)
    def _():
        acc[...] = products
        stat[...] = sums

    @pl.when(kind == 1)
    def _():
        total = stat[...] + sums
        own = lax.rsqrt((total[0:1] + total[1:2]) * (1.0 / 4096.0) + 1e-6)
        extra = lax.rsqrt((total[2:3] + total[3:4]) * (1.0 / 4096.0) + 1e-6)
        own, extra = as_column(own), as_column(extra[:, :128])[:TILE]
        for s in range(3):
            lanes = slice(s * CH, (s + 1) * CH)
            whole = acc[:, lanes] + products[:, lanes]
            proj_ref[s, 0] = (whole[:ROWS] * own).astype(BF16)
            carried = (whole[ROWS:] * extra).astype(BF16).astype(F32)

            @pl.when(first_row)
            def _(s=s, carried=carried):
                ahead[s, :SHARE] = carried[:SHARE]

            @pl.when(jnp.logical_not(first_row))
            def _(s=s, carried=carried):
                ahead[s, SHARE:] = carried

        for end, ref in ((ROWS, tail_ref), (HALF, mid_ref)):
            rows = [proj_ref[s, 0, end - HALO : end].astype(F32) for s in range(3)]
            mixing = three_taps(rows[1], taps_ref, 1) * three_taps(rows[2], taps_ref, 2)
            ref[0, :LH] = mixing[HALO - LH :].astype(BF16)
            ref[0, LH:] = last_rows(rows, HALO - 16, 2)

    @pl.when((pl.program_id(0) == 1) & (kind == 1))
    def _():
        mixing = three_taps(ahead[1], taps_ref, 1) * three_taps(ahead[2], taps_ref, 2)
        front_ref[:LH] = pltpu.roll(mixing, SHARE + TILE - 1, 0)[:LH].astype(BF16)
        front_ref[LH:] = last_rows(ahead, LH - 8, -7)
        for copy in out_copies:
            copy.wait()


def project(at, gathered, weights, taps):
    return pl.pallas_call(
        project_kernel,
        grid_spec=pltpu.PrefetchScalarGridSpec(
            num_scalar_prefetch=1,
            grid=(2, 2),
            in_specs=[
                pl.BlockSpec(
                    (1, 4, 1, ROWS + TILE, WIDE),
                    lambda h, k, at: (h, 0, at[8] + k - 2 * at[8] * k, 0, 0),
                ),
                *[pl.BlockSpec(memory_space=pl.ANY)] * 4,
                pl.BlockSpec((3, 3, CH), lambda h, k, at: (0, 0, 0)),
            ],
            out_specs=[
                pl.BlockSpec((3, 1, ROWS, CH), lambda h, k, at: (0, h, 0, 0)),
                pl.BlockSpec((1, HALO, CH), lambda h, k, at: (h, 0, 0)),
                pl.BlockSpec((1, HALO, CH), lambda h, k, at: (h, 0, 0)),
                pl.BlockSpec((HALO, CH), lambda h, k, at: (0, 0)),
                pl.BlockSpec(memory_space=pl.ANY),
            ],
            scratch_shapes=[
                pltpu.VMEM((2, 4 * WIDE, 3 * CH), BF16),
                pltpu.VMEM((ROWS + TILE, 3 * CH), F32),
                pltpu.VMEM((8, WIDE), F32),
                pltpu.VMEM((3, SHARE + TILE, CH), F32),
                pltpu.SemaphoreType.DMA((2, 4, 4, 3)),
                pltpu.SemaphoreType.DMA((2, 4, 4, 2)),
            ],
        ),
        out_shape=[
            jax.ShapeDtypeStruct((3, 2, ROWS, CH), BF16),
            jax.ShapeDtypeStruct((2, HALO, CH), BF16),
            jax.ShapeDtypeStruct((2, HALO, CH), BF16),
            jax.ShapeDtypeStruct((HALO, CH), BF16),
            jax.ShapeDtypeStruct((4, 2 * CH, WIDE), BF16),
        ],
        compiler_params=pltpu.CompilerParams(vmem_limit_bytes=46 * MIB),
        cost_estimate=pl.CostEstimate(
            flops=2 * 2 * ROWS * 4096 * 3 * CH, bytes_accessed=18_000_000, transcendentals=0
        ),
        name="project",
    )(at, gathered, *weights, taps)


def toeplitz_kernel(u_ref, out_ref):
    for g in range(GROUPS):
        wide = jnp.broadcast_to(u_ref[g : g + 1], (LH, 3 * LH))
        skewed = pltpu.roll(wide, 0, 1, stride=1, stride_axis=0)
        out_ref[g] = skewed[:, : 2 * LH].astype(BF16)


def toeplitz(filters):
    backwards = jnp.flip(filters.astype(F32), 1)
    row = jnp.pad(backwards, ((0, 0), (1, 2 * LH - 1)))
    return pl.pallas_call(
        toeplitz_kernel,
        out_shape=jax.ShapeDtypeStruct((GROUPS, LH, 2 * LH), BF16),
        compiler_params=pltpu.CompilerParams(vmem_limit_bytes=8 * MIB),
        name="toeplitz",
    )(row)


def mix_kernel(proj_ref, halo_ref, band_ref, taps_ref, bias_ref, out_ref, before, edge):
    step = pl.program_id(0)

    @pl.when(step == 0)
    def _():
        for h in range(2):
            before[h] = halo_ref[h, :LH]
            last = halo_ref[h, LH:].astype(F32)
            for s in range(3):
                edge[h, s] = pltpu.roll(last, (6 - 2 * s) % 16, 0)[:8]

    queries = []
    mixes = []
    windows = []
    for h in range(2):
        feats = []
        for s in range(3):
            lifted = proj_ref[s, h].astype(F32)
            rows = jnp.concatenate([edge[h, s], lifted], axis=0)
            feats.append(three_taps(rows, taps_ref, s)[8:])
            edge[h, s] = lifted[LH - 8 :]
        mixing = (feats[1] * feats[2]).astype(BF16)
        queries.append(feats[0])
        mixes.append(mixing)
        windows.append(jnp.concatenate([before[h], mixing], axis=0))
        before[h] = mixing
    lane_group = lax.broadcasted_iota(jnp.int32, (LH, 2 * LH), 1) % LH // GSIZE
    halves = []
    for half in range(2):
        lanes = slice(half * LH, (half + 1) * LH)
        window = jnp.concatenate([windows[0][:, lanes], windows[1][:, lanes]], axis=1)
        total = jnp.zeros((LH, 2 * LH), F32)
        for g in range(GROUPS // 2):
            one = jnp.dot(band_ref[half * 8 + g], window, preferred_element_type=F32)
            total = jnp.where(lane_group == g, one, total)
        halves.append(total)
    for h in range(2):
        rows = slice(h * LH, (h + 1) * LH)
        filtered = jnp.concatenate([halves[0][:, rows], halves[1][:, rows]], axis=1)
        value = queries[h] * (filtered + bias_ref[...] * mixes[h].astype(F32))
        out_ref[h] = value.astype(BF16)


def mix(proj, halo, band, taps, bias, first, count):
    return pl.pallas_call(
        mix_kernel,
        grid=(count,),
        in_specs=[
            pl.BlockSpec((3, 2, LH, CH), lambda b: (0, 0, b + first, 0)),
            pl.BlockSpec((2, HALO, CH), lambda b: (0, 0, 0)),
            pl.BlockSpec((GROUPS, LH, 2 * LH), lambda b: (0, 0, 0)),
            pl.BlockSpec((3, 3, CH), lambda b: (0, 0, 0)),
            pl.BlockSpec((1, CH), lambda b: (0, 0)),
        ],
        out_specs=pl.BlockSpec((2, LH, CH), lambda b: (0, b, 0)),
        out_shape=jax.ShapeDtypeStruct((2, count * LH, CH), BF16),
        scratch_shapes=[
            pltpu.VMEM((2, LH, CH), BF16),
            pltpu.VMEM((2, 3, 8, CH), F32),
        ],
        compiler_params=pltpu.CompilerParams(vmem_limit_bytes=16 * MIB),
        cost_estimate=pl.CostEstimate(
            flops=2 * 512 * CH * 2048, bytes_accessed=2_000_000, transcendentals=0
        ),
        name="mix",
    )(proj, halo, band, taps, bias)


def out_kernel(at_ref, mine_ref, other_ref, w_ref, out_ref, rows):

    @pl.when(pl.program_id(0) == 0)
    def _():
        swap = at_ref[9] == 1
        for h in range(2):
            place = slice(h * HALF, (h + 1) * HALF)
            rows[place, :CH] = jnp.where(swap, other_ref[h], mine_ref[h])
            rows[place, CH:] = jnp.where(swap, mine_ref[h], other_ref[h])

    products = jnp.dot(rows[...], w_ref[0], preferred_element_type=F32).astype(BF16)
    for h in range(2):
        out_ref[h, 0] = products[h * HALF : (h + 1) * HALF]


def project_out(at, mine, other, weights):
    return pl.pallas_call(
        out_kernel,
        grid_spec=pltpu.PrefetchScalarGridSpec(
            num_scalar_prefetch=1,
            grid=(4,),
            in_specs=[
                *[pl.BlockSpec((2, HALF, CH), lambda k, at: (0, 0, 0))] * 2,
                pl.BlockSpec((1, 2 * CH, WIDE), lambda k, at: (k, 0, 0)),
            ],
            out_specs=pl.BlockSpec((2, 1, HALF, WIDE), lambda k, at: (0, k, 0, 0)),
            scratch_shapes=[pltpu.VMEM((2 * HALF, 2 * CH), BF16)],
        ),
        out_shape=jax.ShapeDtypeStruct((2, 4, HALF, WIDE), BF16),
        compiler_params=pltpu.CompilerParams(vmem_limit_bytes=52 * MIB),
        cost_estimate=pl.CostEstimate(
            flops=2 * 512 * 2 * CH * 2048, bytes_accessed=5_000_000, transcendentals=0
        ),
        name="project_out",
    )(at, mine, other, weights)


FIRST, SECOND = (1, 3), (3, 1)


def pair_step(value, axis, masks):
    pairs = [(i * 2 + c, (i ^ masks[c]) * 2 + c) for i in range(4) for c in range(2)]
    return lax.ppermute(value, (axis, "c"), pairs)


def ring_pairs(piece, axis):
    here = jnp.stack([piece, pair_step(piece, axis, FIRST)])
    return here, pair_step(here, axis, SECOND)


def ring_scatter(partial, place):
    ring = ("zh", "zl")
    up = [(i, (i + 1) % 8) for i in range(8)]
    down = [(i, (i + 7) % 8) for i in range(8)]
    half = partial.shape[1] // 2

    def term(offset):
        return lax.dynamic_index_in_dim(partial, (place + offset) % 8, 0, keepdims=False)

    def plus(left, right):
        return (left.astype(F32) + right.astype(F32)).astype(BF16)

    far = term(4)
    rising = lax.ppermute(far[:half], ring, up)
    falling = lax.ppermute(far[half:], ring, down)
    above, below = term(3), term(-3)
    rising = jnp.concatenate([plus(above[:half], rising), above[half:]], axis=0)
    falling = jnp.concatenate([below[:half], plus(below[half:], falling)], axis=0)
    for offset in (2, 1):
        rising = plus(term(offset), lax.ppermute(rising, ring, up))
        falling = plus(term(-offset), lax.ppermute(falling, ring, down))
    return term(0), lax.ppermute(rising, ring, up), lax.ppermute(falling, ring, down)


def on_device(
    tokens, prior_rows, norm_gain, in_weight, short_filter, mr_filter, mr_bias, out_weight
):
    zh = lax.axis_index("zh")
    column = lax.axis_index("x")
    leading = (column == 0) & (lax.axis_index("y") == 0)

    core = lax.axis_index("c")
    turns = jnp.where(core == 0, jnp.array([0, 1, 3, 2]), jnp.array([0, 3, 1, 2]))
    at = jnp.concatenate(
        [lax.axis_index("y") ^ turns, column ^ turns, jnp.stack([zh, zh ^ core])]
    ).astype(jnp.int32)
    ring = ("zh", "zl", "c")
    padded = jnp.pad(prior_rows, ((0, 2 * SHARE - prior_rows.shape[0]), (0, 0)))
    some = lax.dynamic_slice_in_dim(padded, zh * SHARE, SHARE, 0)
    lifted, carried = tokens.astype(F32), some.astype(F32)
    gain = norm_gain.astype(F32)
    sums = jnp.sum(lifted * lifted, axis=1)
    more = jnp.pad(jnp.sum(carried * carried, axis=1), (0, WIDE - SHARE))
    sums = jnp.stack([sums, more])
    coarse = lax.reduce_precision(sums, 8, 7)
    terms = jnp.stack([coarse, sums - coarse], axis=1).reshape(4, WIDE).astype(BF16)
    own = jnp.concatenate(
        [
            (lifted * gain).astype(BF16),
            (carried * gain).astype(BF16),
            jnp.pad(terms, ((0, TILE - SHARE - 4), (0, 0))),
        ],
        axis=0,
    )

    left, right = in_weight[..., :CH], in_weight[..., CH:]
    kept = jnp.where(zh == 0, left, right)
    got = lax.ppermute(jnp.where(zh == 0, right, left), "zh", [(0, 1), (1, 0)])
    out_weight, own = lax.optimization_barrier((out_weight, own))
    pieces = []
    for k in range(2):
        chosen = lax.dynamic_slice_in_dim(out_weight, (core ^ k) * CH, CH, 0)
        pairs = [(a * 2 + b, (b ^ k) * 2 + a) for a in range(2) for b in range(2)]
        chosen = lax.ppermute(chosen, ("zh", "c"), pairs)
        pieces.append(jnp.concatenate([chosen[:128], chosen[128:]], axis=1)[None])
    own, got, pieces = lax.optimization_barrier((own, got, pieces))
    gathered = lax.all_gather(own, ring).reshape(2, 4, 2, ROWS + TILE, WIDE)
    kept = jnp.concatenate([kept, pieces[0]], axis=0)
    got = jnp.concatenate([got, pieces[1]], axis=0)
    weights = (
        *ring_pairs(jnp.concatenate(ring_pairs(kept, "x"), axis=0), "y"),
        *ring_pairs(jnp.concatenate(ring_pairs(got, "y"), axis=0), "x"),
    )
    weights, gathered = lax.optimization_barrier((weights, gathered))

    taps = lax.dynamic_slice_in_dim(short_filter, zh * CH, CH, 2)
    bias = lax.dynamic_slice_in_dim(mr_bias, zh * CH, CH, 0)[None, :]
    band = toeplitz(lax.dynamic_slice_in_dim(mr_filter, zh * GROUPS, GROUPS, 0))

    proj, tail, mid, front, w_out = project(at, gathered, weights, taps)

    last = column == 3
    to_first = jnp.where(last, tail[1], tail[0])
    to_second = jnp.where(last, tail[0], tail[1])
    first = lax.ppermute(to_first, ("y", "x"), [(i, i + 1) for i in range(15)])
    second = lax.ppermute(
        to_second, ("y", "x"), [(i, i // 4 * 4 + (i + 1) % 4) for i in range(16)]
    )
    def swapped(mine):
        return mine, lax.ppermute(mine, "c", [(0, 1), (1, 0)])

    late = project_out(at, *swapped(mix(proj, mid, band, taps, bias, 2, 2)), w_out)
    first, second, late = lax.optimization_barrier((first, second, late))
    halo = jnp.stack([jnp.where(leading, front, first), second])
    early = project_out(at, *swapped(mix(proj, halo, band, taps, bias, 0, 2)), w_out)
    terms = ring_scatter(late.reshape(8, HALF, WIDE), zh * 4 + lax.axis_index("zl"))
    late_sum = sum(term.astype(F32) for term in terms)
    early_sum = lax.psum_scatter(
        early.reshape(8, HALF, WIDE), ("zh", "zl"), scatter_dimension=0
    )
    summed = jnp.concatenate([early_sum.astype(F32), late_sum], axis=0)
    return (tokens.astype(F32) + summed).astype(BF16)


def solution(mesh):
    split = Mesh(mesh.devices.reshape(4, 2, 4, 4, 2), ("y", "zh", "x", "zl", "c"))
    seq, tensor = ("y", "zh", "x"), ("zl", "c")
    in_specs = (
        P(seq, tensor),
        P(None, tensor),
        P(tensor),
        P(None, seq, tensor),
        P(None, None, tensor),
        P(tensor, None),
        P(tensor),
        P(tensor, seq),
    )
    return jax.shard_map(
        on_device, mesh=split, in_specs=in_specs, out_specs=P(seq, tensor), check_vma=False
    )
```

```python
import jax
import jax.numpy as jnp
from jax import lax
from jax.experimental import pallas as pl
from jax.experimental.pallas import tpu as pltpu
from jax.sharding import Mesh, PartitionSpec as P

GSIZE = 16
LH = 128
ROWS = 512
TILE = 80
SHARE = 72
HALF = ROWS // 2
WIDE = 512
CH = 256
GROUPS = CH // GSIZE
HALO = LH + 16
MIB = 1024 * 1024
F32 = jnp.float32
BF16 = jnp.bfloat16


def row_iota(shape):
    return lax.broadcasted_iota(jnp.int32, shape, 0)


def three_taps(rows, taps, s):
    return (
        taps[0, s : s + 1] * rows
        + taps[1, s : s + 1] * pltpu.roll(rows, 1, 0)
        + taps[2, s : s + 1] * pltpu.roll(rows, 2, 0)
    )


def last_rows(parts, first, shift):
    place = row_iota((16, CH)) // 2
    out = jnp.zeros((16, CH), F32)
    for s in range(3):
        moved = pltpu.roll(parts[s][first : first + 16], (2 * s + shift) % 16, 0)
        out = jnp.where(place == s, moved, out)
    return out.astype(BF16)


def as_column(row):
    column = jnp.broadcast_to(row, (128, row.shape[1])).T
    return jnp.concatenate([column] * (CH // 128), axis=1)


def project_kernel(at_ref, x_ref, *refs):
    taps_ref, proj_ref, tail_ref, mid_ref, front_ref, out_w_ref = refs[4:10]
    wide, acc, stat, ahead, sems, out_sems = refs[10:]
    first_row, kind = pl.program_id(0) == 0, pl.program_id(1)
    turns = []
    out_copies = []
    for k in range(2):
        copies = []
        for i in range(4):
            for j in range(4):
                y, x = (i, j) if k == 0 else (j, i)
                start = at_ref[y] * WIDE + at_ref[4 + x] * 128
                rows = pl.ds(pl.multiple_of(start, 128), 128)
                source = refs[2 * k + i // 2].at[i % 2, j, :, pl.ds(0, 3 * CH)]
                copies.append(pltpu.make_async_copy(source, wide.at[k, rows], sems.at[k, i, j]))
                lanes = pl.ds(pl.multiple_of(at_ref[4 + x] * 128, 128), 128)
                for part in range(2):
                    source = refs[2 * k + i // 2].at[i % 2, j, :, pl.ds(3 * CH + part * 128, 128)]
                    place = out_w_ref.at[at_ref[y], pl.ds(k * CH + part * 128, 128), lanes]
                    sem = out_sems.at[k, i, j, part]
                    out_copies.append(pltpu.make_async_copy(source, place, sem))
        turns.append(copies)

    @pl.when(first_row & (kind == 0))
    def _():
        for copies in turns:
            for copy in copies:
                copy.start()

    for k in range(2):

        @pl.when(first_row & (kind == k))
        def _(k=k):
            for copy in turns[k]:
                copy.wait()

    @pl.when(first_row & (kind == 1))
    def _():
        for copy in out_copies:
            copy.start()

    features = jnp.concatenate([x_ref[0, y, 0] for y in range(4)], axis=1)
    products = jnp.dot(features, wide[kind], preferred_element_type=F32)
    sums = jnp.zeros((8, WIDE), F32)
    for y in range(4):
        sums += x_ref[0, y, 0, ROWS + TILE - 16 :].astype(F32)[8:]

    @pl.when(kind == 0)
    def _():
        acc[...] = products
        stat[...] = sums

    @pl.when(kind == 1)
    def _():
        total = stat[...] + sums
        own = lax.rsqrt((total[0:1] + total[1:2]) * (1.0 / 4096.0) + 1e-6)
        extra = lax.rsqrt((total[2:3] + total[3:4]) * (1.0 / 4096.0) + 1e-6)
        own, extra = as_column(own), as_column(extra[:, :128])[:TILE]
        for s in range(3):
            lanes = slice(s * CH, (s + 1) * CH)
            whole = acc[:, lanes] + products[:, lanes]
            proj_ref[s, 0] = (whole[:ROWS] * own).astype(BF16)
            carried = (whole[ROWS:] * extra).astype(BF16).astype(F32)

            @pl.when(first_row)
            def _(s=s, carried=carried):
                ahead[s, :SHARE] = carried[:SHARE]

            @pl.when(jnp.logical_not(first_row))
            def _(s=s, carried=carried):
                ahead[s, SHARE:] = carried

        for end, ref in ((ROWS, tail_ref), (HALF, mid_ref)):
            rows = [proj_ref[s, 0, end - HALO : end].astype(F32) for s in range(3)]
            mixing = three_taps(rows[1], taps_ref, 1) * three_taps(rows[2], taps_ref, 2)
            ref[0, :LH] = mixing[HALO - LH :].astype(BF16)
            ref[0, LH:] = last_rows(rows, HALO - 16, 2)

    @pl.when((pl.program_id(0) == 1) & (kind == 1))
    def _():
        mixing = three_taps(ahead[1], taps_ref, 1) * three_taps(ahead[2], taps_ref, 2)
        front_ref[:LH] = pltpu.roll(mixing, SHARE + TILE - 1, 0)[:LH].astype(BF16)
        front_ref[LH:] = last_rows(ahead, LH - 8, -7)
        for copy in out_copies:
            copy.wait()


def project(at, gathered, weights, taps):
    return pl.pallas_call(
        project_kernel,
        grid_spec=pltpu.PrefetchScalarGridSpec(
            num_scalar_prefetch=1,
            grid=(2, 2),
            in_specs=[
                pl.BlockSpec(
                    (1, 4, 1, ROWS + TILE, WIDE),
                    lambda h, k, at: (h, 0, at[8] + k - 2 * at[8] * k, 0, 0),
                ),
                *[pl.BlockSpec(memory_space=pl.ANY)] * 4,
                pl.BlockSpec((3, 3, CH), lambda h, k, at: (0, 0, 0)),
            ],
            out_specs=[
                pl.BlockSpec((3, 1, ROWS, CH), lambda h, k, at: (0, h, 0, 0)),
                pl.BlockSpec((1, HALO, CH), lambda h, k, at: (h, 0, 0)),
                pl.BlockSpec((1, HALO, CH), lambda h, k, at: (h, 0, 0)),
                pl.BlockSpec((HALO, CH), lambda h, k, at: (0, 0)),
                pl.BlockSpec(memory_space=pltpu.HBM),
            ],
            scratch_shapes=[
                pltpu.VMEM((2, 4 * WIDE, 3 * CH), BF16),
                pltpu.VMEM((ROWS + TILE, 3 * CH), F32),
                pltpu.VMEM((8, WIDE), F32),
                pltpu.VMEM((3, SHARE + TILE, CH), F32),
                pltpu.SemaphoreType.DMA((2, 4, 4)),
                pltpu.SemaphoreType.DMA((2, 4, 4, 2)),
            ],
        ),
        out_shape=[
            jax.ShapeDtypeStruct((3, 2, ROWS, CH), BF16),
            jax.ShapeDtypeStruct((2, HALO, CH), BF16),
            jax.ShapeDtypeStruct((2, HALO, CH), BF16),
            jax.ShapeDtypeStruct((HALO, CH), BF16),
            jax.ShapeDtypeStruct((4, 2 * CH, WIDE), BF16),
        ],
        compiler_params=pltpu.CompilerParams(vmem_limit_bytes=42 * MIB),
        cost_estimate=pl.CostEstimate(
            flops=2 * 2 * ROWS * 4096 * 3 * CH, bytes_accessed=18_000_000, transcendentals=0
        ),
        name="project",
    )(at, gathered, *weights, taps)


def toeplitz_kernel(u_ref, out_ref):
    for g in range(GROUPS):
        wide = jnp.broadcast_to(u_ref[g : g + 1], (LH, 3 * LH))
        skewed = pltpu.roll(wide, 0, 1, stride=1, stride_axis=0)
        out_ref[g] = skewed[:, : 2 * LH].astype(BF16)


def toeplitz(filters):
    backwards = jnp.flip(filters.astype(F32), 1)
    row = jnp.pad(backwards, ((0, 0), (1, 2 * LH - 1)))
    return pl.pallas_call(
        toeplitz_kernel,
        out_shape=jax.ShapeDtypeStruct((GROUPS, LH, 2 * LH), BF16),
        compiler_params=pltpu.CompilerParams(vmem_limit_bytes=8 * MIB),
        name="toeplitz",
    )(row)


def mix_kernel(proj_ref, halo_ref, band_ref, taps_ref, bias_ref, out_ref, before, edge):
    step = pl.program_id(0)

    @pl.when(step == 0)
    def _():
        for h in range(2):
            before[h] = halo_ref[h, :LH]
            last = halo_ref[h, LH:].astype(F32)
            for s in range(3):
                edge[h, s] = pltpu.roll(last, (6 - 2 * s) % 16, 0)[:8]

    queries = []
    mixes = []
    windows = []
    for h in range(2):
        feats = []
        for s in range(3):
            lifted = proj_ref[s, h].astype(F32)
            rows = jnp.concatenate([edge[h, s], lifted], axis=0)
            feats.append(three_taps(rows, taps_ref, s)[8:])
            edge[h, s] = lifted[LH - 8 :]
        mixing = (feats[1] * feats[2]).astype(BF16)
        queries.append(feats[0])
        mixes.append(mixing)
        windows.append(jnp.concatenate([before[h], mixing], axis=0))
        before[h] = mixing
    lane_group = lax.broadcasted_iota(jnp.int32, (LH, 2 * LH), 1) % LH // GSIZE
    halves = []
    for half in range(2):
        lanes = slice(half * LH, (half + 1) * LH)
        window = jnp.concatenate([windows[0][:, lanes], windows[1][:, lanes]], axis=1)
        total = jnp.zeros((LH, 2 * LH), F32)
        for g in range(GROUPS // 2):
            one = jnp.dot(band_ref[half * 8 + g], window, preferred_element_type=F32)
            total = jnp.where(lane_group == g, one, total)
        halves.append(total)
    for h in range(2):
        rows = slice(h * LH, (h + 1) * LH)
        filtered = jnp.concatenate([halves[0][:, rows], halves[1][:, rows]], axis=1)
        value = queries[h] * (filtered + bias_ref[...] * mixes[h].astype(F32))
        out_ref[h] = value.astype(BF16)


def mix(proj, halo, band, taps, bias, first, count):
    return pl.pallas_call(
        mix_kernel,
        grid=(count,),
        in_specs=[
            pl.BlockSpec((3, 2, LH, CH), lambda b: (0, 0, b + first, 0)),
            pl.BlockSpec((2, HALO, CH), lambda b: (0, 0, 0)),
            pl.BlockSpec((GROUPS, LH, 2 * LH), lambda b: (0, 0, 0)),
            pl.BlockSpec((3, 3, CH), lambda b: (0, 0, 0)),
            pl.BlockSpec((1, CH), lambda b: (0, 0)),
        ],
        out_specs=pl.BlockSpec((2, LH, CH), lambda b: (0, b, 0)),
        out_shape=jax.ShapeDtypeStruct((2, count * LH, CH), BF16),
        scratch_shapes=[
            pltpu.VMEM((2, LH, CH), BF16),
            pltpu.VMEM((2, 3, 8, CH), F32),
        ],
        compiler_params=pltpu.CompilerParams(vmem_limit_bytes=16 * MIB),
        cost_estimate=pl.CostEstimate(
            flops=2 * 512 * CH * 2048, bytes_accessed=2_000_000, transcendentals=0
        ),
        name="mix",
    )(proj, halo, band, taps, bias)


def out_kernel(at_ref, mine_ref, other_ref, w_ref, *refs):
    out_ref, rows = refs[-2:]

    @pl.when(pl.program_id(0) == 0)
    def _():
        swap = at_ref[9] == 1
        for h in range(2):
            place = slice(h * HALF, (h + 1) * HALF)
            rows[place, :CH] = jnp.where(swap, other_ref[h], mine_ref[h])
            rows[place, CH:] = jnp.where(swap, mine_ref[h], other_ref[h])

    products = jnp.dot(rows[...], w_ref[0], preferred_element_type=F32).astype(BF16)
    for h in range(2):
        out_ref[h, 0] = products[h * HALF : (h + 1) * HALF]


def project_out(at, mine, other, weights, half, base=None):
    more = () if base is None else (base,)
    return pl.pallas_call(
        out_kernel,
        grid_spec=pltpu.PrefetchScalarGridSpec(
            num_scalar_prefetch=1,
            grid=(4,),
            in_specs=[
                *[pl.BlockSpec((2, HALF, CH), lambda k, at: (0, 0, 0))] * 2,
                pl.BlockSpec((1, 2 * CH, WIDE), lambda k, at: (k, 0, 0)),
                *[pl.BlockSpec(memory_space=pl.ANY)] * len(more),
            ],
            out_specs=pl.BlockSpec((2, 1, HALF, WIDE), lambda k, at: (0, k, half, 0)),
            scratch_shapes=[pltpu.VMEM((2 * HALF, 2 * CH), BF16)],
        ),
        out_shape=jax.ShapeDtypeStruct((2, 4, ROWS, WIDE), BF16),
        input_output_aliases={} if base is None else {4: 0},
        compiler_params=pltpu.CompilerParams(vmem_limit_bytes=50 * MIB),
        cost_estimate=pl.CostEstimate(
            flops=2 * 512 * 2 * CH * 2048, bytes_accessed=5_000_000, transcendentals=0
        ),
        name="project_out",
    )(at, mine, other, weights, *more)


FIRST, SECOND = (1, 3), (3, 1)


def pair_step(value, axis, masks):
    pairs = [(i * 2 + c, (i ^ masks[c]) * 2 + c) for i in range(4) for c in range(2)]
    return lax.ppermute(value, (axis, "c"), pairs)


def ring_pairs(piece, axis):
    here = jnp.stack([piece, pair_step(piece, axis, FIRST)])
    return here, pair_step(here, axis, SECOND)


def on_device(
    tokens, prior_rows, norm_gain, in_weight, short_filter, mr_filter, mr_bias, out_weight
):
    zh = lax.axis_index("zh")
    column = lax.axis_index("x")
    leading = (column == 0) & (lax.axis_index("y") == 0)

    core = lax.axis_index("c")
    turns = jnp.where(core == 0, jnp.array([0, 1, 3, 2]), jnp.array([0, 3, 1, 2]))
    at = jnp.concatenate(
        [lax.axis_index("y") ^ turns, column ^ turns, jnp.stack([zh, zh ^ core])]
    ).astype(jnp.int32)
    ring = ("zh", "zl", "c")
    padded = jnp.pad(prior_rows, ((0, 2 * SHARE - prior_rows.shape[0]), (0, 0)))
    some = lax.dynamic_slice_in_dim(padded, zh * SHARE, SHARE, 0)
    lifted, carried = tokens.astype(F32), some.astype(F32)
    gain = norm_gain.astype(F32)
    sums = jnp.sum(lifted * lifted, axis=1)
    more = jnp.pad(jnp.sum(carried * carried, axis=1), (0, WIDE - SHARE))
    sums = jnp.stack([sums, more])
    coarse = lax.reduce_precision(sums, 8, 7)
    terms = jnp.stack([coarse, sums - coarse], axis=1).reshape(4, WIDE).astype(BF16)
    own = jnp.concatenate(
        [
            (lifted * gain).astype(BF16),
            (carried * gain).astype(BF16),
            jnp.pad(terms, ((0, TILE - SHARE - 4), (0, 0))),
        ],
        axis=0,
    )

    left, right = (
        jnp.concatenate([in_weight[s, :, part * CH : (part + 1) * CH] for s in range(3)], axis=1)
        for part in range(2)
    )
    kept = jnp.where(zh == 0, left, right)
    got = lax.ppermute(jnp.where(zh == 0, right, left), "zh", [(0, 1), (1, 0)])
    pieces = []
    for k in range(2):
        chosen = lax.dynamic_slice_in_dim(out_weight, (core ^ k) * CH, CH, 0)
        pairs = [(a * 2 + b, (b ^ k) * 2 + a) for a in range(2) for b in range(2)]
        chosen = lax.ppermute(chosen, ("zh", "c"), pairs)
        pieces.append(jnp.concatenate([chosen[:128], chosen[128:]], axis=1))
    own, got, pieces = lax.optimization_barrier((own, got, pieces))
    gathered = lax.all_gather(own, ring).reshape(2, 4, 2, ROWS + TILE, WIDE)
    kept = jnp.concatenate([kept, pieces[0]], axis=1)
    got = jnp.concatenate([got, pieces[1]], axis=1)
    weights = (
        *ring_pairs(jnp.concatenate(ring_pairs(kept, "x"), axis=0), "y"),
        *ring_pairs(jnp.concatenate(ring_pairs(got, "y"), axis=0), "x"),
    )
    weights, gathered = lax.optimization_barrier((weights, gathered))

    taps = lax.dynamic_slice_in_dim(short_filter, zh * CH, CH, 2)
    bias = lax.dynamic_slice_in_dim(mr_bias, zh * CH, CH, 0)[None, :]
    band = toeplitz(lax.dynamic_slice_in_dim(mr_filter, zh * GROUPS, GROUPS, 0))

    proj, tail, mid, front, w_out = project(at, gathered, weights, taps)

    last = column == 3
    to_first = jnp.where(last, tail[1], tail[0])
    to_second = jnp.where(last, tail[0], tail[1])
    first = lax.ppermute(to_first, ("y", "x"), [(i, i + 1) for i in range(15)])
    second = lax.ppermute(
        to_second, ("y", "x"), [(i, i // 4 * 4 + (i + 1) % 4) for i in range(16)]
    )
    def swapped(mine):
        return mine, lax.ppermute(mine, "c", [(0, 1), (1, 0)])

    partial = project_out(at, *swapped(mix(proj, mid, band, taps, bias, 2, 2)), w_out, 1)
    first, second, partial = lax.optimization_barrier((first, second, partial))
    halo = jnp.stack([jnp.where(leading, front, first), second])
    partial = project_out(
        at, *swapped(mix(proj, halo, band, taps, bias, 0, 2)), w_out, 0, partial
    )
    summed = lax.psum_scatter(
        partial.reshape(8, ROWS, WIDE), ("zh", "zl"), scatter_dimension=0
    )
    return (tokens.astype(F32) + summed.astype(F32)).astype(BF16)


def solution(mesh):
    split = Mesh(mesh.devices.reshape(4, 2, 4, 4, 2), ("y", "zh", "x", "zl", "c"))
    seq, tensor = ("y", "zh", "x"), ("zl", "c")
    in_specs = (
        P(seq, tensor),
        P(None, tensor),
        P(tensor),
        P(None, seq, tensor),
        P(None, None, tensor),
        P(tensor, None),
        P(tensor),
        P(tensor, seq),
    )
    return jax.shard_map(
        on_device, mesh=split, in_specs=in_specs, out_specs=P(seq, tensor), check_vma=False
    )
```

```python
import jax
import jax.numpy as jnp
from jax import lax
from jax.experimental import pallas as pl
from jax.experimental.pallas import tpu as pltpu
from jax.sharding import Mesh, PartitionSpec as P

GSIZE = 16
LH = 128
ROWS = 512
TILE = 80
SHARE = 72
HALF = ROWS // 2
WIDE = 512
CH = 256
GROUPS = CH // GSIZE
HALO = LH + 16
MIB = 1024 * 1024
F32 = jnp.float32
BF16 = jnp.bfloat16


def row_iota(shape):
    return lax.broadcasted_iota(jnp.int32, shape, 0)


def three_taps(rows, taps, s):
    return (
        taps[0, s : s + 1] * rows
        + taps[1, s : s + 1] * pltpu.roll(rows, 1, 0)
        + taps[2, s : s + 1] * pltpu.roll(rows, 2, 0)
    )


def last_rows(parts, first, shift):
    place = row_iota((16, CH)) // 2
    out = jnp.zeros((16, CH), F32)
    for s in range(3):
        moved = pltpu.roll(parts[s][first : first + 16], (2 * s + shift) % 16, 0)
        out = jnp.where(place == s, moved, out)
    return out.astype(BF16)


def as_column(row):
    column = jnp.broadcast_to(row, (128, row.shape[1])).T
    return jnp.concatenate([column] * (CH // 128), axis=1)


def project_kernel(at_ref, x_ref, *refs):
    taps_ref, proj_ref, tail_ref, mid_ref, front_ref, out_w_ref = refs[4:10]
    wide, acc, stat, ahead, sems, out_sems = refs[10:]
    first_row, kind = pl.program_id(0) == 0, pl.program_id(1)
    turns = []
    out_copies = []
    for k in range(2):
        copies = []
        for i in range(4):
            for j in range(4):
                y, x = (i, j) if k == 0 else (j, i)
                start = at_ref[y] * WIDE + at_ref[4 + x] * 128
                rows = pl.ds(pl.multiple_of(start, 128), 128)
                source = refs[2 * k + i // 2].at[i % 2, j, :, pl.ds(0, 3 * CH)]
                copies.append(pltpu.make_async_copy(source, wide.at[k, rows], sems.at[k, i, j]))
                lanes = pl.ds(pl.multiple_of(at_ref[4 + x] * 128, 128), 128)
                for part in range(2):
                    source = refs[2 * k + i // 2].at[i % 2, j, :, pl.ds(3 * CH + part * 128, 128)]
                    place = out_w_ref.at[at_ref[y], pl.ds(k * CH + part * 128, 128), lanes]
                    sem = out_sems.at[k, i, j, part]
                    out_copies.append(pltpu.make_async_copy(source, place, sem))
        turns.append(copies)

    @pl.when(first_row & (kind == 0))
    def _():
        for copies in turns:
            for copy in copies:
                copy.start()

    for k in range(2):

        @pl.when(first_row & (kind == k))
        def _(k=k):
            for copy in turns[k]:
                copy.wait()

    @pl.when(first_row & (kind == 1))
    def _():
        for copy in out_copies:
            copy.start()

    features = jnp.concatenate([x_ref[0, y, 0] for y in range(4)], axis=1)
    products = jnp.dot(features, wide[kind], preferred_element_type=F32)
    sums = jnp.zeros((8, WIDE), F32)
    for y in range(4):
        sums += x_ref[0, y, 0, ROWS + TILE - 16 :].astype(F32)[8:]

    @pl.when(kind == 0)
    def _():
        acc[...] = products
        stat[...] = sums

    @pl.when(kind == 1)
    def _():
        total = stat[...] + sums
        own = lax.rsqrt((total[0:1] + total[1:2]) * (1.0 / 4096.0) + 1e-6)
        extra = lax.rsqrt((total[2:3] + total[3:4]) * (1.0 / 4096.0) + 1e-6)
        own, extra = as_column(own), as_column(extra[:, :128])[:TILE]
        for s in range(3):
            lanes = slice(s * CH, (s + 1) * CH)
            whole = acc[:, lanes] + products[:, lanes]
            proj_ref[s, 0] = (whole[:ROWS] * own).astype(BF16)
            carried = (whole[ROWS:] * extra).astype(BF16).astype(F32)

            @pl.when(first_row)
            def _(s=s, carried=carried):
                ahead[s, :SHARE] = carried[:SHARE]

            @pl.when(jnp.logical_not(first_row))
            def _(s=s, carried=carried):
                ahead[s, SHARE:] = carried

        for end, ref in ((ROWS, tail_ref), (HALF, mid_ref)):
            rows = [proj_ref[s, 0, end - HALO : end].astype(F32) for s in range(3)]
            mixing = three_taps(rows[1], taps_ref, 1) * three_taps(rows[2], taps_ref, 2)
            ref[0, :LH] = mixing[HALO - LH :].astype(BF16)
            ref[0, LH:] = last_rows(rows, HALO - 16, 2)

    @pl.when((pl.program_id(0) == 1) & (kind == 1))
    def _():
        mixing = three_taps(ahead[1], taps_ref, 1) * three_taps(ahead[2], taps_ref, 2)
        front_ref[:LH] = pltpu.roll(mixing, SHARE + TILE - 1, 0)[:LH].astype(BF16)
        front_ref[LH:] = last_rows(ahead, LH - 8, -7)
        for copy in out_copies:
            copy.wait()


def project(at, gathered, weights, taps):
    return pl.pallas_call(
        project_kernel,
        grid_spec=pltpu.PrefetchScalarGridSpec(
            num_scalar_prefetch=1,
            grid=(2, 2),
            in_specs=[
                pl.BlockSpec(
                    (1, 4, 1, ROWS + TILE, WIDE),
                    lambda h, k, at: (h, 0, at[8] + k - 2 * at[8] * k, 0, 0),
                ),
                *[pl.BlockSpec(memory_space=pl.ANY)] * 4,
                pl.BlockSpec((3, 3, CH), lambda h, k, at: (0, 0, 0)),
            ],
            out_specs=[
                pl.BlockSpec((3, 1, ROWS, CH), lambda h, k, at: (0, h, 0, 0)),
                pl.BlockSpec((1, HALO, CH), lambda h, k, at: (h, 0, 0)),
                pl.BlockSpec((1, HALO, CH), lambda h, k, at: (h, 0, 0)),
                pl.BlockSpec((HALO, CH), lambda h, k, at: (0, 0)),
                pl.BlockSpec(memory_space=pltpu.HBM),
            ],
            scratch_shapes=[
                pltpu.VMEM((2, 4 * WIDE, 3 * CH), BF16),
                pltpu.VMEM((ROWS + TILE, 3 * CH), F32),
                pltpu.VMEM((8, WIDE), F32),
                pltpu.VMEM((3, SHARE + TILE, CH), F32),
                pltpu.SemaphoreType.DMA((2, 4, 4)),
                pltpu.SemaphoreType.DMA((2, 4, 4, 2)),
            ],
        ),
        out_shape=[
            jax.ShapeDtypeStruct((3, 2, ROWS, CH), BF16),
            jax.ShapeDtypeStruct((2, HALO, CH), BF16),
            jax.ShapeDtypeStruct((2, HALO, CH), BF16),
            jax.ShapeDtypeStruct((HALO, CH), BF16),
            jax.ShapeDtypeStruct((4, 2 * CH, WIDE), BF16),
        ],
        compiler_params=pltpu.CompilerParams(vmem_limit_bytes=50 * MIB),
        cost_estimate=pl.CostEstimate(
            flops=2 * 2 * ROWS * 4096 * 3 * CH, bytes_accessed=18_000_000, transcendentals=0
        ),
        name="project",
    )(at, gathered, *weights, taps)


def toeplitz_kernel(u_ref, out_ref):
    for g in range(GROUPS):
        wide = jnp.broadcast_to(u_ref[g : g + 1], (LH, 3 * LH))
        skewed = pltpu.roll(wide, 0, 1, stride=1, stride_axis=0)
        out_ref[g] = skewed[:, : 2 * LH].astype(BF16)


def toeplitz(filters):
    backwards = jnp.flip(filters.astype(F32), 1)
    row = jnp.pad(backwards, ((0, 0), (1, 2 * LH - 1)))
    return pl.pallas_call(
        toeplitz_kernel,
        out_shape=jax.ShapeDtypeStruct((GROUPS, LH, 2 * LH), BF16),
        compiler_params=pltpu.CompilerParams(vmem_limit_bytes=8 * MIB),
        name="toeplitz",
    )(row)


def mix_kernel(proj_ref, halo_ref, band_ref, taps_ref, bias_ref, out_ref, before, edge):
    step = pl.program_id(0)

    @pl.when(step == 0)
    def _():
        for h in range(2):
            before[h] = halo_ref[h, :LH]
            last = halo_ref[h, LH:].astype(F32)
            for s in range(3):
                edge[h, s] = pltpu.roll(last, (6 - 2 * s) % 16, 0)[:8]

    queries = []
    mixes = []
    windows = []
    for h in range(2):
        feats = []
        for s in range(3):
            lifted = proj_ref[s, h].astype(F32)
            rows = jnp.concatenate([edge[h, s], lifted], axis=0)
            feats.append(three_taps(rows, taps_ref, s)[8:])
            edge[h, s] = lifted[LH - 8 :]
        mixing = (feats[1] * feats[2]).astype(BF16)
        queries.append(feats[0])
        mixes.append(mixing)
        windows.append(jnp.concatenate([before[h], mixing], axis=0))
        before[h] = mixing
    lane_group = lax.broadcasted_iota(jnp.int32, (LH, 2 * LH), 1) % LH // GSIZE
    halves = []
    for half in range(2):
        lanes = slice(half * LH, (half + 1) * LH)
        window = jnp.concatenate([windows[0][:, lanes], windows[1][:, lanes]], axis=1)
        total = jnp.zeros((LH, 2 * LH), F32)
        for g in range(GROUPS // 2):
            one = jnp.dot(band_ref[half * 8 + g], window, preferred_element_type=F32)
            total = jnp.where(lane_group == g, one, total)
        halves.append(total)
    for h in range(2):
        rows = slice(h * LH, (h + 1) * LH)
        filtered = jnp.concatenate([halves[0][:, rows], halves[1][:, rows]], axis=1)
        value = queries[h] * (filtered + bias_ref[...] * mixes[h].astype(F32))
        out_ref[h] = value.astype(BF16)


def mix(proj, halo, band, taps, bias, first, count):
    return pl.pallas_call(
        mix_kernel,
        grid=(count,),
        in_specs=[
            pl.BlockSpec((3, 2, LH, CH), lambda b: (0, 0, b + first, 0)),
            pl.BlockSpec((2, HALO, CH), lambda b: (0, 0, 0)),
            pl.BlockSpec((GROUPS, LH, 2 * LH), lambda b: (0, 0, 0)),
            pl.BlockSpec((3, 3, CH), lambda b: (0, 0, 0)),
            pl.BlockSpec((1, CH), lambda b: (0, 0)),
        ],
        out_specs=pl.BlockSpec((2, LH, CH), lambda b: (0, b, 0)),
        out_shape=jax.ShapeDtypeStruct((2, count * LH, CH), BF16),
        scratch_shapes=[
            pltpu.VMEM((2, LH, CH), BF16),
            pltpu.VMEM((2, 3, 8, CH), F32),
        ],
        compiler_params=pltpu.CompilerParams(vmem_limit_bytes=16 * MIB),
        cost_estimate=pl.CostEstimate(
            flops=2 * 512 * CH * 2048, bytes_accessed=2_000_000, transcendentals=0
        ),
        name="mix",
    )(proj, halo, band, taps, bias)


def out_kernel(at_ref, mine_ref, other_ref, w_ref, *refs):
    out_ref, rows = refs[-2:]

    @pl.when(pl.program_id(0) == 0)
    def _():
        swap = at_ref[9] == 1
        for h in range(2):
            place = slice(h * HALF, (h + 1) * HALF)
            rows[place, :CH] = jnp.where(swap, other_ref[h], mine_ref[h])
            rows[place, CH:] = jnp.where(swap, mine_ref[h], other_ref[h])

    products = jnp.dot(rows[...], w_ref[0], preferred_element_type=F32).astype(BF16)
    for h in range(2):
        out_ref[h, 0] = products[h * HALF : (h + 1) * HALF]


def project_out(at, mine, other, weights, half, base=None):
    more = () if base is None else (base,)
    return pl.pallas_call(
        out_kernel,
        grid_spec=pltpu.PrefetchScalarGridSpec(
            num_scalar_prefetch=1,
            grid=(4,),
            in_specs=[
                *[pl.BlockSpec((2, HALF, CH), lambda k, at: (0, 0, 0))] * 2,
                pl.BlockSpec((1, 2 * CH, WIDE), lambda k, at: (k, 0, 0)),
                *[pl.BlockSpec(memory_space=pl.ANY)] * len(more),
            ],
            out_specs=pl.BlockSpec((2, 1, HALF, WIDE), lambda k, at: (0, k, half, 0)),
            scratch_shapes=[pltpu.VMEM((2 * HALF, 2 * CH), BF16)],
        ),
        out_shape=jax.ShapeDtypeStruct((2, 4, ROWS, WIDE), BF16),
        input_output_aliases={} if base is None else {4: 0},
        compiler_params=pltpu.CompilerParams(vmem_limit_bytes=44 * MIB),
        cost_estimate=pl.CostEstimate(
            flops=2 * 512 * 2 * CH * 2048, bytes_accessed=5_000_000, transcendentals=0
        ),
        name="project_out",
    )(at, mine, other, weights, *more)


FIRST, SECOND = (1, 3), (3, 1)


def pair_step(value, axis, masks):
    pairs = [(i * 2 + c, (i ^ masks[c]) * 2 + c) for i in range(4) for c in range(2)]
    return lax.ppermute(value, (axis, "c"), pairs)


def ring_pairs(piece, axis):
    here = jnp.stack([piece, pair_step(piece, axis, FIRST)])
    return here, pair_step(here, axis, SECOND)


def on_device(
    tokens, prior_rows, norm_gain, in_weight, short_filter, mr_filter, mr_bias, out_weight
):
    zh = lax.axis_index("zh")
    column = lax.axis_index("x")
    leading = (column == 0) & (lax.axis_index("y") == 0)

    core = lax.axis_index("c")
    turns = jnp.where(core == 0, jnp.array([0, 1, 3, 2]), jnp.array([0, 3, 1, 2]))
    at = jnp.concatenate(
        [lax.axis_index("y") ^ turns, column ^ turns, jnp.stack([zh, zh ^ core])]
    ).astype(jnp.int32)
    ring = ("zh", "zl", "c")
    padded = jnp.pad(prior_rows, ((0, 2 * SHARE - prior_rows.shape[0]), (0, 0)))
    some = lax.dynamic_slice_in_dim(padded, zh * SHARE, SHARE, 0)
    lifted, carried = tokens.astype(F32), some.astype(F32)
    gain = norm_gain.astype(F32)
    sums = jnp.sum(lifted * lifted, axis=1)
    more = jnp.pad(jnp.sum(carried * carried, axis=1), (0, WIDE - SHARE))
    sums = jnp.stack([sums, more])
    coarse = lax.reduce_precision(sums, 8, 7)
    terms = jnp.stack([coarse, sums - coarse], axis=1).reshape(4, WIDE).astype(BF16)
    own = jnp.concatenate(
        [
            (lifted * gain).astype(BF16),
            (carried * gain).astype(BF16),
            jnp.pad(terms, ((0, TILE - SHARE - 4), (0, 0))),
        ],
        axis=0,
    )

    left, right = (
        jnp.concatenate([in_weight[s, :, part * CH : (part + 1) * CH] for s in range(3)], axis=1)
        for part in range(2)
    )
    kept = jnp.where(zh == 0, left, right)
    got = lax.ppermute(jnp.where(zh == 0, right, left), "zh", [(0, 1), (1, 0)])
    pieces = []
    for k in range(2):
        chosen = lax.dynamic_slice_in_dim(out_weight, (core ^ k) * CH, CH, 0)
        pairs = [(a * 2 + b, (b ^ k) * 2 + a) for a in range(2) for b in range(2)]
        chosen = lax.ppermute(chosen, ("zh", "c"), pairs)
        pieces.append(jnp.concatenate([chosen[:128], chosen[128:]], axis=1))
    own, got, pieces = lax.optimization_barrier((own, got, pieces))
    gathered = lax.all_gather(own, ring).reshape(2, 4, 2, ROWS + TILE, WIDE)
    kept = jnp.concatenate([kept, pieces[0]], axis=1)
    got = jnp.concatenate([got, pieces[1]], axis=1)
    weights = (
        *ring_pairs(jnp.concatenate(ring_pairs(kept, "x"), axis=0), "y"),
        *ring_pairs(jnp.concatenate(ring_pairs(got, "y"), axis=0), "x"),
    )
    weights, gathered = lax.optimization_barrier((weights, gathered))

    taps = lax.dynamic_slice_in_dim(short_filter, zh * CH, CH, 2)
    bias = lax.dynamic_slice_in_dim(mr_bias, zh * CH, CH, 0)[None, :]
    band = toeplitz(lax.dynamic_slice_in_dim(mr_filter, zh * GROUPS, GROUPS, 0))

    proj, tail, mid, front, w_out = project(at, gathered, weights, taps)

    last = column == 3
    to_first = jnp.where(last, tail[1], tail[0])
    to_second = jnp.where(last, tail[0], tail[1])
    first = lax.ppermute(to_first, ("y", "x"), [(i, i + 1) for i in range(15)])
    second = lax.ppermute(
        to_second, ("y", "x"), [(i, i // 4 * 4 + (i + 1) % 4) for i in range(16)]
    )
    def swapped(mine):
        return mine, lax.ppermute(mine, "c", [(0, 1), (1, 0)])

    partial = project_out(at, *swapped(mix(proj, mid, band, taps, bias, 2, 2)), w_out, 1)
    first, second, partial = lax.optimization_barrier((first, second, partial))
    halo = jnp.stack([jnp.where(leading, front, first), second])
    partial = project_out(
        at, *swapped(mix(proj, halo, band, taps, bias, 0, 2)), w_out, 0, partial
    )
    summed = lax.psum_scatter(
        partial.reshape(8, ROWS, WIDE), ("zh", "zl"), scatter_dimension=0
    )
    return (tokens.astype(F32) + summed.astype(F32)).astype(BF16)


def solution(mesh):
    split = Mesh(mesh.devices.reshape(4, 2, 4, 4, 2), ("y", "zh", "x", "zl", "c"))
    seq, tensor = ("y", "zh", "x"), ("zl", "c")
    in_specs = (
        P(seq, tensor),
        P(None, tensor),
        P(tensor),
        P(None, seq, tensor),
        P(None, None, tensor),
        P(tensor, None),
        P(tensor),
        P(tensor, seq),
    )
    return jax.shard_map(
        on_device, mesh=split, in_specs=in_specs, out_specs=P(seq, tensor), check_vma=False
    )
```

```python
import jax
import jax.numpy as jnp
from jax import lax
from jax.experimental import pallas as pl
from jax.experimental.pallas import tpu as pltpu
from jax.sharding import Mesh, PartitionSpec as P

GSIZE = 16
LH = 128
ROWS = 512
TILE = 80
SHARE = 72
HALF = ROWS // 2
WIDE = 512
CH = 256
GROUPS = CH // GSIZE
HALO = LH + 16
MIB = 1024 * 1024
F32 = jnp.float32
BF16 = jnp.bfloat16


def row_iota(shape):
    return lax.broadcasted_iota(jnp.int32, shape, 0)


def three_taps(rows, taps, s):
    return (
        taps[0, s : s + 1] * rows
        + taps[1, s : s + 1] * pltpu.roll(rows, 1, 0)
        + taps[2, s : s + 1] * pltpu.roll(rows, 2, 0)
    )


def last_rows(parts, first, shift):
    place = row_iota((16, CH)) // 2
    out = jnp.zeros((16, CH), F32)
    for s in range(3):
        moved = pltpu.roll(parts[s][first : first + 16], (2 * s + shift) % 16, 0)
        out = jnp.where(place == s, moved, out)
    return out.astype(BF16)


def as_column(row):
    column = jnp.broadcast_to(row, (128, row.shape[1])).T
    return jnp.concatenate([column] * (CH // 128), axis=1)


def project_kernel(at_ref, x_ref, *refs):
    taps_ref, proj_ref, tail_ref, mid_ref, front_ref, out_w_ref = refs[4:10]
    wide, ahead, sems, out_sems = refs[10:]
    first_row = pl.program_id(0) == 0
    copies = []
    out_copies = []
    for k in range(2):
        half = at_ref[8] if k == 0 else 1 - at_ref[8]
        for i in range(4):
            for j in range(4):
                y, x = (i, j) if k == 0 else (j, i)
                start = (2 * at_ref[y] + half) * WIDE + at_ref[4 + x] * 128
                rows = pl.ds(pl.multiple_of(start, 128), 128)
                source = refs[2 * k + i // 2].at[i % 2, j, :, pl.ds(0, 3 * CH)]
                copies.append(pltpu.make_async_copy(source, wide.at[rows], sems.at[k, i, j]))
                lanes = pl.ds(pl.multiple_of(at_ref[4 + x] * 128, 128), 128)
                for part in range(2):
                    source = refs[2 * k + i // 2].at[i % 2, j, :, pl.ds(3 * CH + part * 128, 128)]
                    place = out_w_ref.at[at_ref[y], pl.ds(k * CH + part * 128, 128), lanes]
                    sem = out_sems.at[k, i, j, part]
                    out_copies.append(pltpu.make_async_copy(source, place, sem))

    @pl.when(first_row)
    def _():
        for copy in copies:
            copy.start()
        for copy in out_copies:
            copy.start()
        for copy in copies:
            copy.wait()

    features = jnp.concatenate([x_ref[0, t] for t in range(8)], axis=1)
    products = jnp.dot(features, wide[...], preferred_element_type=F32)
    sums = jnp.zeros((8, WIDE), F32)
    for t in range(8):
        sums += x_ref[0, t, ROWS + TILE - 16 :].astype(F32)[8:]
    own = lax.rsqrt((sums[0:1] + sums[1:2]) * (1.0 / 4096.0) + 1e-6)
    extra = lax.rsqrt((sums[2:3] + sums[3:4]) * (1.0 / 4096.0) + 1e-6)
    own, extra = as_column(own), as_column(extra[:, :128])[:TILE]
    for s in range(3):
        lanes = slice(s * CH, (s + 1) * CH)
        proj_ref[s, 0] = (products[:ROWS, lanes] * own).astype(BF16)
        carried = (products[ROWS:, lanes] * extra).astype(BF16).astype(F32)

        @pl.when(first_row)
        def _(s=s, carried=carried):
            ahead[s, :SHARE] = carried[:SHARE]

        @pl.when(jnp.logical_not(first_row))
        def _(s=s, carried=carried):
            ahead[s, SHARE:] = carried

    for end, ref in ((ROWS, tail_ref), (HALF, mid_ref)):
        rows = [proj_ref[s, 0, end - HALO : end].astype(F32) for s in range(3)]
        mixing = three_taps(rows[1], taps_ref, 1) * three_taps(rows[2], taps_ref, 2)
        ref[0, :LH] = mixing[HALO - LH :].astype(BF16)
        ref[0, LH:] = last_rows(rows, HALO - 16, 2)

    @pl.when(jnp.logical_not(first_row))
    def _():
        mixing = three_taps(ahead[1], taps_ref, 1) * three_taps(ahead[2], taps_ref, 2)
        front_ref[:LH] = pltpu.roll(mixing, SHARE + TILE - 1, 0)[:LH].astype(BF16)
        front_ref[LH:] = last_rows(ahead, LH - 8, -7)
        for copy in out_copies:
            copy.wait()


def project(at, gathered, weights, taps):
    return pl.pallas_call(
        project_kernel,
        grid_spec=pltpu.PrefetchScalarGridSpec(
            num_scalar_prefetch=1,
            grid=(2,),
            in_specs=[
                pl.BlockSpec((1, 8, ROWS + TILE, WIDE), lambda h, at: (h, 0, 0, 0)),
                *[pl.BlockSpec(memory_space=pl.ANY)] * 4,
                pl.BlockSpec((3, 3, CH), lambda h, at: (0, 0, 0)),
            ],
            out_specs=[
                pl.BlockSpec((3, 1, ROWS, CH), lambda h, at: (0, h, 0, 0)),
                pl.BlockSpec((1, HALO, CH), lambda h, at: (h, 0, 0)),
                pl.BlockSpec((1, HALO, CH), lambda h, at: (h, 0, 0)),
                pl.BlockSpec((HALO, CH), lambda h, at: (0, 0)),
                pl.BlockSpec(memory_space=pltpu.HBM),
            ],
            scratch_shapes=[
                pltpu.VMEM((8 * WIDE, 3 * CH), BF16),
                pltpu.VMEM((3, SHARE + TILE, CH), F32),
                pltpu.SemaphoreType.DMA((2, 4, 4)),
                pltpu.SemaphoreType.DMA((2, 4, 4, 2)),
            ],
        ),
        out_shape=[
            jax.ShapeDtypeStruct((3, 2, ROWS, CH), BF16),
            jax.ShapeDtypeStruct((2, HALO, CH), BF16),
            jax.ShapeDtypeStruct((2, HALO, CH), BF16),
            jax.ShapeDtypeStruct((HALO, CH), BF16),
            jax.ShapeDtypeStruct((4, 2 * CH, WIDE), BF16),
        ],
        compiler_params=pltpu.CompilerParams(vmem_limit_bytes=50 * MIB),
        cost_estimate=pl.CostEstimate(
            flops=2 * 2 * ROWS * 4096 * 3 * CH, bytes_accessed=18_000_000, transcendentals=0
        ),
        name="project",
    )(at, gathered, *weights, taps)


def toeplitz_kernel(u_ref, out_ref):
    for g in range(GROUPS):
        wide = jnp.broadcast_to(u_ref[g : g + 1], (LH, 3 * LH))
        skewed = pltpu.roll(wide, 0, 1, stride=1, stride_axis=0)
        out_ref[g] = skewed[:, : 2 * LH].astype(BF16)


def toeplitz(filters):
    backwards = jnp.flip(filters.astype(F32), 1)
    row = jnp.pad(backwards, ((0, 0), (1, 2 * LH - 1)))
    return pl.pallas_call(
        toeplitz_kernel,
        out_shape=jax.ShapeDtypeStruct((GROUPS, LH, 2 * LH), BF16),
        compiler_params=pltpu.CompilerParams(vmem_limit_bytes=8 * MIB),
        name="toeplitz",
    )(row)


def mix_kernel(proj_ref, halo_ref, band_ref, taps_ref, bias_ref, out_ref, before, edge):
    step = pl.program_id(0)

    @pl.when(step == 0)
    def _():
        for h in range(2):
            before[h] = halo_ref[h, :LH]
            last = halo_ref[h, LH:].astype(F32)
            for s in range(3):
                edge[h, s] = pltpu.roll(last, (6 - 2 * s) % 16, 0)[:8]

    queries = []
    mixes = []
    windows = []
    for h in range(2):
        feats = []
        for s in range(3):
            lifted = proj_ref[s, h].astype(F32)
            rows = jnp.concatenate([edge[h, s], lifted], axis=0)
            feats.append(three_taps(rows, taps_ref, s)[8:])
            edge[h, s] = lifted[LH - 8 :]
        mixing = (feats[1] * feats[2]).astype(BF16)
        queries.append(feats[0])
        mixes.append(mixing)
        windows.append(jnp.concatenate([before[h], mixing], axis=0))
        before[h] = mixing
    lane_group = lax.broadcasted_iota(jnp.int32, (LH, 2 * LH), 1) % LH // GSIZE
    halves = []
    for half in range(2):
        lanes = slice(half * LH, (half + 1) * LH)
        window = jnp.concatenate([windows[0][:, lanes], windows[1][:, lanes]], axis=1)
        total = jnp.zeros((LH, 2 * LH), F32)
        for g in range(GROUPS // 2):
            one = jnp.dot(band_ref[half * 8 + g], window, preferred_element_type=F32)
            total = jnp.where(lane_group == g, one, total)
        halves.append(total)
    for h in range(2):
        rows = slice(h * LH, (h + 1) * LH)
        filtered = jnp.concatenate([halves[0][:, rows], halves[1][:, rows]], axis=1)
        value = queries[h] * (filtered + bias_ref[...] * mixes[h].astype(F32))
        out_ref[h] = value.astype(BF16)


def mix(proj, halo, band, taps, bias, first, count):
    return pl.pallas_call(
        mix_kernel,
        grid=(count,),
        in_specs=[
            pl.BlockSpec((3, 2, LH, CH), lambda b: (0, 0, b + first, 0)),
            pl.BlockSpec((2, HALO, CH), lambda b: (0, 0, 0)),
            pl.BlockSpec((GROUPS, LH, 2 * LH), lambda b: (0, 0, 0)),
            pl.BlockSpec((3, 3, CH), lambda b: (0, 0, 0)),
            pl.BlockSpec((1, CH), lambda b: (0, 0)),
        ],
        out_specs=pl.BlockSpec((2, LH, CH), lambda b: (0, b, 0)),
        out_shape=jax.ShapeDtypeStruct((2, count * LH, CH), BF16),
        scratch_shapes=[
            pltpu.VMEM((2, LH, CH), BF16),
            pltpu.VMEM((2, 3, 8, CH), F32),
        ],
        compiler_params=pltpu.CompilerParams(vmem_limit_bytes=16 * MIB),
        cost_estimate=pl.CostEstimate(
            flops=2 * 512 * CH * 2048, bytes_accessed=2_000_000, transcendentals=0
        ),
        name="mix",
    )(proj, halo, band, taps, bias)


def out_kernel(at_ref, mine_ref, other_ref, w_ref, *refs):
    out_ref, rows = refs[-2:]

    @pl.when(pl.program_id(0) == 0)
    def _():
        swap = at_ref[9] == 1
        for h in range(2):
            place = slice(h * HALF, (h + 1) * HALF)
            rows[place, :CH] = jnp.where(swap, other_ref[h], mine_ref[h])
            rows[place, CH:] = jnp.where(swap, mine_ref[h], other_ref[h])

    products = jnp.dot(rows[...], w_ref[0], preferred_element_type=F32).astype(BF16)
    for h in range(2):
        out_ref[h, 0] = products[h * HALF : (h + 1) * HALF]


def project_out(at, mine, other, weights, half, base=None):
    more = () if base is None else (base,)
    return pl.pallas_call(
        out_kernel,
        grid_spec=pltpu.PrefetchScalarGridSpec(
            num_scalar_prefetch=1,
            grid=(4,),
            in_specs=[
                *[pl.BlockSpec((2, HALF, CH), lambda k, at: (0, 0, 0))] * 2,
                pl.BlockSpec((1, 2 * CH, WIDE), lambda k, at: (k, 0, 0)),
                *[pl.BlockSpec(memory_space=pl.ANY)] * len(more),
            ],
            out_specs=pl.BlockSpec((2, 1, HALF, WIDE), lambda k, at: (0, k, half, 0)),
            scratch_shapes=[pltpu.VMEM((2 * HALF, 2 * CH), BF16)],
        ),
        out_shape=jax.ShapeDtypeStruct((2, 4, ROWS, WIDE), BF16),
        input_output_aliases={} if base is None else {4: 0},
        compiler_params=pltpu.CompilerParams(vmem_limit_bytes=44 * MIB),
        cost_estimate=pl.CostEstimate(
            flops=2 * 512 * 2 * CH * 2048, bytes_accessed=5_000_000, transcendentals=0
        ),
        name="project_out",
    )(at, mine, other, weights, *more)


FIRST, SECOND = (1, 3), (3, 1)


def pair_step(value, axis, masks):
    pairs = [(i * 2 + c, (i ^ masks[c]) * 2 + c) for i in range(4) for c in range(2)]
    return lax.ppermute(value, (axis, "c"), pairs)


def ring_pairs(piece, axis):
    here = jnp.stack([piece, pair_step(piece, axis, FIRST)])
    return here, pair_step(here, axis, SECOND)


def on_device(
    tokens, prior_rows, norm_gain, in_weight, short_filter, mr_filter, mr_bias, out_weight
):
    zh = lax.axis_index("zh")
    column = lax.axis_index("x")
    leading = (column == 0) & (lax.axis_index("y") == 0)

    core = lax.axis_index("c")
    turns = jnp.where(core == 0, jnp.array([0, 1, 3, 2]), jnp.array([0, 3, 1, 2]))
    at = jnp.concatenate(
        [lax.axis_index("y") ^ turns, column ^ turns, jnp.stack([zh, zh ^ core])]
    ).astype(jnp.int32)
    ring = ("zh", "zl", "c")
    padded = jnp.pad(prior_rows, ((0, 2 * SHARE - prior_rows.shape[0]), (0, 0)))
    some = lax.dynamic_slice_in_dim(padded, zh * SHARE, SHARE, 0)
    lifted, carried = tokens.astype(F32), some.astype(F32)
    gain = norm_gain.astype(F32)
    sums = jnp.sum(lifted * lifted, axis=1)
    more = jnp.pad(jnp.sum(carried * carried, axis=1), (0, WIDE - SHARE))
    sums = jnp.stack([sums, more])
    coarse = lax.reduce_precision(sums, 8, 7)
    terms = jnp.stack([coarse, sums - coarse], axis=1).reshape(4, WIDE).astype(BF16)
    own = jnp.concatenate(
        [
            (lifted * gain).astype(BF16),
            (carried * gain).astype(BF16),
            jnp.pad(terms, ((0, TILE - SHARE - 4), (0, 0))),
        ],
        axis=0,
    )

    left, right = (
        jnp.concatenate([in_weight[s, :, part * CH : (part + 1) * CH] for s in range(3)], axis=1)
        for part in range(2)
    )
    kept = jnp.where(zh == 0, left, right)
    got = lax.ppermute(jnp.where(zh == 0, right, left), "zh", [(0, 1), (1, 0)])
    pieces = []
    for k in range(2):
        chosen = lax.dynamic_slice_in_dim(out_weight, (core ^ k) * CH, CH, 0)
        pairs = [(a * 2 + b, (b ^ k) * 2 + a) for a in range(2) for b in range(2)]
        chosen = lax.ppermute(chosen, ("zh", "c"), pairs)
        pieces.append(jnp.concatenate([chosen[:128], chosen[128:]], axis=1))
    own, got, pieces = lax.optimization_barrier((own, got, pieces))
    gathered = lax.all_gather(own, ring).reshape(2, 8, ROWS + TILE, WIDE)
    kept = jnp.concatenate([kept, pieces[0]], axis=1)
    got = jnp.concatenate([got, pieces[1]], axis=1)
    weights = (
        *ring_pairs(jnp.concatenate(ring_pairs(kept, "x"), axis=0), "y"),
        *ring_pairs(jnp.concatenate(ring_pairs(got, "y"), axis=0), "x"),
    )
    weights, gathered = lax.optimization_barrier((weights, gathered))

    taps = lax.dynamic_slice_in_dim(short_filter, zh * CH, CH, 2)
    bias = lax.dynamic_slice_in_dim(mr_bias, zh * CH, CH, 0)[None, :]
    band = toeplitz(lax.dynamic_slice_in_dim(mr_filter, zh * GROUPS, GROUPS, 0))

    proj, tail, mid, front, w_out = project(at, gathered, weights, taps)

    last = column == 3
    to_first = jnp.where(last, tail[1], tail[0])
    to_second = jnp.where(last, tail[0], tail[1])
    first = lax.ppermute(to_first, ("y", "x"), [(i, i + 1) for i in range(15)])
    second = lax.ppermute(
        to_second, ("y", "x"), [(i, i // 4 * 4 + (i + 1) % 4) for i in range(16)]
    )
    def swapped(mine):
        return mine, lax.ppermute(mine, "c", [(0, 1), (1, 0)])

    partial = project_out(at, *swapped(mix(proj, mid, band, taps, bias, 2, 2)), w_out, 1)
    first, second, partial = lax.optimization_barrier((first, second, partial))
    halo = jnp.stack([jnp.where(leading, front, first), second])
    partial = project_out(
        at, *swapped(mix(proj, halo, band, taps, bias, 0, 2)), w_out, 0, partial
    )
    summed = lax.psum_scatter(
        partial.reshape(8, ROWS, WIDE), ("zh", "zl"), scatter_dimension=0
    )
    return (tokens.astype(F32) + summed.astype(F32)).astype(BF16)


def solution(mesh):
    split = Mesh(mesh.devices.reshape(4, 2, 4, 4, 2), ("y", "zh", "x", "zl", "c"))
    seq, tensor = ("y", "zh", "x"), ("zl", "c")
    in_specs = (
        P(seq, tensor),
        P(None, tensor),
        P(tensor),
        P(None, seq, tensor),
        P(None, None, tensor),
        P(tensor, None),
        P(tensor),
        P(tensor, seq),
    )
    return jax.shard_map(
        on_device, mesh=split, in_specs=in_specs, out_specs=P(seq, tensor), check_vma=False
    )
```

```python
import jax
import jax.numpy as jnp
from jax import lax
from jax.experimental import pallas as pl
from jax.experimental.pallas import tpu as pltpu
from jax.sharding import Mesh, PartitionSpec as P

GSIZE = 16
LH = 128
ROWS = 512
TILE = 80
SHARE = 72
HALF = ROWS // 2
WIDE = 512
CH = 256
GROUPS = CH // GSIZE
HALO = LH + 16
MIB = 1024 * 1024
F32 = jnp.float32
BF16 = jnp.bfloat16


def row_iota(shape):
    return lax.broadcasted_iota(jnp.int32, shape, 0)


def three_taps(rows, taps, s):
    return (
        taps[0, s : s + 1] * rows
        + taps[1, s : s + 1] * pltpu.roll(rows, 1, 0)
        + taps[2, s : s + 1] * pltpu.roll(rows, 2, 0)
    )


def last_rows(parts, first, shift):
    place = row_iota((16, CH)) // 2
    out = jnp.zeros((16, CH), F32)
    for s in range(3):
        moved = pltpu.roll(parts[s][first : first + 16], (2 * s + shift) % 16, 0)
        out = jnp.where(place == s, moved, out)
    return out.astype(BF16)


def as_column(row):
    column = jnp.broadcast_to(row, (128, row.shape[1])).T
    return jnp.concatenate([column] * (CH // 128), axis=1)


def project_kernel(at_ref, x_ref, *refs):
    taps_ref, proj_ref, tail_ref, mid_ref, front_ref, out_w_ref = refs[4:10]
    wide, acc, stat, ahead, sems, out_sems = refs[10:]
    first_row, kind = pl.program_id(0) == 0, pl.program_id(1)
    turns = []
    out_copies = []
    for k in range(2):
        copies = []
        for i in range(4):
            for j in range(4):
                y, x = (i, j) if k == 0 else (j, i)
                start = at_ref[y] * WIDE + at_ref[4 + x] * 128
                rows = pl.ds(pl.multiple_of(start, 128), 128)
                source = refs[2 * k + i // 2].at[i % 2, j, :, pl.ds(0, 3 * CH)]
                copies.append(pltpu.make_async_copy(source, wide.at[k, rows], sems.at[k, i, j]))
                lanes = pl.ds(pl.multiple_of(at_ref[4 + x] * 128, 128), 128)
                for part in range(2):
                    source = refs[2 * k + i // 2].at[i % 2, j, :, pl.ds(3 * CH + part * 128, 128)]
                    place = out_w_ref.at[at_ref[y], pl.ds(k * CH + part * 128, 128), lanes]
                    sem = out_sems.at[k, i, j, part]
                    out_copies.append(pltpu.make_async_copy(source, place, sem))
        turns.append(copies)

    @pl.when(first_row & (kind == 0))
    def _():
        for copies in turns:
            for copy in copies:
                copy.start()

    for k in range(2):

        @pl.when(first_row & (kind == k))
        def _(k=k):
            for copy in turns[k]:
                copy.wait()

    @pl.when(first_row & (kind == 1))
    def _():
        for copy in out_copies:
            copy.start()

    features = jnp.concatenate([x_ref[0, y, 0] for y in range(4)], axis=1)
    products = jnp.dot(features, wide[kind], preferred_element_type=F32)
    sums = jnp.zeros((8, WIDE), F32)
    for y in range(4):
        sums += x_ref[0, y, 0, ROWS + TILE - 16 :].astype(F32)[8:]

    @pl.when(kind == 0)
    def _():
        acc[...] = products
        stat[...] = sums

    @pl.when(kind == 1)
    def _():
        total = stat[...] + sums
        own = lax.rsqrt((total[0:1] + total[1:2]) * (1.0 / 4096.0) + 1e-6)
        extra = lax.rsqrt((total[2:3] + total[3:4]) * (1.0 / 4096.0) + 1e-6)
        own, extra = as_column(own), as_column(extra[:, :128])[:TILE]
        for s in range(3):
            lanes = slice(s * CH, (s + 1) * CH)
            whole = acc[:, lanes] + products[:, lanes]
            proj_ref[s, 0] = (whole[:ROWS] * own).astype(BF16)
            carried = (whole[ROWS:] * extra).astype(BF16).astype(F32)

            @pl.when(first_row)
            def _(s=s, carried=carried):
                ahead[s, :SHARE] = carried[:SHARE]

            @pl.when(jnp.logical_not(first_row))
            def _(s=s, carried=carried):
                ahead[s, SHARE:] = carried

        for end, ref in ((ROWS, tail_ref), (HALF, mid_ref)):
            rows = [proj_ref[s, 0, end - HALO : end].astype(F32) for s in range(3)]
            mixing = three_taps(rows[1], taps_ref, 1) * three_taps(rows[2], taps_ref, 2)
            ref[0, :LH] = mixing[HALO - LH :].astype(BF16)
            ref[0, LH:] = last_rows(rows, HALO - 16, 2)

    @pl.when((pl.program_id(0) == 1) & (kind == 1))
    def _():
        mixing = three_taps(ahead[1], taps_ref, 1) * three_taps(ahead[2], taps_ref, 2)
        front_ref[:LH] = pltpu.roll(mixing, SHARE + TILE - 1, 0)[:LH].astype(BF16)
        front_ref[LH:] = last_rows(ahead, LH - 8, -7)
        for copy in out_copies:
            copy.wait()


def project(at, gathered, weights, taps):
    return pl.pallas_call(
        project_kernel,
        grid_spec=pltpu.PrefetchScalarGridSpec(
            num_scalar_prefetch=1,
            grid=(2, 2),
            in_specs=[
                pl.BlockSpec(
                    (1, 4, 1, ROWS + TILE, WIDE),
                    lambda h, k, at: (h, 0, at[8] + k - 2 * at[8] * k, 0, 0),
                ),
                *[pl.BlockSpec(memory_space=pl.ANY)] * 4,
                pl.BlockSpec((3, 3, CH), lambda h, k, at: (0, 0, 0)),
            ],
            out_specs=[
                pl.BlockSpec((3, 1, ROWS, CH), lambda h, k, at: (0, h, 0, 0)),
                pl.BlockSpec((1, HALO, CH), lambda h, k, at: (h, 0, 0)),
                pl.BlockSpec((1, HALO, CH), lambda h, k, at: (h, 0, 0)),
                pl.BlockSpec((HALO, CH), lambda h, k, at: (0, 0)),
                pl.BlockSpec(memory_space=pltpu.HBM),
            ],
            scratch_shapes=[
                pltpu.VMEM((2, 4 * WIDE, 3 * CH), BF16),
                pltpu.VMEM((ROWS + TILE, 3 * CH), F32),
                pltpu.VMEM((8, WIDE), F32),
                pltpu.VMEM((3, SHARE + TILE, CH), F32),
                pltpu.SemaphoreType.DMA((2, 4, 4)),
                pltpu.SemaphoreType.DMA((2, 4, 4, 2)),
            ],
        ),
        out_shape=[
            jax.ShapeDtypeStruct((3, 2, ROWS, CH), BF16),
            jax.ShapeDtypeStruct((2, HALO, CH), BF16),
            jax.ShapeDtypeStruct((2, HALO, CH), BF16),
            jax.ShapeDtypeStruct((HALO, CH), BF16),
            jax.ShapeDtypeStruct((4, 2 * CH, WIDE), BF16),
        ],
        compiler_params=pltpu.CompilerParams(vmem_limit_bytes=50 * MIB),
        cost_estimate=pl.CostEstimate(
            flops=2 * 2 * ROWS * 4096 * 3 * CH, bytes_accessed=18_000_000, transcendentals=0
        ),
        name="project",
    )(at, gathered, *weights, taps)


def toeplitz_kernel(u_ref, out_ref):
    for g in range(GROUPS):
        wide = jnp.broadcast_to(u_ref[g : g + 1], (LH, 3 * LH))
        skewed = pltpu.roll(wide, 0, 1, stride=1, stride_axis=0)
        out_ref[g] = skewed[:, : 2 * LH].astype(BF16)


def toeplitz(filters):
    backwards = jnp.flip(filters.astype(F32), 1)
    row = jnp.pad(backwards, ((0, 0), (1, 2 * LH - 1)))
    return pl.pallas_call(
        toeplitz_kernel,
        out_shape=jax.ShapeDtypeStruct((GROUPS, LH, 2 * LH), BF16),
        compiler_params=pltpu.CompilerParams(vmem_limit_bytes=8 * MIB),
        name="toeplitz",
    )(row)


def mix_kernel(proj_ref, halo_ref, band_ref, taps_ref, bias_ref, out_ref, before, edge):
    step = pl.program_id(0)

    @pl.when(step == 0)
    def _():
        for h in range(2):
            before[h] = halo_ref[h, :LH]
            last = halo_ref[h, LH:].astype(F32)
            for s in range(3):
                edge[h, s] = pltpu.roll(last, (6 - 2 * s) % 16, 0)[:8]

    queries = []
    mixes = []
    windows = []
    for h in range(2):
        feats = []
        for s in range(3):
            lifted = proj_ref[s, h].astype(F32)
            rows = jnp.concatenate([edge[h, s], lifted], axis=0)
            feats.append(three_taps(rows, taps_ref, s)[8:])
            edge[h, s] = lifted[LH - 8 :]
        mixing = (feats[1] * feats[2]).astype(BF16)
        queries.append(feats[0])
        mixes.append(mixing)
        windows.append(jnp.concatenate([before[h], mixing], axis=0))
        before[h] = mixing
    lane_group = lax.broadcasted_iota(jnp.int32, (LH, 2 * LH), 1) % LH // GSIZE
    halves = []
    for half in range(2):
        lanes = slice(half * LH, (half + 1) * LH)
        window = jnp.concatenate([windows[0][:, lanes], windows[1][:, lanes]], axis=1)
        total = jnp.zeros((LH, 2 * LH), F32)
        for g in range(GROUPS // 2):
            one = jnp.dot(band_ref[half * 8 + g], window, preferred_element_type=F32)
            total = jnp.where(lane_group == g, one, total)
        halves.append(total)
    for h in range(2):
        rows = slice(h * LH, (h + 1) * LH)
        filtered = jnp.concatenate([halves[0][:, rows], halves[1][:, rows]], axis=1)
        value = queries[h] * (filtered + bias_ref[...] * mixes[h].astype(F32))
        out_ref[h] = value.astype(BF16)


def mix(proj, halo, band, taps, bias, first, count):
    return pl.pallas_call(
        mix_kernel,
        grid=(count,),
        in_specs=[
            pl.BlockSpec((3, 2, LH, CH), lambda b: (0, 0, b + first, 0)),
            pl.BlockSpec((2, HALO, CH), lambda b: (0, 0, 0)),
            pl.BlockSpec((GROUPS, LH, 2 * LH), lambda b: (0, 0, 0)),
            pl.BlockSpec((3, 3, CH), lambda b: (0, 0, 0)),
            pl.BlockSpec((1, CH), lambda b: (0, 0)),
        ],
        out_specs=pl.BlockSpec((2, LH, CH), lambda b: (0, b, 0)),
        out_shape=jax.ShapeDtypeStruct((2, count * LH, CH), BF16),
        scratch_shapes=[
            pltpu.VMEM((2, LH, CH), BF16),
            pltpu.VMEM((2, 3, 8, CH), F32),
        ],
        compiler_params=pltpu.CompilerParams(vmem_limit_bytes=16 * MIB),
        cost_estimate=pl.CostEstimate(
            flops=2 * 512 * CH * 2048, bytes_accessed=2_000_000, transcendentals=0
        ),
        name="mix",
    )(proj, halo, band, taps, bias)


def out_kernel(at_ref, mine_ref, other_ref, w_ref, *refs):
    out_ref, rows = refs[-2:]

    @pl.when(pl.program_id(0) == 0)
    def _():
        swap = at_ref[9] == 1
        for h in range(2):
            place = slice(h * HALF, (h + 1) * HALF)
            rows[place, :CH] = jnp.where(swap, other_ref[h], mine_ref[h])
            rows[place, CH:] = jnp.where(swap, mine_ref[h], other_ref[h])

    products = jnp.dot(rows[...], w_ref[0], preferred_element_type=F32).astype(BF16)
    for h in range(2):
        out_ref[h, 0] = products[h * HALF : (h + 1) * HALF]


def project_out(at, mine, other, weights, half, base=None):
    more = () if base is None else (base,)
    return pl.pallas_call(
        out_kernel,
        grid_spec=pltpu.PrefetchScalarGridSpec(
            num_scalar_prefetch=1,
            grid=(4,),
            in_specs=[
                *[pl.BlockSpec((2, HALF, CH), lambda k, at: (0, 0, 0))] * 2,
                pl.BlockSpec((1, 2 * CH, WIDE), lambda k, at: (k, 0, 0)),
                *[pl.BlockSpec(memory_space=pl.ANY)] * len(more),
            ],
            out_specs=pl.BlockSpec((2, 1, HALF, WIDE), lambda k, at: (0, k, half, 0)),
            scratch_shapes=[pltpu.VMEM((2 * HALF, 2 * CH), BF16)],
        ),
        out_shape=jax.ShapeDtypeStruct((2, 4, ROWS, WIDE), BF16),
        input_output_aliases={} if base is None else {4: 0},
        compiler_params=pltpu.CompilerParams(vmem_limit_bytes=44 * MIB),
        cost_estimate=pl.CostEstimate(
            flops=2 * 512 * 2 * CH * 2048, bytes_accessed=5_000_000, transcendentals=0
        ),
        name="project_out",
    )(at, mine, other, weights, *more)


FIRST, SECOND = (1, 3), (3, 1)


def pair_step(value, axis, masks):
    pairs = [(i * 2 + c, (i ^ masks[c]) * 2 + c) for i in range(4) for c in range(2)]
    return lax.ppermute(value, (axis, "c"), pairs)


def ring_pairs(piece, axis):
    here = jnp.stack([piece, pair_step(piece, axis, FIRST)])
    return here, pair_step(here, axis, SECOND)


def on_device(
    tokens, prior_rows, norm_gain, in_weight, short_filter, mr_filter, mr_bias, out_weight
):
    zh = lax.axis_index("zh")
    column = lax.axis_index("x")
    leading = (column == 0) & (lax.axis_index("y") == 0)

    core = lax.axis_index("c")
    turns = jnp.where(core == 0, jnp.array([0, 1, 3, 2]), jnp.array([0, 3, 1, 2]))
    at = jnp.concatenate(
        [lax.axis_index("y") ^ turns, column ^ turns, jnp.stack([zh, zh ^ core])]
    ).astype(jnp.int32)
    ring = ("zh", "zl", "c")
    padded = jnp.pad(prior_rows, ((0, 2 * SHARE - prior_rows.shape[0]), (0, 0)))
    some = lax.dynamic_slice_in_dim(padded, zh * SHARE, SHARE, 0)
    lifted, carried = tokens.astype(F32), some.astype(F32)
    gain = norm_gain.astype(F32)
    sums = jnp.sum(lifted * lifted, axis=1)
    more = jnp.pad(jnp.sum(carried * carried, axis=1), (0, WIDE - SHARE))
    sums = jnp.stack([sums, more])
    coarse = lax.reduce_precision(sums, 8, 7)
    terms = jnp.stack([coarse, sums - coarse], axis=1).reshape(4, WIDE).astype(BF16)
    own = jnp.concatenate(
        [
            (lifted * gain).astype(BF16),
            (carried * gain).astype(BF16),
            jnp.pad(terms, ((0, TILE - SHARE - 4), (0, 0))),
        ],
        axis=0,
    )

    left, right = (
        jnp.concatenate([in_weight[s, :, part * CH : (part + 1) * CH] for s in range(3)], axis=1)
        for part in range(2)
    )
    kept = jnp.where(zh == 0, left, right)
    got = lax.ppermute(jnp.where(zh == 0, right, left), "zh", [(0, 1), (1, 0)])
    pieces = []
    for k in range(2):
        chosen = lax.dynamic_slice_in_dim(out_weight, (core ^ k) * CH, CH, 0)
        pairs = [(a * 2 + b, (b ^ k) * 2 + a) for a in range(2) for b in range(2)]
        chosen = lax.ppermute(chosen, ("zh", "c"), pairs)
        out_weight, chosen = lax.optimization_barrier((out_weight, chosen))
        pieces.append(jnp.concatenate([chosen[:128], chosen[128:]], axis=1))
    own, got, pieces = lax.optimization_barrier((own, got, pieces))
    gathered = lax.all_gather(own, ring).reshape(2, 4, 2, ROWS + TILE, WIDE)
    kept = jnp.concatenate([kept, pieces[0]], axis=1)
    got = jnp.concatenate([got, pieces[1]], axis=1)
    weights = (
        *ring_pairs(jnp.concatenate(ring_pairs(kept, "x"), axis=0), "y"),
        *ring_pairs(jnp.concatenate(ring_pairs(got, "y"), axis=0), "x"),
    )
    weights, gathered = lax.optimization_barrier((weights, gathered))

    taps = lax.dynamic_slice_in_dim(short_filter, zh * CH, CH, 2)
    bias = lax.dynamic_slice_in_dim(mr_bias, zh * CH, CH, 0)[None, :]
    band = toeplitz(lax.dynamic_slice_in_dim(mr_filter, zh * GROUPS, GROUPS, 0))

    proj, tail, mid, front, w_out = project(at, gathered, weights, taps)

    last = column == 3
    to_first = jnp.where(last, tail[1], tail[0])
    to_second = jnp.where(last, tail[0], tail[1])
    first = lax.ppermute(to_first, ("y", "x"), [(i, i + 1) for i in range(15)])
    second = lax.ppermute(
        to_second, ("y", "x"), [(i, i // 4 * 4 + (i + 1) % 4) for i in range(16)]
    )
    def swapped(mine):
        return mine, lax.ppermute(mine, "c", [(0, 1), (1, 0)])

    partial = project_out(at, *swapped(mix(proj, mid, band, taps, bias, 2, 2)), w_out, 1)
    first, second, partial = lax.optimization_barrier((first, second, partial))
    halo = jnp.stack([jnp.where(leading, front, first), second])
    partial = project_out(
        at, *swapped(mix(proj, halo, band, taps, bias, 0, 2)), w_out, 0, partial
    )
    summed = lax.psum_scatter(
        partial.reshape(8, ROWS, WIDE), ("zh", "zl"), scatter_dimension=0
    )
    return (tokens.astype(F32) + summed.astype(F32)).astype(BF16)


def solution(mesh):
    split = Mesh(mesh.devices.reshape(4, 2, 4, 4, 2), ("y", "zh", "x", "zl", "c"))
    seq, tensor = ("y", "zh", "x"), ("zl", "c")
    in_specs = (
        P(seq, tensor),
        P(None, tensor),
        P(tensor),
        P(None, seq, tensor),
        P(None, None, tensor),
        P(tensor, None),
        P(tensor),
        P(tensor, seq),
    )
    return jax.shard_map(
        on_device, mesh=split, in_specs=in_specs, out_specs=P(seq, tensor), check_vma=False
    )
```
